32 devices in a mesh: sector: 4 (over x, core), term: 8 (over z, y).
Axes of the slice: x: 2, y: 2, z: 4, core: 2. Of those that a mesh axis runs over, the one named last changes fastest.
Arguments:
- lanczos_vector: float32 [8, 512, 512], P('sector'), may hold values from -6 to 6
- left_block: bfloat16 [8, 32, 512, 512], P('sector', 'term'), may hold values from -0.375 to 0.375
- right_block: bfloat16 [8, 32, 512, 512], P('sector', 'term'), may hold values from -0.25 to 0.25
- left_energy: float32 [8, 512], P('sector'), may hold values from 0.5 to 4
- right_energy: float32 [8, 512], P('sector'), may hold values from 0.5 to 4
- sector_shifts: int32 [32], P('term'), may hold values from -1 to 1
- sector_sizes: int32 [8], P('sector'), may hold values from 128 to 512, as said below
Outputs:
- next_vector: float32 [8, 512, 512], P('sector', 'term')
- next_sigma: float32 [8, 512, 512], P('sector', 'term')
The draws below stay inside these ranges and needn't reach their ends.
Inputs may be any that keep to these rules, and one draw needn't show every extreme that they name: `sector_sizes`: each value is a multiple of 128; some sector has exactly 512.
All inputs are finite; a program needn't handle non-finite values.
Results may differ from the reference program's by a relative error of at most 0.0023.
Values may be sent and summed in bfloat16 or wider, within the bound.
No kernel may reach another device: no remote copies, remote signals or barrier semaphores. Data moves between devices by JAX's collectives and lax.ppermute only.
A program may use at most 64 MiB of HBM per device.

```python
import math
import jax
import jax.numpy as jnp
from jax import lax

P_SIZE = 512
SECTORS = 8
TERMS = 32


def draw_sector_sizes(key, part):
    level_key = jax.random.fold_in(key, 11)
    full_key = jax.random.fold_in(key, 12)
    levels = jax.random.randint(level_key, (SECTORS,), 1, 5) * (P_SIZE // 4)
    full_sector = jax.random.randint(full_key, (), 0, SECTORS)
    return jnp.where(jnp.arange(SECTORS) == full_sector, P_SIZE, levels).astype(jnp.int32)


def set_ends(array, stream_key, smallest, top_value):
    longest = array.shape.index(max(array.shape))
    spots = []
    for shift in (0, 1):
        where = [jax.random.randint(jax.random.fold_in(stream_key, axis), (), 0, length) for axis, length in enumerate(array.shape)]
        where[longest] = (where[longest] + shift) % array.shape[longest]
        spots.append(tuple(where))
    return array.at[spots[0]].set(smallest).at[spots[1]].set(top_value)


def with_spikes(entries, rng, source, target, shards_of, factor):
    def block_of(position):
        return (jnp.arange(entries.shape[position]) // (entries.shape[position] // shards_of)).reshape((-1,) + (1,) * (entries.ndim - 1 - position))

    one_side = jax.random.permutation(rng, shards_of)[block_of(target)]
    far = (block_of(target) + shards_of // 2) % shards_of
    return jnp.where((block_of(source) == one_side) | (block_of(source) == far), factor * entries, entries)


def level_of(key, dims, shards, least, largest):
    loudness = 1.0
    for position, blocks in shards:
        steps = jax.random.uniform(jax.random.fold_in(jax.random.fold_in(key, 6), position), (blocks,), jnp.float32, least / len(shards), largest / len(shards))
        loudness = loudness * jnp.repeat(jnp.exp(steps), dims[position] // blocks).reshape((-1,) + (1,) * (len(dims) - 1 - position))
    return loudness


def scatter_about(own_key, shape, deviation, bound, pieces=(), held_as=jnp.bfloat16):
    entries = deviation * jax.random.normal(own_key, shape, jnp.float32)
    if pieces:
        entries = entries * level_of(own_key, shape, pieces, -0.22, 0.18)
    return jnp.clip(entries, -bound, bound).astype(held_as)


def bell_draw_with(key, shape, spread, limit, cuts, heavy, kind=jnp.bfloat16):
    entries = spread * jax.random.normal(key, shape, jnp.float32)
    if cuts:
        entries = entries * level_of(key, shape, cuts, -0.22, 0.18)
    return jnp.clip(with_spikes(entries, jax.random.fold_in(key, 3), *heavy), -limit, limit).astype(kind)


def setup_inputs(seed: int = 0) -> dict:
    seeds = jax.random.split(jax.random.key(seed), 8)
    lanczos_vector = scatter_about(seeds[0], (SECTORS, P_SIZE, P_SIZE), 1.0, 6.0, ((0, 4),), jnp.float32)
    left_block = bell_draw_with(seeds[1], (SECTORS, TERMS, P_SIZE, P_SIZE), P_SIZE ** -0.5, 0.375, ((0, 4), (1, 8)), (1, 2, 8, 2.0))
    right_block = scatter_about(seeds[2], (SECTORS, TERMS, P_SIZE, P_SIZE), P_SIZE ** -0.5, 0.25, ((0, 4), (1, 8)))
    left_energy = jnp.clip(jnp.exp(math.log(4.0) - 2.0794415 * jax.random.uniform(seeds[3], (SECTORS, P_SIZE), jnp.float32) ** level_of(seeds[3], (SECTORS, P_SIZE), ((0, 4),), -0.2, 0.2)), 0.5, 4.0)
    right_energy = jnp.clip(jnp.exp(math.log(4.0) - 2.0794415 * jax.random.uniform(seeds[4], (SECTORS, P_SIZE), jnp.float32) ** level_of(seeds[4], (SECTORS, P_SIZE), ((0, 4),), -0.2, 0.2)), 0.5, 4.0)
    sector_shifts = set_ends(jax.random.randint(seeds[5], (TERMS,), -1, 2), jax.random.fold_in(seeds[5], 1), -1, 1).astype(jnp.int32)
    sector_sizes = draw_sector_sizes(jax.random.fold_in(seeds[7], 71), 0)
    return dict(lanczos_vector=lanczos_vector, left_block=left_block, right_block=right_block, left_energy=left_energy, right_energy=right_energy, sector_shifts=sector_shifts, sector_sizes=sector_sizes)


def apply_hamiltonian(full_blocks, left_block, right_block, energies, live_mask, sector_shifts):
    rounded = full_blocks.astype(jnp.bfloat16)
    empty = jnp.zeros((1, P_SIZE, P_SIZE), jnp.bfloat16)
    padded = jnp.concatenate([empty, rounded, empty], axis=0)

    def one_sector(input_arrays):
        sector_id, left_operator_terms, right_operator_terms = input_arrays
        partner_ids = (sector_id + 1 + sector_shifts).astype(jnp.int32)
        paired_sectors = padded[partner_ids]
        left_blended = jnp.einsum('zxn,znq->zxq', left_operator_terms.astype(jnp.float32), paired_sectors.astype(jnp.float32)).astype(jnp.bfloat16)
        return jnp.einsum('njp,nwp->jw', left_blended.astype(jnp.float32), right_operator_terms.astype(jnp.float32))
    sector_labels = jnp.arange(SECTORS, dtype=jnp.int32)
    partials = lax.map(one_sector, (sector_labels, left_block, right_block))
    term_scale = float(TERMS) ** (-0.5)
    return live_mask * (energies * full_blocks + term_scale * partials)

def reference(lanczos_vector, left_block, right_block, left_energy, right_energy, sector_shifts, sector_sizes):
    sector_positions = jnp.arange(P_SIZE, dtype=jnp.int32)
    limits = sector_sizes[:, None, None]
    live_mask = ((sector_positions[None, :, None] < limits) & (sector_positions[None, None, :] < limits)).astype(jnp.float32)
    energies = left_energy[:, :, None] + right_energy[:, None, :]
    cell_count = float(SECTORS * P_SIZE * P_SIZE)
    start_vector = live_mask * lanczos_vector
    sigma = apply_hamiltonian(start_vector, left_block, right_block, energies, live_mask, sector_shifts)
    correlation = jnp.sum(start_vector * sigma) / cell_count
    norm_sq = jnp.sum(start_vector * start_vector) / cell_count
    ritz_value = correlation / (norm_sq + 1e-06)
    residual = sigma - ritz_value * start_vector
    next_vector = residual / jnp.sqrt(jnp.sum(residual * residual) / cell_count + 1e-06)
    next_sigma = apply_hamiltonian(next_vector, left_block, right_block, energies, live_mask, sector_shifts)
    return (next_vector, next_sigma)
```

```python
import functools
import jax
import jax.numpy as jnp
from jax import lax
from jax.experimental import pallas as pl
from jax.experimental.pallas import tpu as pltpu
from jax.sharding import PartitionSpec as P

epsilon = 1e-06
NT = (((1,), (1,)), ((), ()))


def other(hi, step, count):
    return hi ^ step if count & (count - 1) == 0 else (step - hi) % count


def traced_other(hi, step, count):
    return hi ^ step if count & (count - 1) == 0 else lax.rem(step - hi + count, count)


def pairs_low(size):
    return [(i, i ^ 1) for i in range(size)]


def pairs_high(size, low, step):
    count = size // low
    return [(i, other(i // low, step, count) * low + i % low) for i in range(size)]


def terms_kernel(count, low, span, gathered, place_ref, shift_ref, *refs):
    if gathered:
        blocks, (left_ref, right_ref, send_ref, keep_ref, wb, acc) = refs[:6], refs[6:]
    else:
        blocks, (left_ref, right_ref, send_ref, keep_ref, wb, acc) = refs[:3], refs[3:]
    term, last = pl.program_id(0), pl.num_programs(0) - 1
    hi, lo = place_ref[0], place_ref[1]

    def row_of(step, digit):
        return pl.multiple_of((traced_other(hi, step, count) * low + digit) * span, span)

    @pl.when(term == 0)
    def _():
        acc[...] = jnp.zeros_like(acc)
        for e in range(3):
            if gathered:
                for step in range(count):
                    wb[e, pl.ds(row_of(step, lo), span), :] = blocks[2 * e][step]
                    if low > 1:
                        wb[e, pl.ds(row_of(step, 1 - lo), span), :] = blocks[2 * e + 1][step]
            else:
                wb[e] = blocks[e][...]

    mixed = jnp.dot(left_ref[...], wb[1 + shift_ref[term]], preferred_element_type=jnp.float32)
    acc[...] += lax.dot_general(
        mixed.astype(jnp.bfloat16), right_ref[...], NT, preferred_element_type=jnp.float32
    )

    @pl.when(term == last)
    def _():
        for step in range(count):
            keep_ref[step] = acc[pl.ds(row_of(step, lo), span), :]
            if low > 1:
                send_ref[step] = acc[pl.ds(row_of(step, 1 - lo), span), :].astype(jnp.bfloat16)


def sector_terms(s, place, shifts, blocks, left_block, right_block, count, low, span, gathered):
    terms, size = left_block.shape[1], left_block.shape[2]
    specs, operands = [], []
    for arrays, index in blocks:
        for a in arrays if gathered else (arrays,):
            specs.append(
                pl.BlockSpec(
                    (None,) + a.shape[1:],
                    functools.partial(lambda i, n, t, *_: (i,) + (0,) * n, index, a.ndim - 1),
                )
            )
            operands.append(a)
    matrix = pl.BlockSpec((None, None, size, size), lambda t, *_: (s, t, 0, 0))
    chunks = pl.BlockSpec((count, span, size), lambda t, *_: (0, 0, 0))
    return pl.pallas_call(
        functools.partial(terms_kernel, count, low, span, gathered),
        grid_spec=pltpu.PrefetchScalarGridSpec(
            num_scalar_prefetch=2,
            grid=(terms,),
            in_specs=specs + [matrix, matrix],
            out_specs=[chunks, chunks],
            scratch_shapes=[
                pltpu.VMEM((3, size, size), jnp.bfloat16),
                pltpu.VMEM((size, size), jnp.float32),
            ],
        ),
        out_shape=[
            jax.ShapeDtypeStruct((count, span, size), jnp.bfloat16),
            jax.ShapeDtypeStruct((count, span, size), jnp.float32),
        ],
        compiler_params=pltpu.CompilerParams(
            dimension_semantics=("arbitrary",), vmem_limit_bytes=40 * 2**20
        ),
        cost_estimate=pl.CostEstimate(
            flops=4 * terms * size**3, bytes_accessed=4 * terms * size * size, transcendentals=0
        ),
    )(place, shifts, *operands, left_block, right_block)


def on_device(
    lanczos_vector, left_block, right_block, left_energy, right_energy, sector_shifts, sector_sizes
):
    sectors, size = lanczos_vector.shape[:2]
    terms, ranks = left_block.shape[1], lax.axis_size("term")
    groups = lax.axis_size("sector")
    scale = float(terms * ranks) ** (-0.5)
    cells = float(sectors * groups * size * size)
    span = size // ranks
    low = 2 if ranks % 2 == 0 else 1
    count = ranks // low
    rank = lax.axis_index("term")
    place = jnp.stack([rank // low, rank % low]).astype(jnp.int32)
    row_start = rank * span
    up = [(i, i + 1) for i in range(groups - 1)]
    down = [(j, i) for i, j in up]

    position = jnp.arange(size, dtype=jnp.int32)
    limits = sector_sizes[:, None, None]
    live = (position[None, :, None] < limits) & (position[None, None, :] < limits)
    start = jnp.where(live, lanczos_vector, 0.0)
    energies = left_energy[:, :, None] + right_energy[:, None, :]

    def own_rows(a):
        return lax.dynamic_slice_in_dim(a, row_start, span, 1)

    live_rows = ((row_start + jnp.arange(span, dtype=jnp.int32))[None, :, None] < limits) & (
        position[None, None, :] < limits
    )
    start_rows = jnp.where(live_rows, own_rows(lanczos_vector), 0.0)
    energy_rows = own_rows(left_energy)[:, :, None] + right_energy[:, None, :]

    def halo(first, final):
        return lax.ppermute(final, "sector", up), lax.ppermute(first, "sector", down)

    def neighbours(own, before, after):
        extended = [(before, 0)] + [(own, s) for s in range(sectors)] + [(after, 0)]
        return [extended[s : s + 3] for s in range(sectors)]

    def scatter_sum(send, keep):
        total = keep
        if low > 1:
            total = total + lax.ppermute(send, "term", pairs_low(ranks)).astype(jnp.float32)
        rows = total[0]
        for step in range(1, count):
            got = lax.ppermute(
                total[step].astype(jnp.bfloat16), "term", pairs_high(ranks, low, step)
            )
            rows = rows + got.astype(jnp.float32)
        return rows

    def partial_rows(blocks, gathered):
        return jnp.stack(
            [
                scatter_sum(
                    *sector_terms(
                        s, place, sector_shifts, blocks[s], left_block, right_block,
                        count, low, span, gathered,
                    )
                )
                for s in range(sectors)
            ]
        )

    with jax.named_scope("first"):
        rounded = start.astype(jnp.bfloat16)
        before, after = halo(rounded[:1], rounded[-1:])
        norm_sq, mean_energy = lax.psum(
            (jnp.sum(start * start), jnp.sum(start * start * energies)), "sector"
        )
        guess = (mean_energy / cells) / (norm_sq / cells + epsilon)
        summed = partial_rows(neighbours(rounded, before, after), False)
        mixed_rows = jnp.where(live_rows, scale * summed, 0.0)
        shifted = mixed_rows + (energy_rows - guess) * start_rows

    with jax.named_scope("gather"):
        own = shifted.astype(jnp.bfloat16)
        parts = [own] + [
            lax.ppermute(own, "term", pairs_high(ranks, low, step)) for step in range(1, count)
        ]
        mine = jnp.stack(parts, 1)
        theirs = lax.ppermute(mine, "term", pairs_low(ranks)) if low > 1 else mine
        halo_mine = halo(mine[:1], mine[-1:])
        halo_theirs = halo(theirs[:1], theirs[-1:])

    with jax.named_scope("scalars"):
        shifted_sq, overlap = lax.psum(
            (jnp.sum(shifted * shifted), jnp.sum(shifted * start_rows)), ("sector", "term")
        )
        correlation = overlap + guess * norm_sq
        ritz = (correlation / cells) / (norm_sq / cells + epsilon)
        delta = ritz - guess
        res_sq = shifted_sq - 2.0 * delta * overlap + delta * delta * norm_sq
        inverse = lax.rsqrt(res_sq / cells + epsilon)
        next_rows = (shifted - delta * start_rows) * inverse
        base = energy_rows * next_rows - (delta * inverse) * mixed_rows

    with jax.named_scope("second"):
        blocks = neighbours(
            (mine, theirs), (halo_mine[0], halo_theirs[0]), (halo_mine[1], halo_theirs[1])
        )
        summed = partial_rows(blocks, True)
        next_sigma = base + jnp.where(live_rows, (scale * inverse) * summed, 0.0)
    return next_rows, next_sigma


def solution(mesh):
    return jax.shard_map(
        on_device,
        mesh=mesh,
        in_specs=(
            P("sector", None, None),
            P("sector", "term", None, None),
            P("sector", "term", None, None),
            P("sector", None),
            P("sector", None),
            P("term"),
            P("sector"),
        ),
        out_specs=(P("sector", "term", None), P("sector", "term", None)),
        check_vma=False,
    )
```

```python
import functools
import jax
import jax.numpy as jnp
from jax import lax
from jax.experimental import pallas as pl
from jax.experimental.pallas import tpu as pltpu
from jax.sharding import PartitionSpec as P

epsilon = 1e-06
NT = (((1,), (1,)), ((), ()))


def other(hi, step, count):
    return hi ^ step if count & (count - 1) == 0 else (step - hi) % count


def traced_other(hi, step, count):
    return hi ^ step if count & (count - 1) == 0 else lax.rem(step - hi + count, count)


def pairs_low(size):
    return [(i, i ^ 1) for i in range(size)]


def pairs_high(size, low, step):
    count = size // low
    return [(i, other(i // low, step, count) * low + i % low) for i in range(size)]


def terms_kernel(s, count, low, span, gathered, place_ref, shift_ref, *refs):
    split = 6 if gathered else 3
    blocks, (left_hbm, right_hbm, send_ref, keep_ref, wb, left, right, mixed, acc, sems) = (
        refs[:split],
        refs[split:],
    )
    terms, size = left.shape[0], left.shape[1]
    hi, lo = place_ref[0], place_ref[1]

    def row_of(step, digit):
        return pl.multiple_of((traced_other(hi, step, count) * low + digit) * span, span)

    copies = [
        pltpu.make_async_copy(hbm.at[s, t], vmem.at[t], sems.at[k, t])
        for k, (hbm, vmem) in enumerate(((left_hbm, left), (right_hbm, right)))
        for t in range(terms)
    ]
    for copy in copies:
        copy.start()
    for e in range(3):
        if gathered:
            for step in range(count):
                wb[e, pl.ds(row_of(step, lo), span), :] = blocks[2 * e][step]
                if low > 1:
                    wb[e, pl.ds(row_of(step, 1 - lo), span), :] = blocks[2 * e + 1][step]
        else:
            wb[e] = blocks[e][...]
    for t in range(terms):
        copies[t].wait()
        mixed[t] = jnp.dot(
            left[t], wb[1 + shift_ref[t]], preferred_element_type=jnp.float32
        ).astype(jnp.bfloat16)
    for t in range(terms):
        copies[terms + t].wait()
    tile = min(256, size)
    for first in range(0, size, tile):
        rows = pl.ds(first, tile)
        total = None
        for t in range(terms):
            product = lax.dot_general(
                mixed[t, rows, :], right[t], NT, preferred_element_type=jnp.float32
            )
            total = product if total is None else total + product
        acc[rows, :] = total
    for step in range(count):
        keep_ref[step] = acc[pl.ds(row_of(step, lo), span), :]
        if low > 1:
            send_ref[step] = acc[pl.ds(row_of(step, 1 - lo), span), :].astype(jnp.bfloat16)


def sector_terms(s, place, shifts, blocks, left_block, right_block, count, low, span, gathered):
    terms, size = left_block.shape[1], left_block.shape[2]
    specs, operands = [], []
    for block in blocks:
        for a, index in block if gathered else (block,):
            specs.append(
                pl.BlockSpec(
                    (None,) + a.shape[1:],
                    functools.partial(lambda i, n, g, *_: (i,) + (0,) * n, index, a.ndim - 1),
                )
            )
            operands.append(a)
    chunks = pl.BlockSpec((count, span, size), lambda g, *_: (0, 0, 0))
    whole = pl.BlockSpec(memory_space=pltpu.HBM)
    matrices = pltpu.VMEM((terms, size, size), jnp.bfloat16)
    return pl.pallas_call(
        functools.partial(terms_kernel, s, count, low, span, gathered),
        grid_spec=pltpu.PrefetchScalarGridSpec(
            num_scalar_prefetch=2,
            grid=(1,),
            in_specs=specs + [whole, whole],
            out_specs=[chunks, chunks],
            scratch_shapes=[
                pltpu.VMEM((3, size, size), jnp.bfloat16),
                matrices,
                matrices,
                matrices,
                pltpu.VMEM((size, size), jnp.float32),
                pltpu.SemaphoreType.DMA((2, terms)),
            ],
        ),
        out_shape=[
            jax.ShapeDtypeStruct((count, span, size), jnp.bfloat16),
            jax.ShapeDtypeStruct((count, span, size), jnp.float32),
        ],
        compiler_params=pltpu.CompilerParams(
            dimension_semantics=("arbitrary",), vmem_limit_bytes=24 * 2**20
        ),
        cost_estimate=pl.CostEstimate(
            flops=4 * terms * size**3, bytes_accessed=4 * terms * size * size, transcendentals=0
        ),
    )(place, shifts, *operands, left_block, right_block)


def on_device(
    lanczos_vector, left_block, right_block, left_energy, right_energy, sector_shifts, sector_sizes
):
    sectors, size = lanczos_vector.shape[:2]
    terms, ranks = left_block.shape[1], lax.axis_size("term")
    groups = lax.axis_size("sector")
    scale = float(terms * ranks) ** (-0.5)
    cells = float(sectors * groups * size * size)
    span = size // ranks
    low = 2 if ranks % 2 == 0 else 1
    count = ranks // low
    rank = lax.axis_index("term")
    place = jnp.stack([rank // low, rank % low]).astype(jnp.int32)
    row_start = rank * span
    up = [(i, i + 1) for i in range(groups - 1)]
    down = [(j, i) for i, j in up]

    position = jnp.arange(size, dtype=jnp.int32)
    limits = sector_sizes[:, None, None]
    live = (position[None, :, None] < limits) & (position[None, None, :] < limits)
    start = jnp.where(live, lanczos_vector, 0.0)
    energies = left_energy[:, :, None] + right_energy[:, None, :]

    def own_rows(a):
        return lax.dynamic_slice_in_dim(a, row_start, span, 1)

    live_rows = ((row_start + jnp.arange(span, dtype=jnp.int32))[None, :, None] < limits) & (
        position[None, None, :] < limits
    )
    start_rows = jnp.where(live_rows, own_rows(lanczos_vector), 0.0)
    energy_rows = own_rows(left_energy)[:, :, None] + right_energy[:, None, :]

    def halo(first, final):
        return lax.ppermute(final, "sector", up), lax.ppermute(first, "sector", down)

    def neighbours(own, before, after):
        extended = [(before, 0)] + [(own, s) for s in range(sectors)] + [(after, 0)]
        return [extended[s : s + 3] for s in range(sectors)]

    def scatter_sum(send, keep):
        total = keep
        if low > 1:
            total = total + lax.ppermute(send, "term", pairs_low(ranks)).astype(jnp.float32)
        rows = total[0]
        for step in range(1, count):
            got = lax.ppermute(
                total[step].astype(jnp.bfloat16), "term", pairs_high(ranks, low, step)
            )
            rows = rows + got.astype(jnp.float32)
        return rows

    def partial_rows(blocks, gathered):
        return jnp.stack(
            [
                scatter_sum(
                    *sector_terms(
                        s, place, sector_shifts, blocks[s], left_block, right_block,
                        count, low, span, gathered,
                    )
                )
                for s in range(sectors)
            ]
        )

    with jax.named_scope("first"):
        rounded = start.astype(jnp.bfloat16)
        before, after = halo(rounded[:1], rounded[-1:])
        norm_sq, mean_energy = lax.psum(
            (jnp.sum(start * start), jnp.sum(start * start * energies)), "sector"
        )
        guess = (mean_energy / cells) / (norm_sq / cells + epsilon)
        summed = partial_rows(neighbours(rounded, before, after), False)
        mixed_rows = jnp.where(live_rows, scale * summed, 0.0)
        shifted = mixed_rows + (energy_rows - guess) * start_rows

    with jax.named_scope("gather"):
        mine, theirs, halos = [None] * sectors, [None] * sectors, [None, None]
        for s in reversed(range(sectors)):
            own = shifted[s : s + 1].astype(jnp.bfloat16)
            parts = [own] + [
                lax.ppermute(own, "term", pairs_high(ranks, low, step)) for step in range(1, count)
            ]
            mine[s] = jnp.stack(parts, 1)
            theirs[s] = lax.ppermute(mine[s], "term", pairs_low(ranks)) if low > 1 else mine[s]
            whole = jnp.concatenate([mine[s], theirs[s]], 0)
            if s == sectors - 1:
                halos[0] = lax.ppermute(whole, "sector", up)
            if s == 0:
                halos[1] = lax.ppermute(whole, "sector", down)

    with jax.named_scope("scalars"):
        digits = jnp.stack([place[1], 1 - place[1]])[:low]
        high = jnp.stack([traced_other(place[0], step, count) for step in range(count)])
        order = (high[None, :] * low + digits[:, None]).reshape(-1)
        ordered = jnp.take(start.reshape(sectors, ranks, span, size), order, axis=1)
        gathered = jnp.concatenate(
            [jnp.concatenate(([m, t] if low > 1 else [m]), 1) for m, t in zip(mine, theirs)], 0
        ).astype(jnp.float32)
        shifted_sq, overlap = lax.psum(
            (jnp.sum(gathered * gathered), jnp.sum(gathered * ordered)), "sector"
        )
        correlation = overlap + guess * norm_sq
        ritz = (correlation / cells) / (norm_sq / cells + epsilon)
        delta = ritz - guess
        res_sq = shifted_sq - 2.0 * delta * overlap + delta * delta * norm_sq
        inverse = lax.rsqrt(res_sq / cells + epsilon)
        next_rows = (shifted - delta * start_rows) * inverse
        base = energy_rows * next_rows - (delta * inverse) * mixed_rows

    with jax.named_scope("second"):
        def in_order(halo):
            return ((halo, 0), (halo, 1))

        extended = [in_order(halos[0])]
        extended += [((mine[s], 0), (theirs[s], 0)) for s in range(sectors)]
        extended += [in_order(halos[1])]
        blocks = [extended[s : s + 3] for s in range(sectors)]
        summed = partial_rows(blocks, True)
        next_sigma = base + jnp.where(live_rows, (scale * inverse) * summed, 0.0)
    return next_rows, next_sigma


def solution(mesh):
    return jax.shard_map(
        on_device,
        mesh=mesh,
        in_specs=(
            P("sector", None, None),
            P("sector", "term", None, None),
            P("sector", "term", None, None),
            P("sector", None),
            P("sector", None),
            P("term"),
            P("sector"),
        ),
        out_specs=(P("sector", "term", None), P("sector", "term", None)),
        check_vma=False,
    )
```

```python
import functools
import jax
import jax.numpy as jnp
from jax import lax
from jax.experimental import pallas as pl
from jax.experimental.pallas import tpu as pltpu
from jax.sharding import PartitionSpec as P

epsilon = 1e-06
NT = (((1,), (1,)), ((), ()))
GUESS = 4.5
GRANT = 121 * 2**19


def other(hi, step, count):
    return hi ^ step if count & (count - 1) == 0 else (step - hi) % count


def traced_other(hi, step, count):
    return hi ^ step if count & (count - 1) == 0 else lax.rem(step - hi + count, count)


def pairs_low(size):
    return [(i, i ^ 1) for i in range(size)]


def pairs_high(size, low, step):
    count = size // low
    return [(i, other(i // low, step, count) * low + i % low) for i in range(size)]


def row_finder(place_ref, count, low, span):
    hi, lo = place_ref[0], place_ref[1]

    def row_of(step, far):
        digit = 1 - lo if far else lo
        return pl.multiple_of((traced_other(hi, step, count) * low + digit) * span, span)

    return row_of


def add_pair(acc, left, right, block):
    mixed = jnp.dot(left[...], block, preferred_element_type=jnp.float32)
    acc[...] += lax.dot_general(
        mixed.astype(jnp.bfloat16), right[...], NT, preferred_element_type=jnp.float32
    )


def inner_kernel(dims, gathered, place_ref, shift_ref, size_ref, *refs):
    sectors, terms, size, count, low, span = dims
    if gathered:
        blocks, refs = refs[: 2 * sectors], refs[2 * sectors :]
        vector_ref, left_hbm, right_hbm, acc, sums, left, right, sems, wb = refs
    else:
        wb, left_hbm, right_hbm, acc, left, right, sems = refs
    pairs = [(s, t) for s in range(sectors) for t in range(terms)]

    def copies(s, t):
        return [
            pltpu.make_async_copy(hbm.at[s, t], vmem.at[s, t], sems.at[k, s, t])
            for k, (hbm, vmem) in enumerate(((left_hbm, left), (right_hbm, right)))
        ]

    def inside(s, t):
        partner = s + shift_ref[t]
        return (partner >= 0) & (partner < sectors)

    for s, t in pairs:

        @pl.when(inside(s, t))
        def _():
            for copy in copies(s, t):
                copy.start()

    acc[...] = jnp.zeros_like(acc)
    if gathered:
        row_of = row_finder(place_ref, count, low, span)
        for s in range(sectors):
            for step in range(count):
                for far in range(low):
                    wb[s, pl.ds(row_of(step, far), span), :] = blocks[2 * s + far][step]
    for s, t in pairs:

        @pl.when(inside(s, t))
        def _():
            for copy in copies(s, t):
                copy.wait()
            add_pair(acc.at[s], left.at[s, t], right.at[s, t], wb[s + shift_ref[t]])

    if gathered:
        sums[...] = jnp.zeros_like(sums)
        tile = min(64, size)
        for s in range(sectors):

            @pl.loop(0, size // tile)
            def _(n):
                rows = pl.ds(pl.multiple_of(n * tile, tile), tile)
                row = n * tile + lax.broadcasted_iota(jnp.int32, (tile, size), 0)
                column = lax.broadcasted_iota(jnp.int32, (tile, size), 1)
                live = (row < size_ref[s]) & (column < size_ref[s])
                start = jnp.where(live, vector_ref[s, rows, :], 0.0)
                shifted = wb[s, rows, :].astype(jnp.float32)
                for k, term in enumerate((shifted * shifted, shifted * start, start * start)):
                    sums[k : k + 1, :] += jnp.sum(term, 0, keepdims=True)


def outer_kernel(s, dims, gathered, place_ref, shift_ref, acc_ref, *refs):
    sectors, terms, size, count, low, span = dims
    sides = ([-1] if s == 0 else []) + ([1] if s == sectors - 1 else [])
    blocks, refs = refs[: len(sides)], refs[len(sides) :]
    left_hbm, right_hbm, send_ref, keep_ref, acc, left, right, wb, sems = refs
    row_of = row_finder(place_ref, count, low, span)

    def copies(t):
        return [
            pltpu.make_async_copy(hbm.at[s, t], vmem.at[t], sems.at[k, t])
            for k, (hbm, vmem) in enumerate(((left_hbm, left), (right_hbm, right)))
        ]

    def outside(t, side):
        there = place_ref[2] > 0 if side < 0 else place_ref[2] < place_ref[3] - 1
        return (shift_ref[t] == side) & there

    for t in range(terms):
        for side in sides:

            @pl.when(outside(t, side))
            def _():
                for copy in copies(t):
                    copy.start()

    acc[...] = acc_ref[s]
    for block, side in zip(blocks, sides):
        if gathered:
            for step in range(count):
                for far in range(low):
                    wb[pl.ds(row_of(step, far), span), :] = block[far, step]
            held = wb
        else:
            held = block.at[0]
        for t in range(terms):

            @pl.when(outside(t, side))
            def _():
                for copy in copies(t):
                    copy.wait()
                add_pair(acc, left.at[t], right.at[t], held[...])

    for step in range(count):
        keep_ref[step] = acc[pl.ds(row_of(step, 0), span), :]
        if low > 1:
            send_ref[step] = acc[pl.ds(row_of(step, 1), span), :].astype(jnp.bfloat16)


SMEM = pl.BlockSpec(memory_space=pltpu.SMEM)
VMEM = pl.BlockSpec(memory_space=pltpu.VMEM)
HBM = pl.BlockSpec(memory_space=pltpu.HBM)


def call(kernel, out_shape, scalars, arrays, matrices, scratch, flops):
    return pl.pallas_call(
        kernel,
        out_shape=out_shape,
        in_specs=[SMEM] * len(scalars) + [VMEM] * len(arrays) + [HBM] * len(matrices),
        out_specs=[VMEM] * len(out_shape),
        scratch_shapes=scratch,
        compiler_params=pltpu.CompilerParams(vmem_limit_bytes=GRANT),
        cost_estimate=pl.CostEstimate(flops=flops, bytes_accessed=flops // 256, transcendentals=0),
    )(*scalars, *arrays, *matrices)


def on_device(
    lanczos_vector, left_block, right_block, left_energy, right_energy, sector_shifts, sector_sizes
):
    sectors, size = lanczos_vector.shape[:2]
    terms, ranks = left_block.shape[1], lax.axis_size("term")
    groups = lax.axis_size("sector")
    scale = float(terms * ranks) ** (-0.5)
    cells = float(sectors * groups * size * size)
    span = size // ranks
    low = 2 if ranks % 2 == 0 else 1
    count = ranks // low
    rank = lax.axis_index("term")
    place = jnp.stack([rank // low, rank % low, lax.axis_index("sector"), groups])
    place = place.astype(jnp.int32)
    row_start = rank * span
    up = [(i, i + 1) for i in range(groups - 1)]
    down = [(j, i) for i, j in up]
    dims = (sectors, terms, size, count, low, span)
    matrices = (left_block, right_block)
    pair_flops = 4 * size**3

    position = jnp.arange(size, dtype=jnp.int32)
    limits = sector_sizes[:, None, None]
    rows_live = (row_start + jnp.arange(span, dtype=jnp.int32))[None, :, None] < limits
    live_rows = rows_live & (position[None, None, :] < limits)

    def own_rows(a):
        return lax.dynamic_slice_in_dim(a, row_start, span, 1)

    start_rows = jnp.where(live_rows, own_rows(lanczos_vector), 0.0)
    energy_rows = own_rows(left_energy)[:, :, None] + right_energy[:, None, :]

    def scatter_sum(send, keep):
        total = keep
        if low > 1:
            total = total + lax.ppermute(send, "term", pairs_low(ranks)).astype(jnp.float32)
        rows = total[0]
        for step in range(1, count):
            got = lax.ppermute(
                total[step].astype(jnp.bfloat16), "term", pairs_high(ranks, low, step)
            )
            rows = rows + got.astype(jnp.float32)
        return rows

    def tiles(*lead):
        return pltpu.VMEM((*lead, size, size), jnp.bfloat16)

    def inner(arrays, gathered):
        out = [jax.ShapeDtypeStruct((sectors, size, size), jnp.float32)]
        scratch = [tiles(sectors, terms)] * 2 + [pltpu.SemaphoreType.DMA((2, sectors, terms))]
        if gathered:
            out.append(jax.ShapeDtypeStruct((8, size), jnp.float32))
            scratch.append(tiles(sectors))
        return call(
            functools.partial(inner_kernel, dims, gathered),
            out,
            (place, sector_shifts, sector_sizes),
            arrays,
            matrices,
            scratch,
            sectors * terms * pair_flops * 2 // 3,
        )

    def outer(s, acc, before, after, gathered):
        sides = ([before] if s == 0 else []) + ([after] if s == sectors - 1 else [])
        return call(
            functools.partial(outer_kernel, s, dims, gathered),
            [jax.ShapeDtypeStruct((count, span, size), d) for d in (jnp.bfloat16, jnp.float32)],
            (place, sector_shifts),
            (acc, *sides),
            matrices,
            [pltpu.VMEM((size, size), jnp.float32), tiles(terms), tiles(terms), tiles()]
            + [pltpu.SemaphoreType.DMA((2, terms))],
            terms * pair_flops // 3,
        )

    def partial_rows(acc, before, after, gathered):
        return jnp.stack(
            [scatter_sum(*outer(s, acc, before, after, gathered)) for s in range(sectors)]
        )

    with jax.named_scope("first"):
        live = (position[None, :, None] < limits) & (position[None, None, :] < limits)
        rounded = jnp.where(live, lanczos_vector, 0.0).astype(jnp.bfloat16)
        before = lax.ppermute(rounded[-1:], "sector", up)
        after = lax.ppermute(rounded[:1], "sector", down)
        (acc,) = inner((rounded,), False)
        summed = partial_rows(acc, before, after, False)
        mixed_rows = jnp.where(live_rows, scale * summed, 0.0)
        shifted = mixed_rows + (energy_rows - GUESS) * start_rows

    with jax.named_scope("gather"):
        mine, theirs = [None] * sectors, [None] * sectors
        for s in reversed(range(sectors)):
            own = shifted[s].astype(jnp.bfloat16)
            parts = [own] + [
                lax.ppermute(own, "term", pairs_high(ranks, low, step)) for step in range(1, count)
            ]
            mine[s] = jnp.stack(parts)
            theirs[s] = lax.ppermute(mine[s], "term", pairs_low(ranks)) if low > 1 else mine[s]
            whole = jnp.stack([mine[s], theirs[s]])
            if s == sectors - 1:
                before = lax.ppermute(whole, "sector", up)
            if s == 0:
                after = lax.ppermute(whole, "sector", down)

    with jax.named_scope("second"):
        blocks = [b for both in zip(mine, theirs) for b in both]
        acc, sums = inner((*blocks, lanczos_vector), True)

    with jax.named_scope("scalars"):
        if groups & (groups - 1) == 0:
            reach = 1
            while reach < groups:
                sums = sums + lax.ppermute(
                    sums, "sector", [(i, i ^ reach) for i in range(groups)]
                )
                reach *= 2
        else:
            sums = lax.psum(sums, "sector")
        shifted_sq, overlap, norm_sq = [jnp.sum(sums[k]) for k in range(3)]
        correlation = overlap + GUESS * norm_sq
        ritz = (correlation / cells) / (norm_sq / cells + epsilon)
        delta = ritz - GUESS
        res_sq = shifted_sq - 2.0 * delta * overlap + delta * delta * norm_sq
        inverse = lax.rsqrt(res_sq / cells + epsilon)
        next_rows = (shifted - delta * start_rows) * inverse
        base = energy_rows * next_rows - (delta * inverse) * mixed_rows
        factor = jnp.where(live_rows, scale * inverse, 0.0)
        next_rows, base, factor = lax.optimization_barrier((next_rows, base, factor))

    with jax.named_scope("second"):
        next_sigma = base + factor * partial_rows(acc, before, after, True)
    return next_rows, next_sigma


def solution(mesh):
    return jax.shard_map(
        on_device,
        mesh=mesh,
        in_specs=(
            P("sector", None, None),
            P("sector", "term", None, None),
            P("sector", "term", None, None),
            P("sector", None),
            P("sector", None),
            P("term"),
            P("sector"),
        ),
        out_specs=(P("sector", "term", None), P("sector", "term", None)),
        check_vma=False,
    )
```

```python
import functools
import jax
import jax.numpy as jnp
from jax import lax
from jax.experimental import pallas as pl
from jax.experimental.pallas import tpu as pltpu
from jax.sharding import PartitionSpec as P

epsilon = 1e-06
NT = (((1,), (1,)), ((), ()))
GUESS = 4.5
GRANT = 24 * 2**20


def other(hi, step, count):
    return hi ^ step if count & (count - 1) == 0 else (step - hi) % count


def traced_other(hi, step, count):
    return hi ^ step if count & (count - 1) == 0 else lax.rem(step - hi + count, count)


def pairs_low(size):
    return [(i, i ^ 1) for i in range(size)]


def pairs_high(size, low, step):
    count = size // low
    return [(i, other(i // low, step, count) * low + i % low) for i in range(size)]


def hop_order(count):
    if count & (count - 1):
        return list(range(count))
    order, step = [0], count // 2
    while step:
        order += [o ^ step for o in order]
        step //= 2
    return order


def row_finder(count, low, span):
    rank = lax.axis_index("term")
    hi, lo = rank // low, lax.rem(rank, low)

    def row_of(step, far):
        digit = 1 - lo if far else lo
        return pl.multiple_of((traced_other(hi, step, count) * low + digit) * span, span)

    return row_of


def add_pair(acc, left, right, block):
    mixed = jnp.dot(left[...], block, preferred_element_type=jnp.float32)
    acc[...] += lax.dot_general(
        mixed.astype(jnp.bfloat16), right[...], NT, preferred_element_type=jnp.float32
    )


def live_tile(shape, first_row, limit):
    row = first_row + lax.broadcasted_iota(jnp.int32, shape, 0)
    return (row < limit) & (lax.broadcasted_iota(jnp.int32, shape, 1) < limit)


def round_kernel(size_ref, vector_ref, rounded_ref):
    live = live_tile(vector_ref.shape, 0, size_ref[pl.program_id(0)])
    rounded_ref[...] = jnp.where(live, vector_ref[...], 0.0).astype(jnp.bfloat16)


def inside(shift_ref, sectors, s, t):
    partner = s + shift_ref[t]
    return (partner >= 0) & (partner < sectors)


def load_kernel(dims, shift_ref, wb, left_hbm, right_hbm, acc, left, right, sems):
    sectors, terms, size, count, low, span = dims
    pairs = [(s, t) for s in range(sectors) for t in range(terms)]
    copies = {
        (s, t): [
            pltpu.make_async_copy(hbm.at[s, t], vmem.at[s, t], sems.at[k, s, t])
            for k, (hbm, vmem) in enumerate(((left_hbm, left), (right_hbm, right)))
        ]
        for s, t in pairs
    }
    for pair in pairs:
        for copy in copies[pair]:
            copy.start()
    acc[...] = jnp.zeros_like(acc)
    for s, t in pairs:
        for copy in copies[s, t]:
            copy.wait()

        @pl.when(inside(shift_ref, sectors, s, t))
        def _():
            add_pair(acc.at[s], left.at[s, t], right.at[s, t], wb[s + shift_ref[t]])


def inner_kernel(dims, shift_ref, size_ref, *refs):
    sectors, terms, size, count, low, span = dims
    blocks, refs = refs[: 2 * sectors], refs[2 * sectors :]
    vector_ref, left, right, acc, sums, wb = refs
    acc[...] = jnp.zeros_like(acc)
    sums[...] = jnp.zeros_like(sums)
    row_of = row_finder(count, low, span)
    for s in range(sectors):
        for n, step in enumerate(hop_order(count)):
            for far in range(low):
                wb[s, pl.ds(row_of(step, far), span), :] = blocks[2 * s + far][n]
    tile = min(64, size)
    for s in range(sectors):

        @pl.loop(0, size // tile)
        def _(n):
            first = pl.multiple_of(n * tile, tile)
            rows = pl.ds(first, tile)
            live = live_tile((tile, size), first, size_ref[s])
            start = jnp.where(live, vector_ref[s, rows, :], 0.0)
            shifted = wb[s, rows, :].astype(jnp.float32)
            for k, term in enumerate((shifted * shifted, shifted * start, start * start)):
                sums[k : k + 1, :] += jnp.sum(term, 0, keepdims=True)

    for s in range(sectors):
        for t in range(terms):

            @pl.when(inside(shift_ref, sectors, s, t))
            def _():
                add_pair(acc.at[s], left.at[s, t], right.at[s, t], wb[s + shift_ref[t]])


def outer_kernel(s, dims, gathered, shift_ref, acc_ref, left, right, *refs):
    sectors, terms, size, count, low, span = dims
    sides = ([-1] if s == 0 else []) + ([1] if s == sectors - 1 else [])
    blocks, refs = refs[: len(sides)], refs[len(sides) :]
    send_ref, keep_ref, acc, wb = refs
    row_of = row_finder(count, low, span)
    here, groups = lax.axis_index("sector"), lax.axis_size("sector")

    acc[...] = acc_ref[s]
    for block, side in zip(blocks, sides):
        if gathered:
            for n, step in enumerate(hop_order(count)):
                for far in range(low):
                    wb[pl.ds(row_of(step, far), span), :] = block[far, n]
            held = wb
        else:
            held = block.at[0]
        there = here > 0 if side < 0 else here < groups - 1
        for t in range(terms):

            @pl.when((shift_ref[t] == side) & there)
            def _():
                add_pair(acc, left.at[s, t], right.at[s, t], held[...])

    for step in range(count):
        keep_ref[step] = acc[pl.ds(row_of(step, 0), span), :]
        if low > 1:
            send_ref[step] = acc[pl.ds(row_of(step, 1), span), :].astype(jnp.bfloat16)


def finish_kernel(
    cells, scale, sums, shifted, start, mixed, energy, live, next_ref, base_ref, factor_ref
):
    shifted_sq, overlap, norm_sq = [
        jnp.sum(sums[k : k + 1, :], axis=1, keepdims=True) for k in range(3)
    ]
    correlation = overlap + GUESS * norm_sq
    ritz = (correlation / cells) / (norm_sq / cells + epsilon)
    delta = ritz - GUESS
    res_sq = shifted_sq - 2.0 * delta * overlap + delta * delta * norm_sq
    inverse = lax.rsqrt(res_sq / cells + epsilon)
    for s in range(shifted.shape[0]):
        vector = (shifted[s] - delta * start[s]) * inverse
        next_ref[s] = vector
        base_ref[s] = energy[s] * vector - (delta * inverse) * mixed[s]
        factor_ref[s] = live[s] * (scale * inverse)


SMEM = pl.BlockSpec(memory_space=pltpu.SMEM)
VMEM = pl.BlockSpec(memory_space=pltpu.VMEM)
HBM = pl.BlockSpec(memory_space=pltpu.HBM)


def call(kernel, out_shape, scalars, arrays, matrices, scratch, flops):
    matrices = [pltpu.with_memory_space_constraint(m, pltpu.HBM) for m in matrices]
    return pl.pallas_call(
        kernel,
        out_shape=out_shape,
        in_specs=[SMEM] * len(scalars) + [VMEM] * len(arrays) + [HBM] * len(matrices),
        out_specs=[VMEM] * len(out_shape),
        scratch_shapes=scratch,
        compiler_params=pltpu.CompilerParams(vmem_limit_bytes=GRANT),
        cost_estimate=pl.CostEstimate(flops=flops, bytes_accessed=flops // 256, transcendentals=0),
    )(*scalars, *arrays, *matrices)


def after_all(value, *others):
    return lax.optimization_barrier((value, *others))[0]


def on_device(
    lanczos_vector, left_block, right_block, left_energy, right_energy, sector_shifts, sector_sizes
):
    sectors, size = lanczos_vector.shape[:2]
    terms, ranks = left_block.shape[1], lax.axis_size("term")
    groups = lax.axis_size("sector")
    scale = float(terms * ranks) ** (-0.5)
    cells = float(sectors * groups * size * size)
    span = size // ranks
    low = 2 if ranks % 2 == 0 else 1
    count = ranks // low
    row_start = lax.axis_index("term") * span
    up = [(i, i + 1) for i in range(groups - 1)]
    down = [(j, i) for i, j in up]
    dims = (sectors, terms, size, count, low, span)
    pair_flops = 4 * size**3
    sector_sums = pltpu.VMEM((sectors, size, size), jnp.float32)

    limits = sector_sizes[:, None, None]
    rows_live = (row_start + jnp.arange(span, dtype=jnp.int32))[None, :, None] < limits
    live_rows = rows_live & (jnp.arange(size, dtype=jnp.int32)[None, None, :] < limits)

    def own_rows(a):
        return lax.dynamic_slice_in_dim(a, row_start, span, 1)

    start_rows = jnp.where(live_rows, own_rows(lanczos_vector), 0.0)
    energy_rows = own_rows(left_energy)[:, :, None] + right_energy[:, None, :]

    def outer(s, acc, before, after, gathered):
        sides = ([before] if s == 0 else []) + ([after] if s == sectors - 1 else [])
        return call(
            functools.partial(outer_kernel, s, dims, gathered),
            [jax.ShapeDtypeStruct((count, span, size), d) for d in (jnp.bfloat16, jnp.float32)],
            (sector_shifts,),
            (acc, left, right, *sides),
            (),
            [pltpu.VMEM((size, size), jnp.float32), pltpu.VMEM((size, size), jnp.bfloat16)],
            terms * pair_flops // 3,
        )

    def low_sum(send, keep):
        if low == 1:
            return keep
        return keep + lax.ppermute(send, "term", pairs_low(ranks)).astype(jnp.float32)

    def high_sum(total):
        rows = total[0]
        for step in range(1, count):
            got = lax.ppermute(
                total[step].astype(jnp.bfloat16), "term", pairs_high(ranks, low, step)
            )
            rows = rows + got.astype(jnp.float32)
        return rows

    with jax.named_scope("first"):
        rounded = pl.pallas_call(
            round_kernel,
            out_shape=jax.ShapeDtypeStruct(lanczos_vector.shape, jnp.bfloat16),
            grid=(sectors,),
            in_specs=[SMEM, pl.BlockSpec((None, size, size), lambda s: (s, 0, 0))],
            out_specs=pl.BlockSpec((None, size, size), lambda s: (s, 0, 0)),
        )(sector_sizes, lanczos_vector)
        before = lax.ppermute(rounded[-1:], "sector", up)
        after = lax.ppermute(rounded[:1], "sector", down)
        matrices = pltpu.VMEM(left_block.shape, jnp.bfloat16)
        acc, left, right = call(
            functools.partial(load_kernel, dims),
            [sector_sums, matrices, matrices],
            (sector_shifts,),
            (rounded,),
            (left_block, right_block),
            [pltpu.SemaphoreType.DMA((2, sectors, terms))],
            sectors * terms * pair_flops * 2 // 3,
        )
        totals = [low_sum(*outer(s, acc, before, after, False)) for s in range(sectors)]
        summed = jnp.stack([high_sum(total) for total in totals])
        mixed_rows = jnp.where(live_rows, scale * summed, 0.0)
        shifted = mixed_rows + (energy_rows - GUESS) * start_rows

    with jax.named_scope("gather"):
        mine, theirs = [None] * sectors, [None] * sectors
        for s in reversed(range(sectors)):
            held = shifted[s : s + 1].astype(jnp.bfloat16)
            if count & (count - 1):
                hops = [lax.ppermute(held, "term", pairs_high(ranks, low, k)) for k in range(1, count)]
                held = jnp.concatenate([held, *hops])
            else:
                step = count // 2
                while step:
                    other_half = lax.ppermute(held, "term", pairs_high(ranks, low, step))
                    held = jnp.concatenate([held, other_half])
                    step //= 2
            mine[s] = held
            theirs[s] = lax.ppermute(held, "term", pairs_low(ranks)) if low > 1 else held
            whole = jnp.stack([mine[s], theirs[s]])
            if s == sectors - 1:
                before = lax.ppermute(whole, "sector", up)
            if s == 0:
                after = lax.ppermute(whole, "sector", down)

    with jax.named_scope("second"):
        blocks = [b for both in zip(mine, theirs) for b in both]
        acc, sums = call(
            functools.partial(inner_kernel, dims),
            [sector_sums, jax.ShapeDtypeStruct((8, size), jnp.float32)],
            (sector_shifts, sector_sizes),
            (*blocks, lanczos_vector, left, right),
            (),
            [pltpu.VMEM((sectors, size, size), jnp.bfloat16)],
            sectors * terms * pair_flops * 2 // 3,
        )
        cuts = [outer(s, acc, before, after, True) for s in range(sectors)]
        totals = [low_sum(*cut) for cut in cuts]

    with jax.named_scope("scalars"):
        if groups & (groups - 1) == 0:
            reach = 1
            while reach < groups:
                got = lax.ppermute(sums, "sector", [(i, i ^ reach) for i in range(groups)])
                sums = after_all(sums + got, *cuts[-1])
                reach *= 2
        else:
            sums = lax.psum(sums, "sector")
        sums = after_all(sums, *totals)
        rows = jax.ShapeDtypeStruct(shifted.shape, jnp.float32)
        next_rows, base, factor = call(
            functools.partial(finish_kernel, cells, scale),
            [rows, rows, rows],
            (),
            (sums, shifted, start_rows, mixed_rows, energy_rows, live_rows.astype(jnp.float32)),
            (),
            [],
            20 * sectors * span * size,
        )

    with jax.named_scope("second"):
        next_sigma = base + factor * jnp.stack([high_sum(total) for total in totals])
    return next_rows, next_sigma


def solution(mesh):
    return jax.shard_map(
        on_device,
        mesh=mesh,
        in_specs=(
            P("sector", None, None),
            P("sector", "term", None, None),
            P("sector", "term", None, None),
            P("sector", None),
            P("sector", None),
            P("term"),
            P("sector"),
        ),
        out_specs=(P("sector", "term", None), P("sector", "term", None)),
        check_vma=False,
    )
```

```python
import functools
import jax
import jax.numpy as jnp
from jax import lax
from jax.experimental import pallas as pl
from jax.experimental.pallas import tpu as pltpu
from jax.sharding import PartitionSpec as P

epsilon = 1e-06
NT = (((1,), (1,)), ((), ()))
GUESS = 4.5


def other(hi, step, count):
    return hi ^ step if count & (count - 1) == 0 else (step - hi) % count


def traced_other(hi, step, count):
    return hi ^ step if count & (count - 1) == 0 else lax.rem(step - hi + count, count)


def pairs_low(size):
    return [(i, i ^ 1) for i in range(size)]


def pairs_high(size, low, step):
    count = size // low
    return [(i, other(i // low, step, count) * low + i % low) for i in range(size)]


def row_finder(count, low, span):
    rank = lax.axis_index("term")
    hi, lo = rank // low, lax.rem(rank, low)

    def row_of(step, far):
        digit = 1 - lo if far else lo
        return pl.multiple_of((traced_other(hi, step, count) * low + digit) * span, span)

    return row_of


def add_pair(acc, left, right, block):
    mixed = jnp.dot(left[...], block[...], preferred_element_type=jnp.float32)
    acc[...] += lax.dot_general(
        mixed.astype(jnp.bfloat16), right[...], NT, preferred_element_type=jnp.float32
    )


def add_inner(dims, s, shift_ref, acc, left, right, wb, before_term=lambda t: None):
    sectors, terms = dims[:2]
    for t in range(terms):
        before_term(t)
        partner = s + shift_ref[t]

        @pl.when((partner >= 0) & (partner < sectors))
        def _():
            add_pair(acc, left.at[s, t], right.at[s, t], wb.at[partner])


def add_outer(dims, s, gathered, shift_ref, acc, left, right, blocks, wb):
    sectors, terms, size, count, low, span = dims
    row_of = row_finder(count, low, span)
    here, groups = lax.axis_index("sector"), lax.axis_size("sector")
    for block, side in zip(blocks, sides_of(s, sectors)):
        if gathered:
            for step in range(count):
                for far in range(low):
                    wb[pl.ds(row_of(step, far), span), :] = block[far, step]
            held = wb
        else:
            held = block.at[0]
        there = here > 0 if side < 0 else here < groups - 1
        for t in range(terms):

            @pl.when((shift_ref[t] == side) & there)
            def _():
                add_pair(acc, left.at[s, t], right.at[s, t], held)


def cut(dims, acc, send_ref, keep_ref):
    sectors, terms, size, count, low, span = dims
    row_of = row_finder(count, low, span)
    for step in range(count):
        if low > 1:
            send_ref[step] = acc[pl.ds(row_of(step, 1), span), :].astype(jnp.bfloat16)
        keep_ref[step] = acc[pl.ds(row_of(step, 0), span), :]


def sides_of(s, sectors):
    return ([-1] if s == 0 else []) + ([1] if s == sectors - 1 else [])


def live_tile(shape, first_row, limit):
    row = first_row + lax.broadcasted_iota(jnp.int32, shape, 0)
    return (row < limit) & (lax.broadcasted_iota(jnp.int32, shape, 1) < limit)


def round_kernel(size_ref, vector_ref, rounded_ref):
    rows, size = vector_ref.shape
    tile = min(64, rows)

    @pl.loop(0, rows // tile)
    def _(n):
        first = pl.multiple_of(n * tile, tile)
        live = live_tile((tile, size), first, size_ref[pl.program_id(0)])
        part = vector_ref[pl.ds(first, tile), :]
        rounded_ref[pl.ds(first, tile), :] = jnp.where(live, part, 0.0).astype(jnp.bfloat16)


def load_kernel(
    dims, shift_ref, size_ref, wb, left_hbm, right_hbm, vector_hbm,
    acc, left, right, start, sems, row_sems,
):
    sectors, terms, size, count, low, span = dims
    first = row_finder(count, low, span)(0, 0)
    rows = [
        pltpu.make_async_copy(vector_hbm.at[s, pl.ds(first, span), :], start.at[s], row_sems.at[s])
        for s in range(sectors)
    ]
    copies = {
        (s, t): [
            pltpu.make_async_copy(hbm.at[s, t], vmem.at[s, t], sems.at[k, s, t])
            for k, (hbm, vmem) in enumerate(((left_hbm, left), (right_hbm, right)))
        ]
        for s in range(sectors)
        for t in range(terms)
    }
    for pair in copies.values():
        for copy in pair:
            copy.start()
    for copy in rows:
        copy.start()
    acc[...] = jnp.zeros_like(acc)

    def arrived(t):
        for copy in copies[0, t]:
            copy.wait()

    add_inner(dims, 0, shift_ref, acc, left, right, wb, arrived)
    for s in range(sectors):
        rows[s].wait()
        live = live_tile((span, size), first, size_ref[s])
        start[s] = jnp.where(live, start[s], 0.0)
    for s in range(1, sectors):
        for t in range(terms):
            for copy in copies[s, t]:
                copy.wait()


def inner_kernel(dims, shift_ref, size_ref, *refs):
    sectors, terms, size, count, low, span = dims
    blocks, refs = refs[: 2 * sectors], refs[2 * sectors :]
    vector_ref, left, right, acc, sums, wb = refs
    acc[...] = jnp.zeros_like(acc)
    sums[...] = jnp.zeros_like(sums)
    row_of = row_finder(count, low, span)
    for s in range(sectors):
        for step in range(count):
            for far in range(low):
                wb[s, pl.ds(row_of(step, far), span), :] = blocks[2 * s + far][step]
    tile = min(64, size)
    for s in range(sectors):

        @pl.loop(0, size // tile)
        def _(n):
            first = pl.multiple_of(n * tile, tile)
            rows = pl.ds(first, tile)
            live = live_tile((tile, size), first, size_ref[s])
            start = jnp.where(live, vector_ref[s, rows, :], 0.0)
            shifted = wb[s, rows, :].astype(jnp.float32)
            for k, term in enumerate((shifted * shifted, shifted * start, start * start)):
                sums[k : k + 1, :] += jnp.sum(term, 0, keepdims=True)

    add_inner(dims, 0, shift_ref, acc, left, right, wb)


def outer_kernel(dims, gathered, shift_ref, acc_ref, left, right, *refs):
    blocks, (send_ref, keep_ref, acc, wb) = refs[:-4], refs[-4:]
    acc[...] = acc_ref[...]
    add_outer(dims, 0, gathered, shift_ref, acc, left, right, blocks, wb)
    cut(dims, acc, send_ref, keep_ref)


def full_kernel(s, dims, gathered, shift_ref, own, left, right, *refs):
    blocks, (send_ref, keep_ref, acc, wb) = refs[:-4], refs[-4:]
    acc[...] = jnp.zeros_like(acc)
    add_inner(dims, s, shift_ref, acc, left, right, own)
    add_outer(dims, s, gathered, shift_ref, acc, left, right, blocks, wb)
    cut(dims, acc, send_ref, keep_ref)


def shift_kernel(dims, scale, size_ref, start, left_column, right_row, *refs):
    sectors, terms, size, count, low, span = dims
    parts, (held_ref, shifted_ref, mixed_ref) = refs[:-3], refs[-3:]
    first = row_finder(count, low, span)(0, 0)
    for s in range(sectors):
        total = parts[s * count][...]
        for k in range(1, count):
            total += parts[s * count + k][...].astype(jnp.float32)
        mixed = jnp.where(live_tile((span, size), first, size_ref[s]), scale * total, 0.0)
        energy = left_column[s, pl.ds(first, span), :] + right_row[s : s + 1, :]
        shifted = mixed + (energy - GUESS) * start[s]
        held_ref[s] = shifted.astype(jnp.bfloat16)
        shifted_ref[s] = shifted
        mixed_ref[s] = mixed


def finish_kernel(
    dims, cells, scale, size_ref, sums, start, left_column, right_row, shifted, mixed,
    next_ref, base_ref, factor_ref,
):
    sectors, terms, size, count, low, span = dims
    first = row_finder(count, low, span)(0, 0)
    shifted_sq, overlap, norm_sq = [
        jnp.sum(sums[k : k + 1, :], axis=1, keepdims=True) for k in range(3)
    ]
    correlation = overlap + GUESS * norm_sq
    ritz = (correlation / cells) / (norm_sq / cells + epsilon)
    delta = ritz - GUESS
    res_sq = shifted_sq - 2.0 * delta * overlap + delta * delta * norm_sq
    inverse = lax.rsqrt(res_sq / cells + epsilon)
    for s in range(sectors):
        vector = (shifted[s] - delta * start[s]) * inverse
        energy = left_column[s, pl.ds(first, span), :] + right_row[s : s + 1, :]
        next_ref[s] = vector
        base_ref[s] = energy * vector - (delta * inverse) * mixed[s]
        live = live_tile((span, size), first, size_ref[s])
        factor_ref[s] = jnp.where(live, scale * inverse, 0.0)


SMEM = pl.BlockSpec(memory_space=pltpu.SMEM)
VMEM = pl.BlockSpec(memory_space=pltpu.VMEM)
HBM = pl.BlockSpec(memory_space=pltpu.HBM)
LIMIT = pltpu.CompilerParams(vmem_limit_bytes=24 * 2**20)


def call(kernel, out_shape, scalars, arrays, matrices=(), scratch=(), flops=2**20):
    matrices = [pltpu.with_memory_space_constraint(m, pltpu.HBM) for m in matrices]
    return pl.pallas_call(
        kernel,
        out_shape=out_shape,
        in_specs=[SMEM] * len(scalars) + [VMEM] * len(arrays) + [HBM] * len(matrices),
        out_specs=[VMEM] * len(out_shape),
        scratch_shapes=scratch,
        compiler_params=LIMIT,
        cost_estimate=pl.CostEstimate(flops=flops, bytes_accessed=flops // 256, transcendentals=0),
    )(*scalars, *arrays, *matrices)


def after_all(value, *others):
    return lax.optimization_barrier((value, *others))[0]


def on_device(
    lanczos_vector, left_block, right_block, left_energy, right_energy, sector_shifts, sector_sizes
):
    sectors, size = lanczos_vector.shape[:2]
    terms, ranks = left_block.shape[1], lax.axis_size("term")
    groups = lax.axis_size("sector")
    scale = float(terms * ranks) ** (-0.5)
    cells = float(sectors * groups * size * size)
    span = size // ranks
    low = 2 if ranks % 2 == 0 else 1
    count = ranks // low
    up = [(i, i + 1) for i in range(groups - 1)]
    down = [(j, i) for i, j in up]
    dims = (sectors, terms, size, count, low, span)
    pair_flops = 4 * size**3
    left_column = left_energy[:, :, None]
    rows = pltpu.VMEM((sectors, span, size), jnp.float32)
    square = pltpu.VMEM((size, size), jnp.float32)
    square_low = pltpu.VMEM((size, size), jnp.bfloat16)
    cut_shapes = [jax.ShapeDtypeStruct((count, span, size), d) for d in (jnp.bfloat16, jnp.float32)]

    def low_sum(send, keep):
        if low == 1:
            return keep
        return keep + lax.ppermute(send, "term", pairs_low(ranks)).astype(jnp.float32)

    def high_parts(total):
        return [total[0]] + [
            lax.ppermute(total[k].astype(jnp.bfloat16), "term", pairs_high(ranks, low, k))
            for k in range(1, count)
        ]

    def sector_cuts(acc, own, before, after, gathered):
        halos = {-1: before, 1: after}
        cuts = []
        for s in range(sectors):
            blocks = [halos[side] for side in sides_of(s, sectors)]
            if s == 0:
                kernel, flops = functools.partial(outer_kernel, dims, gathered), pair_flops
            else:
                kernel = functools.partial(full_kernel, s, dims, gathered)
                flops = terms * pair_flops
            first = acc if s == 0 else own
            cuts.append(
                call(
                    kernel, cut_shapes, (sector_shifts,), (first, left, right, *blocks),
                    scratch=[square, square_low], flops=flops,
                )
            )
        return cuts

    with jax.named_scope("first"):
        rounded = pl.pallas_call(
            round_kernel,
            out_shape=jax.ShapeDtypeStruct(lanczos_vector.shape, jnp.bfloat16),
            grid=(sectors,),
            in_specs=[SMEM, pl.BlockSpec((None, size, size), lambda s: (s, 0, 0))],
            out_specs=pl.BlockSpec((None, size, size), lambda s: (s, 0, 0)),
            compiler_params=LIMIT,
        )(sector_sizes, lanczos_vector)
        before = lax.ppermute(rounded[-1:], "sector", up)
        after = lax.ppermute(rounded[:1], "sector", down)
        matrices = pltpu.VMEM(left_block.shape, jnp.bfloat16)
        acc, left, right, start = call(
            functools.partial(load_kernel, dims),
            [square, matrices, matrices, rows],
            (sector_shifts, sector_sizes),
            (rounded,),
            (left_block, right_block, lanczos_vector),
            [pltpu.SemaphoreType.DMA((2, sectors, terms)), pltpu.SemaphoreType.DMA((sectors,))],
            terms * pair_flops,
        )
        totals = [low_sum(*c) for c in sector_cuts(acc, rounded, before, after, False)]
        parts = [part for total in totals for part in high_parts(total)]
        held, shifted, mixed = call(
            functools.partial(shift_kernel, dims, scale),
            [jax.ShapeDtypeStruct((sectors, span, size), jnp.bfloat16), rows, rows],
            (sector_sizes,),
            (start, left_column, right_energy, *parts),
        )

    with jax.named_scope("gather"):
        mine, theirs = [None] * sectors, [None] * sectors
        for s in reversed(range(sectors)):
            own = held[s]
            hops = [lax.ppermute(own, "term", pairs_high(ranks, low, k)) for k in range(1, count)]
            mine[s] = jnp.stack([own, *hops])
            theirs[s] = lax.ppermute(mine[s], "term", pairs_low(ranks)) if low > 1 else mine[s]
            whole = jnp.stack([mine[s], theirs[s]])
            if s == sectors - 1:
                before = lax.ppermute(whole, "sector", up)
            if s == 0:
                after = lax.ppermute(whole, "sector", down)

    with jax.named_scope("second"):
        blocks = [b for both in zip(mine, theirs) for b in both]
        acc, sums, own = call(
            functools.partial(inner_kernel, dims),
            [
                square,
                jax.ShapeDtypeStruct((8, size), jnp.float32),
                pltpu.VMEM((sectors, size, size), jnp.bfloat16),
            ],
            (sector_shifts, sector_sizes),
            (*blocks, lanczos_vector, left, right),
            flops=terms * pair_flops,
        )
        cuts = sector_cuts(acc, own, before, after, True)
        totals = [low_sum(*c) for c in cuts]

    with jax.named_scope("scalars"):
        sums = after_all(sums, *cuts[-1])
        if groups & (groups - 1) == 0:
            reach = 1
            while reach < groups:
                got = lax.ppermute(sums, "sector", [(i, i ^ reach) for i in range(groups)])
                sums = after_all(sums + got, totals[0])
                reach *= 2
        else:
            sums = lax.psum(sums, "sector")
        sums = after_all(sums, *totals)
        out_rows = jax.ShapeDtypeStruct((sectors, span, size), jnp.float32)
        next_rows, base, factor = call(
            functools.partial(finish_kernel, dims, cells, scale),
            [out_rows, rows, rows],
            (sector_sizes,),
            (sums, start, left_column, right_energy, shifted, mixed),
        )

    with jax.named_scope("second"):
        sums = [sum(p.astype(jnp.float32) for p in high_parts(total)) for total in totals]
        next_sigma = base + factor * jnp.stack(sums)
    return next_rows, next_sigma


def solution(mesh):
    return jax.shard_map(
        on_device,
        mesh=mesh,
        in_specs=(
            P("sector", None, None),
            P("sector", "term", None, None),
            P("sector", "term", None, None),
            P("sector", None),
            P("sector", None),
            P("term"),
            P("sector"),
        ),
        out_specs=(P("sector", "term", None), P("sector", "term", None)),
        check_vma=False,
    )
```

```python
import functools
import jax
import jax.numpy as jnp
from jax import lax
from jax.experimental import pallas as pl
from jax.experimental.pallas import tpu as pltpu
from jax.sharding import PartitionSpec as P

epsilon = 1e-06
NT = (((1,), (1,)), ((), ()))
GUESS = 4.5


def other(hi, step, count):
    return hi ^ step if count & (count - 1) == 0 else (step - hi) % count


def traced_other(hi, step, count):
    return hi ^ step if count & (count - 1) == 0 else lax.rem(step - hi + count, count)


def pairs_low(size):
    return [(i, i ^ 1) for i in range(size)]


def pairs_high(size, low, step):
    count = size // low
    return [(i, other(i // low, step, count) * low + i % low) for i in range(size)]


def row_finder(count, low, span):
    rank = lax.axis_index("term")
    hi, lo = rank // low, lax.rem(rank, low)

    def row_of(step, far):
        digit = 1 - lo if far else lo
        return pl.multiple_of((traced_other(hi, step, count) * low + digit) * span, span)

    return row_of


def add_pair(acc, left, right, block):
    mixed = jnp.dot(left[...], block[...], preferred_element_type=jnp.float32)
    acc[...] += lax.dot_general(
        mixed.astype(jnp.bfloat16), right[...], NT, preferred_element_type=jnp.float32
    )


def add_inner(dims, s, shift_ref, acc, left, right, wb, before_term=lambda t: None):
    sectors, terms = dims[:2]
    for t in range(terms):
        before_term(t)
        partner = s + shift_ref[t]

        @pl.when((partner >= 0) & (partner < sectors))
        def _():
            add_pair(acc, left.at[s, t], right.at[s, t], wb.at[partner])


def add_outer(dims, s, gathered, shift_ref, acc, left, right, blocks, wb):
    sectors, terms, size, count, low, span = dims
    row_of = row_finder(count, low, span)
    here, groups = lax.axis_index("sector"), lax.axis_size("sector")
    for block, side in zip(blocks, sides_of(s, sectors)):
        if gathered:
            for step in range(count):
                for far in range(low):
                    wb[pl.ds(row_of(step, far), span), :] = block[far, step]
            held = wb
        else:
            held = block.at[0]
        there = here > 0 if side < 0 else here < groups - 1
        for t in range(terms):

            @pl.when((shift_ref[t] == side) & there)
            def _():
                add_pair(acc, left.at[s, t], right.at[s, t], held)


def cut(dims, acc, send_ref, keep_ref):
    sectors, terms, size, count, low, span = dims
    row_of = row_finder(count, low, span)
    for step in range(count):
        if low > 1:
            send_ref[step] = acc[pl.ds(row_of(step, 1), span), :].astype(jnp.bfloat16)
        keep_ref[step] = acc[pl.ds(row_of(step, 0), span), :]


def sides_of(s, sectors):
    return ([-1] if s == 0 else []) + ([1] if s == sectors - 1 else [])


def live_tile(shape, first_row, limit):
    row = first_row + lax.broadcasted_iota(jnp.int32, shape, 0)
    return (row < limit) & (lax.broadcasted_iota(jnp.int32, shape, 1) < limit)


def energy_rows(left_row, right_row, s, first, span):
    shape = (span, left_row.shape[1])
    row = first + lax.broadcasted_iota(jnp.int32, shape, 0)
    here = row == lax.broadcasted_iota(jnp.int32, shape, 1)
    left = jnp.sum(jnp.where(here, left_row[s : s + 1, :], 0.0), axis=1, keepdims=True)
    return left + right_row[s : s + 1, :]


def round_kernel(size_hbm, vector_hbm, rounded, first_block, last_block, vector, sizes, sems):
    sectors, size = vector.shape[:2]
    parts = sems.shape[0] // sectors
    rows = size // parts
    tile = min(64, rows)
    limits = pltpu.make_async_copy(size_hbm, sizes, sems.at[sectors * parts])
    limits.start()
    copies = [
        pltpu.make_async_copy(
            vector_hbm.at[s, pl.ds(n * rows, rows), :],
            vector.at[s, pl.ds(n * rows, rows), :],
            sems.at[s * parts + n],
        )
        for s in range(sectors)
        for n in range(parts)
    ]
    for copy in copies:
        copy.start()
    limits.wait()
    for s in range(sectors):
        for n in range(parts):
            copies[s * parts + n].wait()

            @pl.loop(0, rows // tile)
            def _(k):
                first = pl.multiple_of(n * rows + k * tile, tile)
                part = pl.ds(first, tile)
                live = live_tile((tile, size), first, sizes[s])
                value = jnp.where(live, vector[s, part, :], 0.0).astype(jnp.bfloat16)
                rounded[s, part, :] = value
                if s == 0:
                    first_block[0, part, :] = value
                if s == sectors - 1:
                    last_block[0, part, :] = value


def load_kernel(
    dims, shift_ref, size_ref, wb, left_hbm, right_hbm, vector_hbm,
    acc, left, right, start, sems, row_sems,
):
    sectors, terms, size, count, low, span = dims
    first = row_finder(count, low, span)(0, 0)
    rows = [
        pltpu.make_async_copy(vector_hbm.at[s, pl.ds(first, span), :], start.at[s], row_sems.at[s])
        for s in range(sectors)
    ]
    copies = {
        (s, t): [
            pltpu.make_async_copy(hbm.at[s, t], vmem.at[s, t], sems.at[k, s, t])
            for k, (hbm, vmem) in enumerate(((left_hbm, left), (right_hbm, right)))
        ]
        for s in range(sectors)
        for t in range(terms)
    }
    for pair in copies.values():
        for copy in pair:
            copy.start()
    for copy in rows:
        copy.start()
    acc[...] = jnp.zeros_like(acc)

    def arrived(t):
        for copy in copies[0, t]:
            copy.wait()

    add_inner(dims, 0, shift_ref, acc, left, right, wb, arrived)
    for s in range(sectors):
        rows[s].wait()
        live = live_tile((span, size), first, size_ref[s])
        start[s] = jnp.where(live, start[s], 0.0)
    for s in range(1, sectors):
        for t in range(terms):
            for copy in copies[s, t]:
                copy.wait()


def inner_kernel(dims, shift_ref, size_ref, *refs):
    sectors, terms, size, count, low, span = dims
    blocks, refs = refs[: 2 * sectors], refs[2 * sectors :]
    vector_ref, left, right, acc, sums, wb = refs
    acc[...] = jnp.zeros_like(acc)
    sums[...] = jnp.zeros_like(sums)
    row_of = row_finder(count, low, span)
    for s in range(sectors):
        for step in range(count):
            for far in range(low):
                wb[s, pl.ds(row_of(step, far), span), :] = blocks[2 * s + far][step]
    tile = min(64, size)
    for s in range(sectors):

        @pl.loop(0, size // tile)
        def _(n):
            first = pl.multiple_of(n * tile, tile)
            rows = pl.ds(first, tile)
            live = live_tile((tile, size), first, size_ref[s])
            start = jnp.where(live, vector_ref[s, rows, :], 0.0)
            shifted = wb[s, rows, :].astype(jnp.float32)
            for k, term in enumerate((shifted * shifted, shifted * start, start * start)):
                sums[k : k + 1, :] += jnp.sum(term, 0, keepdims=True)

    add_inner(dims, 0, shift_ref, acc, left, right, wb)


def outer_kernel(dims, gathered, shift_ref, acc_ref, left, right, *refs):
    blocks, (send_ref, keep_ref, acc, wb) = refs[:-4], refs[-4:]
    acc[...] = acc_ref[...]
    add_outer(dims, 0, gathered, shift_ref, acc, left, right, blocks, wb)
    cut(dims, acc, send_ref, keep_ref)


def full_kernel(s, dims, gathered, shift_ref, own, left, right, *refs):
    blocks, (send_ref, keep_ref, acc, wb) = refs[:-4], refs[-4:]
    acc[...] = jnp.zeros_like(acc)
    add_inner(dims, s, shift_ref, acc, left, right, own)
    add_outer(dims, s, gathered, shift_ref, acc, left, right, blocks, wb)
    cut(dims, acc, send_ref, keep_ref)


def shift_kernel(dims, scale, size_ref, start, left_row, right_row, *refs):
    sectors, terms, size, count, low, span = dims
    parts, (held_ref, shifted_ref, mixed_ref) = refs[:-3], refs[-3:]
    first = row_finder(count, low, span)(0, 0)
    for s in range(sectors):
        total = parts[s * count][...]
        for k in range(1, count):
            total += parts[s * count + k][...].astype(jnp.float32)
        mixed = jnp.where(live_tile((span, size), first, size_ref[s]), scale * total, 0.0)
        energy = energy_rows(left_row, right_row, s, first, span)
        shifted = mixed + (energy - GUESS) * start[s]
        held_ref[s] = shifted.astype(jnp.bfloat16)
        shifted_ref[s] = shifted
        mixed_ref[s] = mixed


def finish_kernel(
    dims, cells, scale, size_ref, sums, start, left_row, right_row, shifted, mixed,
    next_ref, base_ref, factor_ref,
):
    sectors, terms, size, count, low, span = dims
    first = row_finder(count, low, span)(0, 0)
    shifted_sq, overlap, norm_sq = [
        jnp.sum(sums[k : k + 1, :], axis=1, keepdims=True) for k in range(3)
    ]
    correlation = overlap + GUESS * norm_sq
    ritz = (correlation / cells) / (norm_sq / cells + epsilon)
    delta = ritz - GUESS
    res_sq = shifted_sq - 2.0 * delta * overlap + delta * delta * norm_sq
    inverse = lax.rsqrt(res_sq / cells + epsilon)
    for s in range(sectors):
        vector = (shifted[s] - delta * start[s]) * inverse
        energy = energy_rows(left_row, right_row, s, first, span)
        next_ref[s] = vector
        base_ref[s] = energy * vector - (delta * inverse) * mixed[s]
        live = live_tile((span, size), first, size_ref[s])
        factor_ref[s] = jnp.where(live, scale * inverse, 0.0)


SMEM = pl.BlockSpec(memory_space=pltpu.SMEM)
VMEM = pl.BlockSpec(memory_space=pltpu.VMEM)
HBM = pl.BlockSpec(memory_space=pltpu.HBM)
LIMIT = pltpu.CompilerParams(vmem_limit_bytes=24 * 2**20)


def call(kernel, out_shape, scalars, arrays, matrices=(), scratch=(), flops=2**20):
    matrices = [pltpu.with_memory_space_constraint(m, pltpu.HBM) for m in matrices]
    return pl.pallas_call(
        kernel,
        out_shape=out_shape,
        in_specs=[SMEM] * len(scalars) + [VMEM] * len(arrays) + [HBM] * len(matrices),
        out_specs=[VMEM] * len(out_shape),
        scratch_shapes=scratch,
        compiler_params=LIMIT,
        cost_estimate=pl.CostEstimate(flops=flops, bytes_accessed=flops // 256, transcendentals=0),
    )(*scalars, *arrays, *matrices)


def after_all(value, *others):
    return lax.optimization_barrier((value, *others))[0]


def on_device(
    lanczos_vector, left_block, right_block, left_energy, right_energy, sector_shifts, sector_sizes
):
    sectors, size = lanczos_vector.shape[:2]
    terms, ranks = left_block.shape[1], lax.axis_size("term")
    groups = lax.axis_size("sector")
    scale = float(terms * ranks) ** (-0.5)
    cells = float(sectors * groups * size * size)
    span = size // ranks
    low = 2 if ranks % 2 == 0 else 1
    count = ranks // low
    up = [(i, i + 1) for i in range(groups - 1)]
    down = [(j, i) for i, j in up]
    dims = (sectors, terms, size, count, low, span)
    pair_flops = 4 * size**3
    rows = pltpu.VMEM((sectors, span, size), jnp.float32)
    square = pltpu.VMEM((size, size), jnp.float32)
    square_low = pltpu.VMEM((size, size), jnp.bfloat16)
    cut_shapes = [jax.ShapeDtypeStruct((count, span, size), d) for d in (jnp.bfloat16, jnp.float32)]

    def low_sum(send, keep):
        if low == 1:
            return keep
        return keep + lax.ppermute(send, "term", pairs_low(ranks)).astype(jnp.float32)

    def high_parts(total):
        return [total[0]] + [
            lax.ppermute(total[k].astype(jnp.bfloat16), "term", pairs_high(ranks, low, k))
            for k in range(1, count)
        ]

    def sector_cuts(acc, own, before, after, gathered):
        halos = {-1: before, 1: after}
        cuts = []
        for s in range(sectors):
            blocks = [halos[side] for side in sides_of(s, sectors)]
            if s == 0:
                kernel, flops = functools.partial(outer_kernel, dims, gathered), pair_flops
            else:
                kernel = functools.partial(full_kernel, s, dims, gathered)
                flops = terms * pair_flops
            first = acc if s == 0 else own
            cuts.append(
                call(
                    kernel, cut_shapes, (sector_shifts,), (first, left, right, *blocks),
                    scratch=[square, square_low], flops=flops,
                )
            )
        return cuts

    with jax.named_scope("first"):
        parts = 2 if size % 256 == 0 else 1
        block = jax.ShapeDtypeStruct((1, size, size), jnp.bfloat16)
        rounded, first_block, last_block = call(
            round_kernel,
            [pltpu.VMEM(lanczos_vector.shape, jnp.bfloat16), block, block],
            (),
            (),
            (sector_sizes, lanczos_vector),
            [
                pltpu.VMEM(lanczos_vector.shape, jnp.float32),
                pltpu.SMEM((sectors,), jnp.int32),
                pltpu.SemaphoreType.DMA((sectors * parts + 1,)),
            ],
        )
        before = lax.ppermute(last_block, "sector", up)
        after = lax.ppermute(first_block, "sector", down)
        matrices = pltpu.VMEM(left_block.shape, jnp.bfloat16)
        acc, left, right, start = call(
            functools.partial(load_kernel, dims),
            [square, matrices, matrices, rows],
            (sector_shifts, sector_sizes),
            (rounded,),
            (left_block, right_block, lanczos_vector),
            [pltpu.SemaphoreType.DMA((2, sectors, terms)), pltpu.SemaphoreType.DMA((sectors,))],
            terms * pair_flops,
        )
        totals = [low_sum(*c) for c in sector_cuts(acc, rounded, before, after, False)]
        parts = [part for total in totals for part in high_parts(total)]
        held, shifted, mixed = call(
            functools.partial(shift_kernel, dims, scale),
            [jax.ShapeDtypeStruct((sectors, span, size), jnp.bfloat16), rows, rows],
            (sector_sizes,),
            (start, left_energy, right_energy, *parts),
        )

    with jax.named_scope("gather"):
        mine, theirs = [None] * sectors, [None] * sectors
        for s in reversed(range(sectors)):
            own = held[s]
            hops = [lax.ppermute(own, "term", pairs_high(ranks, low, k)) for k in range(1, count)]
            mine[s] = jnp.stack([own, *hops])
            theirs[s] = lax.ppermute(mine[s], "term", pairs_low(ranks)) if low > 1 else mine[s]
            whole = jnp.stack([mine[s], theirs[s]])
            if s == sectors - 1:
                before = lax.ppermute(whole, "sector", up)
            if s == 0:
                after = lax.ppermute(whole, "sector", down)

    with jax.named_scope("second"):
        blocks = [b for both in zip(mine, theirs) for b in both]
        acc, sums, own = call(
            functools.partial(inner_kernel, dims),
            [
                square,
                jax.ShapeDtypeStruct((8, size), jnp.float32),
                pltpu.VMEM((sectors, size, size), jnp.bfloat16),
            ],
            (sector_shifts, sector_sizes),
            (*blocks, lanczos_vector, left, right),
            flops=terms * pair_flops,
        )
        cuts = sector_cuts(acc, own, before, after, True)
        totals = [low_sum(*c) for c in cuts]

    with jax.named_scope("scalars"):
        sums = after_all(sums, *cuts[-1])
        if groups & (groups - 1) == 0:
            reach = 1
            while reach < groups:
                got = lax.ppermute(sums, "sector", [(i, i ^ reach) for i in range(groups)])
                sums = after_all(sums + got, totals[0])
                reach *= 2
        else:
            sums = lax.psum(sums, "sector")
        sums = after_all(sums, *totals)
        out_rows = jax.ShapeDtypeStruct((sectors, span, size), jnp.float32)
        next_rows, base, factor = call(
            functools.partial(finish_kernel, dims, cells, scale),
            [out_rows, rows, rows],
            (sector_sizes,),
            (sums, start, left_energy, right_energy, shifted, mixed),
        )

    with jax.named_scope("second"):
        sums = [sum(p.astype(jnp.float32) for p in high_parts(total)) for total in totals]
        next_sigma = base + factor * jnp.stack(sums)
    return next_rows, next_sigma


def solution(mesh):
    return jax.shard_map(
        on_device,
        mesh=mesh,
        in_specs=(
            P("sector", None, None),
            P("sector", "term", None, None),
            P("sector", "term", None, None),
            P("sector", None),
            P("sector", None),
            P("term"),
            P("sector"),
        ),
        out_specs=(P("sector", "term", None), P("sector", "term", None)),
        check_vma=False,
    )
```

```python
import functools
import jax
import jax.numpy as jnp
from jax import lax
from jax.experimental import pallas as pl
from jax.experimental.pallas import tpu as pltpu
from jax.sharding import PartitionSpec as P

epsilon = 1e-06
NT = (((1,), (1,)), ((), ()))
GUESS = 4.5


def other(hi, step, count):
    return hi ^ step if count & (count - 1) == 0 else (step - hi) % count


def traced_other(hi, step, count):
    return hi ^ step if count & (count - 1) == 0 else lax.rem(step - hi + count, count)


def pairs_low(size):
    return [(i, i ^ 1) for i in range(size)]


def pairs_high(size, low, step):
    count = size // low
    return [(i, other(i // low, step, count) * low + i % low) for i in range(size)]


def row_finder(count, low, span):
    rank = lax.axis_index("term")
    hi, lo = rank // low, lax.rem(rank, low)

    def row_of(step, far):
        digit = 1 - lo if far else lo
        return pl.multiple_of((traced_other(hi, step, count) * low + digit) * span, span)

    return row_of


def add_pair(acc, left, right, block):
    mixed = jnp.dot(left[...], block[...], preferred_element_type=jnp.float32)
    acc[...] += lax.dot_general(
        mixed.astype(jnp.bfloat16), right[...], NT, preferred_element_type=jnp.float32
    )


def add_inner(dims, s, shift_ref, acc, left, right, wb, before_term=lambda t: None):
    sectors, terms = dims[:2]
    for t in range(terms):
        before_term(t)
        partner = s + shift_ref[t]

        @pl.when((partner >= 0) & (partner < sectors))
        def _():
            add_pair(acc, left.at[s, t], right.at[s, t], wb.at[partner])


def add_outer(dims, s, gathered, shift_ref, acc, left, right, blocks, wb):
    sectors, terms, size, count, low, span = dims
    row_of = row_finder(count, low, span)
    here, groups = lax.axis_index("sector"), lax.axis_size("sector")
    for block, side in zip(blocks, sides_of(s, sectors)):
        if gathered:
            for step in range(count):
                for far in range(low):
                    wb[pl.ds(row_of(step, far), span), :] = block[far, step]
            held = wb
        else:
            held = block.at[0]
        there = here > 0 if side < 0 else here < groups - 1
        for t in range(terms):

            @pl.when((shift_ref[t] == side) & there)
            def _():
                add_pair(acc, left.at[s, t], right.at[s, t], held)


def cut(dims, acc, send_ref, keep_ref):
    sectors, terms, size, count, low, span = dims
    row_of = row_finder(count, low, span)
    for step in range(count):
        if low > 1:
            send_ref[step] = acc[pl.ds(row_of(step, 1), span), :].astype(jnp.bfloat16)
        keep_ref[step] = acc[pl.ds(row_of(step, 0), span), :]


def sides_of(s, sectors):
    return ([-1] if s == 0 else []) + ([1] if s == sectors - 1 else [])


def live_tile(shape, first_row, limit):
    row = first_row + lax.broadcasted_iota(jnp.int32, shape, 0)
    return (row < limit) & (lax.broadcasted_iota(jnp.int32, shape, 1) < limit)


def energy_rows(left_row, right_row, s, first, span):
    shape = (span, left_row.shape[1])
    row = first + lax.broadcasted_iota(jnp.int32, shape, 0)
    here = row == lax.broadcasted_iota(jnp.int32, shape, 1)
    left = jnp.sum(jnp.where(here, left_row[s : s + 1, :], 0.0), axis=1, keepdims=True)
    return left + right_row[s : s + 1, :]


def round_kernel(size_hbm, vector_hbm, rounded, first_block, last_block, vector, sizes, sems):
    sectors, size = vector.shape[:2]
    parts = sems.shape[0] // sectors
    rows = size // parts
    tile = min(64, rows)
    limits = pltpu.make_async_copy(size_hbm, sizes, sems.at[sectors * parts])
    limits.start()
    copies = [
        pltpu.make_async_copy(
            vector_hbm.at[s, pl.ds(n * rows, rows), :],
            vector.at[s, pl.ds(n * rows, rows), :],
            sems.at[s * parts + n],
        )
        for s in range(sectors)
        for n in range(parts)
    ]
    for copy in copies:
        copy.start()
    limits.wait()
    for s in range(sectors):
        for n in range(parts):
            copies[s * parts + n].wait()

            @pl.loop(0, rows // tile)
            def _(k):
                first = pl.multiple_of(n * rows + k * tile, tile)
                part = pl.ds(first, tile)
                live = live_tile((tile, size), first, sizes[s])
                value = jnp.where(live, vector[s, part, :], 0.0).astype(jnp.bfloat16)
                rounded[s, part, :] = value
                if s == 0:
                    first_block[0, part, :] = value
                if s == sectors - 1:
                    last_block[0, part, :] = value


def load_kernel(
    dims, wb, shift_hbm, size_hbm, left_hbm, right_hbm, vector_hbm,
    acc, left, right, start, shift_ref, size_ref, sems, row_sems, scalar_sems,
):
    sectors, terms, size, count, low, span = dims
    scalars = [
        pltpu.make_async_copy(shift_hbm, shift_ref, scalar_sems.at[0]),
        pltpu.make_async_copy(size_hbm, size_ref, scalar_sems.at[1]),
    ]
    for copy in scalars:
        copy.start()
    first = row_finder(count, low, span)(0, 0)
    rows = [
        pltpu.make_async_copy(vector_hbm.at[s, pl.ds(first, span), :], start.at[s], row_sems.at[s])
        for s in range(sectors)
    ]
    copies = {
        (s, t): [
            pltpu.make_async_copy(hbm.at[s, t], vmem.at[s, t], sems.at[k, s, t])
            for k, (hbm, vmem) in enumerate(((left_hbm, left), (right_hbm, right)))
        ]
        for s in range(sectors)
        for t in range(terms)
    }
    for pair in copies.values():
        for copy in pair:
            copy.start()
    for copy in rows:
        copy.start()
    acc[...] = jnp.zeros_like(acc)
    for copy in scalars:
        copy.wait()

    def arrived(t):
        for copy in copies[0, t]:
            copy.wait()

    add_inner(dims, 0, shift_ref, acc, left, right, wb, arrived)
    for s in range(sectors):
        rows[s].wait()
        live = live_tile((span, size), first, size_ref[s])
        start[s] = jnp.where(live, start[s], 0.0)
    for s in range(1, sectors):
        for t in range(terms):
            for copy in copies[s, t]:
                copy.wait()


def inner_kernel(dims, s, shift_ref, *refs):
    sectors, terms, size, count, low, span = dims
    blocks, (left, right, acc, wb) = refs[: 2 * sectors], refs[2 * sectors :]
    acc[...] = jnp.zeros_like(acc)
    row_of = row_finder(count, low, span)
    for e in range(sectors):
        for step in range(count):
            for far in range(low):
                wb[e, pl.ds(row_of(step, far), span), :] = blocks[2 * e + far][step]
    add_inner(dims, s, shift_ref, acc, left, right, wb)


def sums_kernel(dims, size_ref, vector_ref, wb, sums):
    sectors, size = dims[0], dims[2]
    sums[...] = jnp.zeros_like(sums)
    tile = min(64, size)
    for s in range(sectors):

        @pl.loop(0, size // tile)
        def _(n):
            first = pl.multiple_of(n * tile, tile)
            rows = pl.ds(first, tile)
            live = live_tile((tile, size), first, size_ref[s])
            start = jnp.where(live, vector_ref[s, rows, :], 0.0)
            shifted = wb[s, rows, :].astype(jnp.float32)
            for k, term in enumerate((shifted * shifted, shifted * start, start * start)):
                sums[k : k + 1, :] += jnp.sum(term, 0, keepdims=True)


def outer_kernel(dims, s, gathered, shift_ref, acc_ref, left, right, *refs):
    blocks, (send_ref, keep_ref, acc, wb) = refs[:-4], refs[-4:]
    acc[...] = acc_ref[...]
    add_outer(dims, s, gathered, shift_ref, acc, left, right, blocks, wb)
    cut(dims, acc, send_ref, keep_ref)


def full_kernel(dims, s, gathered, shift_ref, own, left, right, *refs):
    blocks, (send_ref, keep_ref, acc, wb) = refs[:-4], refs[-4:]
    acc[...] = jnp.zeros_like(acc)
    add_inner(dims, s, shift_ref, acc, left, right, own)
    add_outer(dims, s, gathered, shift_ref, acc, left, right, blocks, wb)
    cut(dims, acc, send_ref, keep_ref)


def shift_kernel(dims, s, scale, size_ref, start, left_row, right_row, *refs):
    sectors, terms, size, count, low, span = dims
    parts, (held_ref, shifted_ref, mixed_ref) = refs[:-3], refs[-3:]
    first = row_finder(count, low, span)(0, 0)
    total = parts[0][...]
    for part in parts[1:]:
        total += part[...].astype(jnp.float32)
    mixed = jnp.where(live_tile((span, size), first, size_ref[s]), scale * total, 0.0)
    energy = energy_rows(left_row, right_row, s, first, span)
    shifted = mixed + (energy - GUESS) * start[s]
    held_ref[...] = shifted.astype(jnp.bfloat16)
    shifted_ref[...] = shifted
    mixed_ref[...] = mixed


def finish_kernel(dims, cells, scale, size_ref, sums, start, left_row, right_row, *refs):
    sectors, terms, size, count, low, span = dims
    (shifted, mixed), refs = (refs[:sectors], refs[sectors : 2 * sectors]), refs[2 * sectors :]
    next_ref, base_ref, factor_ref = refs
    first = row_finder(count, low, span)(0, 0)
    shifted_sq, overlap, norm_sq = [
        jnp.sum(sums[k : k + 1, :], axis=1, keepdims=True) for k in range(3)
    ]
    correlation = overlap + GUESS * norm_sq
    ritz = (correlation / cells) / (norm_sq / cells + epsilon)
    delta = ritz - GUESS
    res_sq = shifted_sq - 2.0 * delta * overlap + delta * delta * norm_sq
    inverse = lax.rsqrt(res_sq / cells + epsilon)
    for s in range(sectors):
        vector = (shifted[s][...] - delta * start[s]) * inverse
        energy = energy_rows(left_row, right_row, s, first, span)
        next_ref[s] = vector
        base_ref[s] = energy * vector - (delta * inverse) * mixed[s][...]
        live = live_tile((span, size), first, size_ref[s])
        factor_ref[s] = jnp.where(live, scale * inverse, 0.0)


SMEM = pl.BlockSpec(memory_space=pltpu.SMEM)
VMEM = pl.BlockSpec(memory_space=pltpu.VMEM)
HBM = pl.BlockSpec(memory_space=pltpu.HBM)
LIMIT = pltpu.CompilerParams(vmem_limit_bytes=24 * 2**20)


def call(kernel, out_shape, scalars, arrays, matrices=(), scratch=(), flops=2**20):
    matrices = [pltpu.with_memory_space_constraint(m, pltpu.HBM) for m in matrices]
    return pl.pallas_call(
        kernel,
        out_shape=out_shape,
        in_specs=[SMEM] * len(scalars) + [VMEM] * len(arrays) + [HBM] * len(matrices),
        out_specs=[VMEM] * len(out_shape),
        scratch_shapes=scratch,
        compiler_params=LIMIT,
        cost_estimate=pl.CostEstimate(flops=flops, bytes_accessed=flops // 256, transcendentals=0),
    )(*scalars, *arrays, *matrices)


def after_all(value, *others):
    return lax.optimization_barrier((value, *others))[0]


def on_device(
    lanczos_vector, left_block, right_block, left_energy, right_energy, sector_shifts, sector_sizes
):
    sectors, size = lanczos_vector.shape[:2]
    terms, ranks = left_block.shape[1], lax.axis_size("term")
    groups = lax.axis_size("sector")
    scale = float(terms * ranks) ** (-0.5)
    cells = float(sectors * groups * size * size)
    span = size // ranks
    low = 2 if ranks % 2 == 0 else 1
    count = ranks // low
    up = [(i, i + 1) for i in range(groups - 1)]
    down = [(j, i) for i, j in up]
    dims = (sectors, terms, size, count, low, span)
    pair_flops = 4 * size**3
    rows = pltpu.VMEM((sectors, span, size), jnp.float32)
    square = pltpu.VMEM((size, size), jnp.float32)
    square_low = pltpu.VMEM((size, size), jnp.bfloat16)
    cut_shapes = [jax.ShapeDtypeStruct((count, span, size), d) for d in (jnp.bfloat16, jnp.float32)]

    def low_sum(send, keep):
        if low == 1:
            return keep
        return keep + lax.ppermute(send, "term", pairs_low(ranks)).astype(jnp.float32)

    hops = range(count - 1, 0, -1)

    def high_parts(total):
        return [total[0]] + [
            lax.ppermute(total[k].astype(jnp.bfloat16), "term", pairs_high(ranks, low, k))
            for k in hops
        ]

    def sector_cuts(order, acc, own, before, after, gathered):
        halos, cuts = {-1: before, 1: after}, [None] * sectors
        for s in order:
            blocks = [halos[side] for side in sides_of(s, sectors)]
            opening = s == order[0]
            cuts[s] = call(
                functools.partial(outer_kernel if opening else full_kernel, dims, s, gathered),
                cut_shapes,
                (sector_shifts,),
                (acc if opening else own, left, right, *blocks),
                scratch=[square, square_low],
                flops=terms * pair_flops // (3 if opening else 1),
            )
        return cuts

    with jax.named_scope("first"):
        parts = 2 if size % 256 == 0 else 1
        block = jax.ShapeDtypeStruct((1, size, size), jnp.bfloat16)
        rounded, first_block, last_block = call(
            round_kernel,
            [pltpu.VMEM(lanczos_vector.shape, jnp.bfloat16), block, block],
            (),
            (),
            (sector_sizes, lanczos_vector),
            [
                pltpu.VMEM(lanczos_vector.shape, jnp.float32),
                pltpu.SMEM((sectors,), jnp.int32),
                pltpu.SemaphoreType.DMA((sectors * parts + 1,)),
            ],
        )
        before = lax.ppermute(last_block, "sector", up)
        after = lax.ppermute(first_block, "sector", down)
        matrices = pltpu.VMEM(left_block.shape, jnp.bfloat16)
        acc, left, right, start = call(
            functools.partial(load_kernel, dims),
            [square, matrices, matrices, rows],
            (),
            (rounded,),
            (sector_shifts, sector_sizes, left_block, right_block, lanczos_vector),
            [
                pltpu.SMEM((terms,), jnp.int32),
                pltpu.SMEM((sectors,), jnp.int32),
                pltpu.SemaphoreType.DMA((2, sectors, terms)),
                pltpu.SemaphoreType.DMA((sectors,)),
                pltpu.SemaphoreType.DMA((2,)),
            ],
            terms * pair_flops,
        )
        order = list(range(sectors))
        cuts = sector_cuts(order, acc, rounded, before, after, False)
        totals = [low_sum(*c) for c in cuts]

    with jax.named_scope("gather"):
        mine, theirs, shifted, mixed = [[None] * sectors for _ in range(4)]
        row = pltpu.VMEM((span, size), jnp.float32)
        for s in order:
            own, shifted[s], mixed[s] = call(
                functools.partial(shift_kernel, dims, s, scale),
                [jax.ShapeDtypeStruct((span, size), jnp.bfloat16), row, row],
                (sector_sizes,),
                (start, left_energy, right_energy, *high_parts(totals[s])),
            )
            got = {k: lax.ppermute(own, "term", pairs_high(ranks, low, k)) for k in hops}
            mine[s] = jnp.stack([own] + [got[k] for k in range(1, count)])
            theirs[s] = lax.ppermute(mine[s], "term", pairs_low(ranks)) if low > 1 else mine[s]
            whole = jnp.stack([mine[s], theirs[s]])
            if s == 0:
                after = lax.ppermute(whole, "sector", down)
            if s == sectors - 1:
                before = lax.ppermute(whole, "sector", up)

    with jax.named_scope("second"):
        order = order[::-1]
        blocks = [b for both in zip(mine, theirs) for b in both]
        acc, own = call(
            functools.partial(inner_kernel, dims, order[0]),
            [square, pltpu.VMEM((sectors, size, size), jnp.bfloat16)],
            (sector_shifts,),
            (*blocks, left, right),
            flops=terms * pair_flops,
        )
        cuts = sector_cuts(order, acc, own, before, after, True)
        totals = [low_sum(*c) for c in cuts]

    with jax.named_scope("scalars"):
        (sums,) = call(
            functools.partial(sums_kernel, dims),
            [jax.ShapeDtypeStruct((8, size), jnp.float32)],
            (sector_sizes,),
            (lanczos_vector, after_all(own, *cuts[order[-1]])),
        )
        sums = after_all(sums, totals[order[0]])
        if groups & (groups - 1) == 0:
            reach = 1
            while reach < groups:
                got = lax.ppermute(sums, "sector", [(i, i ^ reach) for i in range(groups)])
                sums = after_all(sums + got, totals[order[-1]])
                reach *= 2
        else:
            sums = lax.psum(sums, "sector")
        out_rows = jax.ShapeDtypeStruct((sectors, span, size), jnp.float32)
        next_rows, base, factor = call(
            functools.partial(finish_kernel, dims, cells, scale),
            [out_rows, rows, rows],
            (sector_sizes,),
            (sums, start, left_energy, right_energy, *shifted, *mixed),
        )

    with jax.named_scope("second"):
        parts = {s: high_parts(totals[s]) for s in order}
        last = [sum(p.astype(jnp.float32) for p in parts[s]) for s in range(sectors)]
        next_sigma = base + factor * jnp.stack(last)
    return next_rows, next_sigma


def solution(mesh):
    return jax.shard_map(
        on_device,
        mesh=mesh,
        in_specs=(
            P("sector", None, None),
            P("sector", "term", None, None),
            P("sector", "term", None, None),
            P("sector", None),
            P("sector", None),
            P("term"),
            P("sector"),
        ),
        out_specs=(P("sector", "term", None), P("sector", "term", None)),
        check_vma=False,
    )
```

```python
import functools
import jax
import jax.numpy as jnp
from jax import lax
from jax.experimental import pallas as pl
from jax.experimental.pallas import tpu as pltpu
from jax.sharding import PartitionSpec as P

epsilon = 1e-06
NT = (((1,), (1,)), ((), ()))
GUESS = 4.5


def other(hi, step, count):
    return hi ^ step if count & (count - 1) == 0 else (step - hi) % count


def traced_other(hi, step, count):
    return hi ^ step if count & (count - 1) == 0 else lax.rem(step - hi + count, count)


def pairs_low(size):
    return [(i, i ^ 1) for i in range(size)]


def pairs_high(size, low, step):
    count = size // low
    return [(i, other(i // low, step, count) * low + i % low) for i in range(size)]


def powers(count):
    return [1 << b for b in range(count.bit_length() - 1)] if count & (count - 1) == 0 else None


def gather_order(count):
    steps = powers(count)
    if steps is None:
        return list(range(count))
    order = [0]
    for step in reversed(steps):
        order += [o ^ step for o in order]
    return order


def row_finder(count, low, span):
    rank = lax.axis_index("term")
    hi, lo = rank // low, lax.rem(rank, low)

    def row_of(step, far):
        digit = 1 - lo if far else lo
        return pl.multiple_of((traced_other(hi, step, count) * low + digit) * span, span)

    return row_of


def add_pair(acc, left, right, block):
    mixed = jnp.dot(left[...], block[...], preferred_element_type=jnp.float32)
    acc[...] += lax.dot_general(
        mixed.astype(jnp.bfloat16), right[...], NT, preferred_element_type=jnp.float32
    )


def add_inner(dims, s, shift_ref, acc, left, right, wb, before_term=lambda t: None):
    sectors, terms = dims[:2]
    for t in range(terms):
        before_term(t)
        partner = s + shift_ref[t]

        @pl.when((partner >= 0) & (partner < sectors))
        def _():
            add_pair(acc, left.at[s, t], right.at[s, t], wb.at[partner])


def place_rows(dims, wb, pieces):
    sectors, terms, size, count, low, span = dims
    row_of = row_finder(count, low, span)
    for far in range(low):
        for n, step in enumerate(gather_order(count)):
            wb[pl.ds(row_of(step, far), span), :] = pieces[far][n]


def add_outer(dims, s, gathered, shift_ref, acc, left, right, blocks, wb):
    sectors, terms = dims[:2]
    here, groups = lax.axis_index("sector"), lax.axis_size("sector")
    for n, side in enumerate(sides_of(s, sectors)):
        if gathered:
            place_rows(dims, wb, blocks[2 * n : 2 * n + 2])
            held = wb
        else:
            held = blocks[n].at[0]
        there = here > 0 if side < 0 else here < groups - 1
        for t in range(terms):

            @pl.when((shift_ref[t] == side) & there)
            def _():
                add_pair(acc, left.at[s, t], right.at[s, t], held)


def cut(dims, acc, send_ref, keep_ref):
    sectors, terms, size, count, low, span = dims
    row_of = row_finder(count, low, span)
    for step in range(count):
        if low > 1:
            send_ref[step] = acc[pl.ds(row_of(step, 1), span), :].astype(jnp.bfloat16)
        keep_ref[step] = acc[pl.ds(row_of(step, 0), span), :]


def sides_of(s, sectors):
    return ([-1] if s == 0 else []) + ([1] if s == sectors - 1 else [])


def live_tile(shape, first_row, limit):
    row = first_row + lax.broadcasted_iota(jnp.int32, shape, 0)
    return (row < limit) & (lax.broadcasted_iota(jnp.int32, shape, 1) < limit)


def energy_rows(left_row, right_row, s, first, span):
    shape = (span, left_row.shape[1])
    row = first + lax.broadcasted_iota(jnp.int32, shape, 0)
    here = row == lax.broadcasted_iota(jnp.int32, shape, 1)
    left = jnp.sum(jnp.where(here, left_row[s : s + 1, :], 0.0), axis=1, keepdims=True)
    return left + right_row[s : s + 1, :]


def round_kernel(size_hbm, vector_hbm, rounded, first_block, last_block, vector, sizes, sems):
    sectors, size = vector.shape[:2]
    parts = sems.shape[0] // sectors
    rows = size // parts
    tile = min(64, rows)
    limits = pltpu.make_async_copy(size_hbm, sizes, sems.at[sectors * parts])
    limits.start()
    copies = [
        pltpu.make_async_copy(
            vector_hbm.at[s, pl.ds(n * rows, rows), :],
            vector.at[s, pl.ds(n * rows, rows), :],
            sems.at[s * parts + n],
        )
        for s in range(sectors)
        for n in range(parts)
    ]
    for copy in copies:
        copy.start()
    limits.wait()
    for s in range(sectors):
        for n in range(parts):
            copies[s * parts + n].wait()

            @pl.loop(0, rows // tile)
            def _(k):
                first = pl.multiple_of(n * rows + k * tile, tile)
                part = pl.ds(first, tile)
                live = live_tile((tile, size), first, sizes[s])
                value = jnp.where(live, vector[s, part, :], 0.0).astype(jnp.bfloat16)
                rounded[s, part, :] = value
                if s == 0:
                    first_block[0, part, :] = value
                if s == sectors - 1:
                    last_block[0, part, :] = value


def load_kernel(
    dims, wb, shift_hbm, size_hbm, left_hbm, right_hbm, vector_hbm,
    acc, left, right, start, shift_ref, size_ref, sems, row_sems, scalar_sems,
):
    sectors, terms, size, count, low, span = dims
    scalars = [
        pltpu.make_async_copy(shift_hbm, shift_ref, scalar_sems.at[0]),
        pltpu.make_async_copy(size_hbm, size_ref, scalar_sems.at[1]),
    ]
    for copy in scalars:
        copy.start()
    first = row_finder(count, low, span)(0, 0)
    rows = [
        pltpu.make_async_copy(vector_hbm.at[s, pl.ds(first, span), :], start.at[s], row_sems.at[s])
        for s in range(sectors)
    ]
    copies = {
        (s, t): [
            pltpu.make_async_copy(hbm.at[s, t], vmem.at[s, t], sems.at[k, s, t])
            for k, (hbm, vmem) in enumerate(((left_hbm, left), (right_hbm, right)))
        ]
        for s in range(sectors)
        for t in range(terms)
    }
    for pair in copies.values():
        for copy in pair:
            copy.start()
    for copy in rows:
        copy.start()
    acc[...] = jnp.zeros_like(acc)
    for copy in scalars:
        copy.wait()

    def arrived(t):
        for copy in copies[0, t]:
            copy.wait()

    add_inner(dims, 0, shift_ref, acc, left, right, wb, arrived)
    for s in range(sectors):
        rows[s].wait()
        live = live_tile((span, size), first, size_ref[s])
        start[s] = jnp.where(live, start[s], 0.0)
    for s in range(1, sectors):
        for t in range(terms):
            for copy in copies[s, t]:
                copy.wait()


def inner_kernel(dims, s, shift_ref, *refs):
    sectors = dims[0]
    blocks, (left, right, acc, wb) = refs[: 2 * sectors], refs[2 * sectors :]
    acc[...] = jnp.zeros_like(acc)
    for e in range(sectors):
        place_rows(dims, wb.at[e], blocks[2 * e : 2 * e + 2])
    add_inner(dims, s, shift_ref, acc, left, right, wb)


def sums_kernel(dims, size_ref, vector_ref, wb, sums):
    sectors, size = dims[0], dims[2]
    sums[...] = jnp.zeros_like(sums)
    tile = min(64, size)
    for s in range(sectors):

        @pl.loop(0, size // tile)
        def _(n):
            first = pl.multiple_of(n * tile, tile)
            rows = pl.ds(first, tile)
            live = live_tile((tile, size), first, size_ref[s])
            start = jnp.where(live, vector_ref[s, rows, :], 0.0)
            shifted = wb[s, rows, :].astype(jnp.float32)
            for k, term in enumerate((shifted * shifted, shifted * start, start * start)):
                sums[k : k + 1, :] += jnp.sum(term, 0, keepdims=True)


def outer_kernel(dims, s, gathered, shift_ref, acc_ref, left, right, *refs):
    blocks, (send_ref, keep_ref, acc, wb) = refs[:-4], refs[-4:]
    acc[...] = acc_ref[...]
    add_outer(dims, s, gathered, shift_ref, acc, left, right, blocks, wb)
    cut(dims, acc, send_ref, keep_ref)


def full_kernel(dims, s, gathered, shift_ref, own, left, right, *refs):
    blocks, (send_ref, keep_ref, acc, wb) = refs[:-4], refs[-4:]
    acc[...] = jnp.zeros_like(acc)
    add_inner(dims, s, shift_ref, acc, left, right, own)
    add_outer(dims, s, gathered, shift_ref, acc, left, right, blocks, wb)
    cut(dims, acc, send_ref, keep_ref)


def shift_kernel(dims, s, scale, size_ref, start, left_row, right_row, *refs):
    sectors, terms, size, count, low, span = dims
    parts, (held_ref, shifted_ref, plus_ref, minus_ref) = refs[:-4], refs[-4:]
    first = row_finder(count, low, span)(0, 0)
    total = parts[0][...]
    for part in parts[1:]:
        total += part[...].astype(jnp.float32)
    mixed = jnp.where(live_tile((span, size), first, size_ref[s]), scale * total, 0.0)
    energy = energy_rows(left_row, right_row, s, first, span)
    shifted = mixed + (energy - GUESS) * start[s]
    held_ref[...] = shifted.astype(jnp.bfloat16)
    shifted_ref[...] = shifted
    plus_ref[...] = energy * shifted
    minus_ref[...] = energy * start[s] + mixed


def finish_kernel(dims, cells, scale, size_ref, sums, start, *refs):
    sectors, terms, size, count, low, span = dims
    shifted, plus, minus = [refs[k * sectors : (k + 1) * sectors] for k in range(3)]
    parts, (next_ref, sigma_ref) = refs[3 * sectors : -2], refs[-2:]
    first = row_finder(count, low, span)(0, 0)
    shifted_sq, overlap, norm_sq = [
        jnp.sum(sums[k : k + 1, :], axis=1, keepdims=True) for k in range(3)
    ]
    correlation = overlap + GUESS * norm_sq
    ritz = (correlation / cells) / (norm_sq / cells + epsilon)
    delta = ritz - GUESS
    res_sq = shifted_sq - 2.0 * delta * overlap + delta * delta * norm_sq
    inverse = lax.rsqrt(res_sq / cells + epsilon)
    each = len(parts) // sectors
    for s in range(sectors):
        next_ref[s] = (shifted[s][...] - delta * start[s]) * inverse
        total = parts[s * each][...]
        for part in parts[s * each + 1 : (s + 1) * each]:
            total += part[...].astype(jnp.float32)
        mixed = jnp.where(live_tile((span, size), first, size_ref[s]), scale * total, 0.0)
        sigma_ref[s] = (plus[s][...] - delta * minus[s][...] + mixed) * inverse


SMEM = pl.BlockSpec(memory_space=pltpu.SMEM)
VMEM = pl.BlockSpec(memory_space=pltpu.VMEM)
HBM = pl.BlockSpec(memory_space=pltpu.HBM)
LIMIT = pltpu.CompilerParams(vmem_limit_bytes=24 * 2**20)


def call(kernel, out_shape, scalars, arrays, matrices=(), scratch=(), flops=2**20):
    matrices = [pltpu.with_memory_space_constraint(m, pltpu.HBM) for m in matrices]
    return pl.pallas_call(
        kernel,
        out_shape=out_shape,
        in_specs=[SMEM] * len(scalars) + [VMEM] * len(arrays) + [HBM] * len(matrices),
        out_specs=[VMEM] * len(out_shape),
        scratch_shapes=scratch,
        compiler_params=LIMIT,
        cost_estimate=pl.CostEstimate(flops=flops, bytes_accessed=flops // 256, transcendentals=0),
    )(*scalars, *arrays, *matrices)


def after_all(value, *others):
    return lax.optimization_barrier((value, *others))[0]


def on_device(
    lanczos_vector, left_block, right_block, left_energy, right_energy, sector_shifts, sector_sizes
):
    sectors, size = lanczos_vector.shape[:2]
    terms, ranks = left_block.shape[1], lax.axis_size("term")
    groups = lax.axis_size("sector")
    scale = float(terms * ranks) ** (-0.5)
    cells = float(sectors * groups * size * size)
    span = size // ranks
    low = 2 if ranks % 2 == 0 else 1
    count = ranks // low
    up = [(i, i + 1) for i in range(groups - 1)]
    down = [(j, i) for i, j in up]
    dims = (sectors, terms, size, count, low, span)
    pair_flops = 4 * size**3
    rows = pltpu.VMEM((sectors, span, size), jnp.float32)
    square = pltpu.VMEM((size, size), jnp.float32)
    square_low = pltpu.VMEM((size, size), jnp.bfloat16)
    cut_shapes = [jax.ShapeDtypeStruct((count, span, size), d) for d in (jnp.bfloat16, jnp.float32)]

    def low_sum(send, keep):
        if low == 1:
            return keep
        return keep + lax.ppermute(send, "term", pairs_low(ranks)).astype(jnp.float32)

    steps = powers(count)

    def swap(value, step):
        return lax.ppermute(value, "term", pairs_high(ranks, low, step))

    def high_sums(totals, order):
        if steps is None:
            return {
                s: [totals[s][0]]
                + [swap(totals[s][k].astype(jnp.bfloat16), k) for k in range(1, count)]
                for s in order
            }
        parts = {s: [totals[s]] for s in order}
        for step in steps:
            ready = {s: sum(p.astype(jnp.float32) for p in parts[s]) for s in order}
            for s in order:
                half = ready[s].reshape(-1, 2, span, size)
                parts[s] = [half[:, 0], swap(half[:, 1].astype(jnp.bfloat16), step)]
        return {s: [p.reshape(span, size) for p in parts[s]] for s in order}

    def gather_high(held):
        if steps is None:
            return jnp.concatenate([held] + [swap(held, k) for k in range(1, count)])
        for step in reversed(steps):
            held = jnp.concatenate([held, swap(held, step)])
        return held

    def sector_cuts(order, acc, own, before, after, gathered):
        halos, cuts = {-1: before, 1: after}, [None] * sectors
        for s in order:
            blocks = [block for side in sides_of(s, sectors) for block in halos[side]]
            opening = s == order[0]
            cuts[s] = call(
                functools.partial(outer_kernel if opening else full_kernel, dims, s, gathered),
                cut_shapes,
                (sector_shifts,),
                (acc if opening else own, left, right, *blocks),
                scratch=[square, square_low],
                flops=terms * pair_flops // (3 if opening else 1),
            )
        return cuts

    with jax.named_scope("first"):
        parts = 2 if size % 256 == 0 else 1
        block = jax.ShapeDtypeStruct((1, size, size), jnp.bfloat16)
        rounded, first_block, last_block = call(
            round_kernel,
            [pltpu.VMEM(lanczos_vector.shape, jnp.bfloat16), block, block],
            (),
            (),
            (sector_sizes, lanczos_vector),
            [
                pltpu.VMEM(lanczos_vector.shape, jnp.float32),
                pltpu.SMEM((sectors,), jnp.int32),
                pltpu.SemaphoreType.DMA((sectors * parts + 1,)),
            ],
        )
        before = [lax.ppermute(last_block, "sector", up)]
        after = [lax.ppermute(first_block, "sector", down)]
        matrices = pltpu.VMEM(left_block.shape, jnp.bfloat16)
        acc, left, right, start = call(
            functools.partial(load_kernel, dims),
            [square, matrices, matrices, rows],
            (),
            (rounded,),
            (sector_shifts, sector_sizes, left_block, right_block, lanczos_vector),
            [
                pltpu.SMEM((terms,), jnp.int32),
                pltpu.SMEM((sectors,), jnp.int32),
                pltpu.SemaphoreType.DMA((2, sectors, terms)),
                pltpu.SemaphoreType.DMA((sectors,)),
                pltpu.SemaphoreType.DMA((2,)),
            ],
            terms * pair_flops,
        )
        order = list(range(sectors))
        cuts = sector_cuts(order, acc, rounded, before, after, False)
        totals = [low_sum(*c) for c in cuts]

    with jax.named_scope("gather"):
        shifted, plus, minus, pieces = [[None] * sectors for _ in range(4)]
        row = pltpu.VMEM((span, size), jnp.float32)
        parts = high_sums(totals, order)
        for s in order:
            held, shifted[s], plus[s], minus[s] = call(
                functools.partial(shift_kernel, dims, s, scale),
                [jax.ShapeDtypeStruct((span, size), jnp.bfloat16), row, row, row],
                (sector_sizes,),
                (start, left_energy, right_energy, *parts[s]),
            )
            mine = gather_high(held[None])
            theirs = lax.ppermute(mine, "term", pairs_low(ranks)) if low > 1 else mine
            pieces[s] = [mine, theirs]
        after = [lax.ppermute(piece, "sector", down) for piece in pieces[0]]
        before = [lax.ppermute(piece, "sector", up) for piece in pieces[-1]]

    with jax.named_scope("second"):
        order = order[::-1]
        blocks = [piece for both in pieces for piece in both]
        acc, own = call(
            functools.partial(inner_kernel, dims, order[0]),
            [square, pltpu.VMEM((sectors, size, size), jnp.bfloat16)],
            (sector_shifts,),
            (*blocks, left, right),
            flops=terms * pair_flops,
        )
        cuts = sector_cuts(order, acc, own, before, after, True)
        totals = [low_sum(*c) for c in cuts]

    with jax.named_scope("scalars"):
        (sums,) = call(
            functools.partial(sums_kernel, dims),
            [jax.ShapeDtypeStruct((8, size), jnp.float32)],
            (sector_sizes,),
            (lanczos_vector, after_all(own, *cuts[order[-1]])),
        )
        parts = high_sums(totals, order)
        sums = after_all(sums, *parts[order[0]])
        if groups & (groups - 1) == 0:
            reach = 1
            while reach < groups:
                sums += lax.ppermute(sums, "sector", [(i, i ^ reach) for i in range(groups)])
                reach *= 2
        else:
            sums = lax.psum(sums, "sector")
        out = jax.ShapeDtypeStruct((sectors, span, size), jnp.float32)
        flat = [part for s in range(sectors) for part in parts[s]]
        return call(
            functools.partial(finish_kernel, dims, cells, scale),
            [out, out],
            (sector_sizes,),
            (sums, start, *shifted, *plus, *minus, *flat),
        )


def solution(mesh):
    return jax.shard_map(
        on_device,
        mesh=mesh,
        in_specs=(
            P("sector", None, None),
            P("sector", "term", None, None),
            P("sector", "term", None, None),
            P("sector", None),
            P("sector", None),
            P("term"),
            P("sector"),
        ),
        out_specs=(P("sector", "term", None), P("sector", "term", None)),
        check_vma=False,
    )
```

```python
import functools
import jax
import jax.numpy as jnp
from jax import lax
from jax.experimental import pallas as pl
from jax.experimental.pallas import tpu as pltpu
from jax.sharding import PartitionSpec as P

epsilon = 1e-06
NT = (((1,), (1,)), ((), ()))
GUESS = 4.5


def other(hi, step, count):
    return hi ^ step if count & (count - 1) == 0 else (step - hi) % count


def traced_other(hi, step, count):
    return hi ^ step if count & (count - 1) == 0 else lax.rem(step - hi + count, count)


def pairs_low(size):
    return [(i, i ^ 1) for i in range(size)]


def pairs_high(size, low, step):
    count = size // low
    return [(i, other(i // low, step, count) * low + i % low) for i in range(size)]


def row_finder(count, low, span):
    rank = lax.axis_index("term")
    hi, lo = rank // low, lax.rem(rank, low)

    def row_of(step, far):
        digit = 1 - lo if far else lo
        return pl.multiple_of((traced_other(hi, step, count) * low + digit) * span, span)

    return row_of


def add_pair(acc, left, right, block):
    mixed = jnp.dot(left[...], block[...], preferred_element_type=jnp.float32)
    acc[...] += lax.dot_general(
        mixed.astype(jnp.bfloat16), right[...], NT, preferred_element_type=jnp.float32
    )


def add_inner(dims, s, shift_ref, acc, left, right, wb, before_term=lambda t: None):
    sectors, terms = dims[:2]
    for t in range(terms):
        before_term(t)
        partner = s + shift_ref[t]

        @pl.when((partner >= 0) & (partner < sectors))
        def _():
            add_pair(acc, left.at[s, t], right.at[s, t], wb.at[partner])


def place_rows(dims, wb, pieces):
    sectors, terms, size, count, low, span = dims
    row_of = row_finder(count, low, span)
    for far in range(low):
        for step in range(count):
            wb[pl.ds(row_of(step, far), span), :] = pieces[far][step]


def add_outer(dims, s, gathered, shift_ref, acc, left, right, blocks, wb):
    sectors, terms = dims[:2]
    here, groups = lax.axis_index("sector"), lax.axis_size("sector")
    for n, side in enumerate(sides_of(s, sectors)):
        if gathered:
            place_rows(dims, wb, [blocks[n].at[0], blocks[n].at[1]])
            held = wb
        else:
            held = blocks[n].at[0]
        there = here > 0 if side < 0 else here < groups - 1
        for t in range(terms):

            @pl.when((shift_ref[t] == side) & there)
            def _():
                add_pair(acc, left.at[s, t], right.at[s, t], held)


def cut(dims, acc, send_ref, keep_ref):
    sectors, terms, size, count, low, span = dims
    row_of = row_finder(count, low, span)
    for step in range(count):
        if low > 1:
            send_ref[step] = acc[pl.ds(row_of(step, 1), span), :].astype(jnp.bfloat16)
        keep_ref[step] = acc[pl.ds(row_of(step, 0), span), :]


def sides_of(s, sectors):
    return ([-1] if s == 0 else []) + ([1] if s == sectors - 1 else [])


def live_tile(shape, first_row, limit):
    row = first_row + lax.broadcasted_iota(jnp.int32, shape, 0)
    return (row < limit) & (lax.broadcasted_iota(jnp.int32, shape, 1) < limit)


def energy_rows(left_row, right_row, s, first, span):
    shape = (span, left_row.shape[1])
    row = first + lax.broadcasted_iota(jnp.int32, shape, 0)
    here = row == lax.broadcasted_iota(jnp.int32, shape, 1)
    left = jnp.sum(jnp.where(here, left_row[s : s + 1, :], 0.0), axis=1, keepdims=True)
    return left + right_row[s : s + 1, :]


def round_kernel(size_hbm, vector_hbm, rounded, first_block, last_block, vector, sizes, sems):
    sectors, size = vector.shape[:2]
    parts = sems.shape[0] // sectors
    rows = size // parts
    tile = min(64, rows)
    limits = pltpu.make_async_copy(size_hbm, sizes, sems.at[sectors * parts])
    limits.start()
    copies = [
        pltpu.make_async_copy(
            vector_hbm.at[s, pl.ds(n * rows, rows), :],
            vector.at[s, pl.ds(n * rows, rows), :],
            sems.at[s * parts + n],
        )
        for s in range(sectors)
        for n in range(parts)
    ]
    for copy in copies:
        copy.start()
    limits.wait()
    for s in range(sectors):
        for n in range(parts):
            copies[s * parts + n].wait()

            @pl.loop(0, rows // tile)
            def _(k):
                first = pl.multiple_of(n * rows + k * tile, tile)
                part = pl.ds(first, tile)
                live = live_tile((tile, size), first, sizes[s])
                value = jnp.where(live, vector[s, part, :], 0.0).astype(jnp.bfloat16)
                rounded[s, part, :] = value
                if s == 0:
                    first_block[0, part, :] = value
                if s == sectors - 1:
                    last_block[0, part, :] = value


def load_kernel(
    dims, wb, shift_hbm, size_hbm, left_hbm, right_hbm, vector_hbm,
    acc, left, right, start, shift_ref, size_ref, sems, row_sems, scalar_sems,
):
    sectors, terms, size, count, low, span = dims
    scalars = [
        pltpu.make_async_copy(shift_hbm, shift_ref, scalar_sems.at[0]),
        pltpu.make_async_copy(size_hbm, size_ref, scalar_sems.at[1]),
    ]
    for copy in scalars:
        copy.start()
    first = row_finder(count, low, span)(0, 0)
    rows = [
        pltpu.make_async_copy(vector_hbm.at[s, pl.ds(first, span), :], start.at[s], row_sems.at[s])
        for s in range(sectors)
    ]
    copies = {
        (s, t): [
            pltpu.make_async_copy(hbm.at[s, t], vmem.at[s, t], sems.at[k, s, t])
            for k, (hbm, vmem) in enumerate(((left_hbm, left), (right_hbm, right)))
        ]
        for s in range(sectors)
        for t in range(terms)
    }
    for pair in copies.values():
        for copy in pair:
            copy.start()
    for copy in rows:
        copy.start()
    acc[...] = jnp.zeros_like(acc)
    for copy in scalars:
        copy.wait()

    def arrived(t):
        for copy in copies[0, t]:
            copy.wait()

    add_inner(dims, 0, shift_ref, acc, left, right, wb, arrived)
    for s in range(sectors):
        rows[s].wait()
        live = live_tile((span, size), first, size_ref[s])
        start[s] = jnp.where(live, start[s], 0.0)
    for s in range(1, sectors):
        for t in range(terms):
            for copy in copies[s, t]:
                copy.wait()


def inner_kernel(dims, s, shift_ref, *refs):
    sectors = dims[0]
    blocks, (left, right, acc, wb) = refs[: 2 * sectors], refs[2 * sectors :]
    acc[...] = jnp.zeros_like(acc)
    for e in range(sectors):
        place_rows(dims, wb.at[e], blocks[2 * e : 2 * e + 2])
    add_inner(dims, s, shift_ref, acc, left, right, wb)


def sums_kernel(dims, size_ref, vector_ref, wb, sums):
    sectors, size = dims[0], dims[2]
    sums[...] = jnp.zeros_like(sums)
    tile = min(64, size)
    for s in range(sectors):

        @pl.loop(0, size // tile)
        def _(n):
            first = pl.multiple_of(n * tile, tile)
            rows = pl.ds(first, tile)
            live = live_tile((tile, size), first, size_ref[s])
            start = jnp.where(live, vector_ref[s, rows, :], 0.0)
            shifted = wb[s, rows, :].astype(jnp.float32)
            for k, term in enumerate((shifted * shifted, shifted * start, start * start)):
                sums[k : k + 1, :] += jnp.sum(term, 0, keepdims=True)


def outer_kernel(dims, s, gathered, shift_ref, acc_ref, left, right, *refs):
    blocks, (send_ref, keep_ref, acc, wb) = refs[:-4], refs[-4:]
    acc[...] = acc_ref[...]
    add_outer(dims, s, gathered, shift_ref, acc, left, right, blocks, wb)
    cut(dims, acc, send_ref, keep_ref)


def full_kernel(dims, s, gathered, shift_ref, own, left, right, *refs):
    blocks, (send_ref, keep_ref, acc, wb) = refs[:-4], refs[-4:]
    acc[...] = jnp.zeros_like(acc)
    add_inner(dims, s, shift_ref, acc, left, right, own)
    add_outer(dims, s, gathered, shift_ref, acc, left, right, blocks, wb)
    cut(dims, acc, send_ref, keep_ref)


def shift_kernel(dims, s, scale, size_ref, start, left_row, right_row, *refs):
    sectors, terms, size, count, low, span = dims
    parts, (held_ref, shifted_ref, plus_ref, minus_ref) = refs[:-4], refs[-4:]
    first = row_finder(count, low, span)(0, 0)
    total = parts[0][...]
    for part in parts[1:]:
        total += part[...].astype(jnp.float32)
    mixed = jnp.where(live_tile((span, size), first, size_ref[s]), scale * total, 0.0)
    energy = energy_rows(left_row, right_row, s, first, span)
    shifted = mixed + (energy - GUESS) * start[s]
    held_ref[...] = shifted.astype(jnp.bfloat16)
    shifted_ref[...] = shifted
    plus_ref[...] = energy * shifted
    minus_ref[...] = energy * start[s] + mixed


def finish_kernel(dims, cells, scale, size_ref, sums, start, *refs):
    sectors, terms, size, count, low, span = dims
    shifted, plus, minus = [refs[k * sectors : (k + 1) * sectors] for k in range(3)]
    parts, (next_ref, sigma_ref) = refs[3 * sectors : -2], refs[-2:]
    first = row_finder(count, low, span)(0, 0)
    shifted_sq, overlap, norm_sq = [
        jnp.sum(sums[k : k + 1, :], axis=1, keepdims=True) for k in range(3)
    ]
    correlation = overlap + GUESS * norm_sq
    ritz = (correlation / cells) / (norm_sq / cells + epsilon)
    delta = ritz - GUESS
    res_sq = shifted_sq - 2.0 * delta * overlap + delta * delta * norm_sq
    inverse = lax.rsqrt(res_sq / cells + epsilon)
    each = len(parts) // sectors
    for s in range(sectors):
        next_ref[s] = (shifted[s][...] - delta * start[s]) * inverse
        total = parts[s * each][...]
        for part in parts[s * each + 1 : (s + 1) * each]:
            total += part[...].astype(jnp.float32)
        mixed = jnp.where(live_tile((span, size), first, size_ref[s]), scale * total, 0.0)
        sigma_ref[s] = (plus[s][...] - delta * minus[s][...] + mixed) * inverse


SMEM = pl.BlockSpec(memory_space=pltpu.SMEM)
VMEM = pl.BlockSpec(memory_space=pltpu.VMEM)
HBM = pl.BlockSpec(memory_space=pltpu.HBM)
LIMIT = pltpu.CompilerParams(vmem_limit_bytes=24 * 2**20)


def call(kernel, out_shape, scalars, arrays, matrices=(), scratch=(), flops=2**20):
    matrices = [pltpu.with_memory_space_constraint(m, pltpu.HBM) for m in matrices]
    return pl.pallas_call(
        kernel,
        out_shape=out_shape,
        in_specs=[SMEM] * len(scalars) + [VMEM] * len(arrays) + [HBM] * len(matrices),
        out_specs=[VMEM] * len(out_shape),
        scratch_shapes=scratch,
        compiler_params=LIMIT,
        cost_estimate=pl.CostEstimate(flops=flops, bytes_accessed=flops // 256, transcendentals=0),
    )(*scalars, *arrays, *matrices)


def after_all(value, *others):
    return lax.optimization_barrier((value, *others))[0]


def on_device(
    lanczos_vector, left_block, right_block, left_energy, right_energy, sector_shifts, sector_sizes
):
    sectors, size = lanczos_vector.shape[:2]
    terms, ranks = left_block.shape[1], lax.axis_size("term")
    groups = lax.axis_size("sector")
    scale = float(terms * ranks) ** (-0.5)
    cells = float(sectors * groups * size * size)
    span = size // ranks
    low = 2 if ranks % 2 == 0 else 1
    count = ranks // low
    up = [(i, i + 1) for i in range(groups - 1)]
    down = [(j, i) for i, j in up]
    dims = (sectors, terms, size, count, low, span)
    pair_flops = 4 * size**3
    rows = pltpu.VMEM((sectors, span, size), jnp.float32)
    square = pltpu.VMEM((size, size), jnp.float32)
    square_low = pltpu.VMEM((size, size), jnp.bfloat16)
    cut_shapes = [jax.ShapeDtypeStruct((count, span, size), d) for d in (jnp.bfloat16, jnp.float32)]

    def low_sum(send, keep):
        if low == 1:
            return keep
        return keep + lax.ppermute(send, "term", pairs_low(ranks)).astype(jnp.float32)

    hops = range(count - 1, 0, -1)

    def high_parts(total):
        return [total[0]] + [
            lax.ppermute(total[k].astype(jnp.bfloat16), "term", pairs_high(ranks, low, k))
            for k in hops
        ]

    def gather_high(held):
        got = {k: lax.ppermute(held, "term", pairs_high(ranks, low, k)) for k in hops}
        return jnp.concatenate([held] + [got[k] for k in range(1, count)])

    def sector_cuts(order, acc, own, before, after, gathered):
        halos, cuts = {-1: before, 1: after}, [None] * sectors
        for s in order:
            blocks = [block for side in sides_of(s, sectors) for block in halos[side]]
            opening = s == order[0]
            cuts[s] = call(
                functools.partial(outer_kernel if opening else full_kernel, dims, s, gathered),
                cut_shapes,
                (sector_shifts,),
                (acc if opening else own, left, right, *blocks),
                scratch=[square, square_low],
                flops=terms * pair_flops // (3 if opening else 1),
            )
        return cuts

    with jax.named_scope("first"):
        parts = 2 if size % 256 == 0 else 1
        block = jax.ShapeDtypeStruct((1, size, size), jnp.bfloat16)
        rounded, first_block, last_block = call(
            round_kernel,
            [pltpu.VMEM(lanczos_vector.shape, jnp.bfloat16), block, block],
            (),
            (),
            (sector_sizes, lanczos_vector),
            [
                pltpu.VMEM(lanczos_vector.shape, jnp.float32),
                pltpu.SMEM((sectors,), jnp.int32),
                pltpu.SemaphoreType.DMA((sectors * parts + 1,)),
            ],
        )
        before = [lax.ppermute(last_block, "sector", up)]
        after = [lax.ppermute(first_block, "sector", down)]
        matrices = pltpu.VMEM(left_block.shape, jnp.bfloat16)
        acc, left, right, start = call(
            functools.partial(load_kernel, dims),
            [square, matrices, matrices, rows],
            (),
            (rounded,),
            (sector_shifts, sector_sizes, left_block, right_block, lanczos_vector),
            [
                pltpu.SMEM((terms,), jnp.int32),
                pltpu.SMEM((sectors,), jnp.int32),
                pltpu.SemaphoreType.DMA((2, sectors, terms)),
                pltpu.SemaphoreType.DMA((sectors,)),
                pltpu.SemaphoreType.DMA((2,)),
            ],
            terms * pair_flops,
        )
        order = list(range(sectors))
        cuts = sector_cuts(order, acc, rounded, before, after, False)
        totals = [low_sum(*c) for c in cuts]

    with jax.named_scope("gather"):
        shifted, plus, minus, pieces = [[None] * sectors for _ in range(4)]
        row = pltpu.VMEM((span, size), jnp.float32)
        for s in order:
            held, shifted[s], plus[s], minus[s] = call(
                functools.partial(shift_kernel, dims, s, scale),
                [jax.ShapeDtypeStruct((span, size), jnp.bfloat16), row, row, row],
                (sector_sizes,),
                (start, left_energy, right_energy, *high_parts(totals[s])),
            )
            mine = gather_high(held[None])
            theirs = lax.ppermute(mine, "term", pairs_low(ranks)) if low > 1 else mine
            pieces[s] = [mine, theirs]
            whole = jnp.stack(pieces[s])
            if s == 0:
                after = [lax.ppermute(whole, "sector", down)]
            if s == sectors - 1:
                before = [lax.ppermute(whole, "sector", up)]

    with jax.named_scope("second"):
        order = order[::-1]
        blocks = [piece for both in pieces for piece in both]
        acc, own = call(
            functools.partial(inner_kernel, dims, order[0]),
            [square, pltpu.VMEM((sectors, size, size), jnp.bfloat16)],
            (sector_shifts,),
            (*blocks, left, right),
            flops=terms * pair_flops,
        )
        cuts = sector_cuts(order, acc, own, before, after, True)
        totals = [low_sum(*c) for c in cuts]

    with jax.named_scope("scalars"):
        (sums,) = call(
            functools.partial(sums_kernel, dims),
            [jax.ShapeDtypeStruct((8, size), jnp.float32)],
            (sector_sizes,),
            (lanczos_vector, after_all(own, *cuts[order[-1]])),
        )
        parts = {s: high_parts(totals[s]) for s in order}
        sums = after_all(sums, totals[order[0]])
        if groups & (groups - 1) == 0:
            reach = 1
            while reach < groups:
                got = lax.ppermute(sums, "sector", [(i, i ^ reach) for i in range(groups)])
                sums = after_all(sums + got, *parts[order[0]])
                reach *= 2
        else:
            sums = lax.psum(sums, "sector")
        out = jax.ShapeDtypeStruct((sectors, span, size), jnp.float32)
        flat = [part for s in range(sectors) for part in parts[s]]
        return call(
            functools.partial(finish_kernel, dims, cells, scale),
            [out, out],
            (sector_sizes,),
            (sums, start, *shifted, *plus, *minus, *flat),
        )


def solution(mesh):
    return jax.shard_map(
        on_device,
        mesh=mesh,
        in_specs=(
            P("sector", None, None),
            P("sector", "term", None, None),
            P("sector", "term", None, None),
            P("sector", None),
            P("sector", None),
            P("term"),
            P("sector"),
        ),
        out_specs=(P("sector", "term", None), P("sector", "term", None)),
        check_vma=False,
    )
```

```python
import functools
import jax
import jax.numpy as jnp
from jax import lax
from jax.experimental import pallas as pl
from jax.experimental.pallas import tpu as pltpu
from jax.sharding import PartitionSpec as P

epsilon = 1e-06
NT = (((1,), (1,)), ((), ()))
GUESS = 4.5


def other(hi, step, count):
    return hi ^ step if count & (count - 1) == 0 else (step - hi) % count


def traced_other(hi, step, count):
    return hi ^ step if count & (count - 1) == 0 else lax.rem(step - hi + count, count)


def pairs_low(size):
    return [(i, i ^ 1) for i in range(size)]


def pairs_high(size, low, step):
    count = size // low
    return [(i, other(i // low, step, count) * low + i % low) for i in range(size)]


def row_finder(count, low, span):
    rank = lax.axis_index("term")
    hi, lo = rank // low, lax.rem(rank, low)

    def row_of(step, far):
        digit = 1 - lo if far else lo
        return pl.multiple_of((traced_other(hi, step, count) * low + digit) * span, span)

    return row_of


def add_pair(acc, left, right, block):
    mixed = jnp.dot(left[...], block[...], preferred_element_type=jnp.float32)
    acc[...] += lax.dot_general(
        mixed.astype(jnp.bfloat16), right[...], NT, preferred_element_type=jnp.float32
    )


def sector_at(turn, sectors):
    odd = lax.rem(lax.axis_index("sector"), 2)
    return odd * turn + (1 - odd) * (sectors - 1 - turn)


def halos_at(turn, sectors):
    return ([0] if turn == 0 else []) + ([1] if turn == sectors - 1 else [])


def halo_side(halo):
    here, groups = lax.axis_index("sector"), lax.axis_size("sector")
    side = (1 - 2 * lax.rem(here, 2)) * (1 - 2 * halo)
    return side, (here + side >= 0) & (here + side < groups)


def add_inner(dims, s, shift_ref, acc, left, right, wb, before_term=lambda t: None):
    sectors, terms = dims[:2]
    for t in range(terms):
        before_term(t)
        partner = s + shift_ref[t]

        @pl.when((partner >= 0) & (partner < sectors))
        def _():
            add_pair(acc, left.at[s, t], right.at[s, t], wb.at[partner])


def place_rows(dims, wb, pieces):
    sectors, terms, size, count, low, span = dims
    row_of = row_finder(count, low, span)
    for far in range(low):
        for step in range(count):
            wb[pl.ds(row_of(step, far), span), :] = pieces[far][step]


def add_outer(dims, turn, gathered, shift_ref, acc, left, right, blocks, wb):
    sectors, terms = dims[:2]
    s = sector_at(turn, sectors)
    for block, halo in zip(blocks, halos_at(turn, sectors)):
        if gathered:
            place_rows(dims, wb, [block.at[0], block.at[1]])
            held = wb
        else:
            held = block.at[0]
        side, there = halo_side(halo)
        for t in range(terms):

            @pl.when((shift_ref[t] == side) & there)
            def _():
                add_pair(acc, left.at[s, t], right.at[s, t], held)


def cut(dims, acc, send_ref, keep_ref):
    sectors, terms, size, count, low, span = dims
    row_of = row_finder(count, low, span)
    for step in range(count):
        if low > 1:
            send_ref[step] = acc[pl.ds(row_of(step, 1), span), :].astype(jnp.bfloat16)
        keep_ref[step] = acc[pl.ds(row_of(step, 0), span), :]


def live_tile(shape, first_row, limit):
    row = first_row + lax.broadcasted_iota(jnp.int32, shape, 0)
    return (row < limit) & (lax.broadcasted_iota(jnp.int32, shape, 1) < limit)


def energy_rows(left_row, right_row, s, first, span):
    shape = (span, left_row.shape[1])
    row = first + lax.broadcasted_iota(jnp.int32, shape, 0)
    here = row == lax.broadcasted_iota(jnp.int32, shape, 1)
    left = jnp.sum(jnp.where(here, left_row[pl.ds(s, 1), :], 0.0), axis=1, keepdims=True)
    return left + right_row[pl.ds(s, 1), :]


def round_kernel(size_hbm, vector_hbm, rounded, edge, other_edge, vector, sizes, sems):
    sectors, size = vector.shape[:2]
    parts = sems.shape[0] // sectors
    rows = size // parts
    tile = min(64, rows)
    limits = pltpu.make_async_copy(size_hbm, sizes, sems.at[sectors * parts])
    limits.start()
    copies = [
        pltpu.make_async_copy(
            vector_hbm.at[sector_at(turn, sectors), pl.ds(n * rows, rows), :],
            vector.at[turn, pl.ds(n * rows, rows), :],
            sems.at[turn * parts + n],
        )
        for turn in range(sectors)
        for n in range(parts)
    ]
    for copy in copies:
        copy.start()
    limits.wait()
    for turn in range(sectors):
        s = sector_at(turn, sectors)
        for n in range(parts):
            copies[turn * parts + n].wait()

            @pl.loop(0, rows // tile)
            def _(k):
                first = pl.multiple_of(n * rows + k * tile, tile)
                part = pl.ds(first, tile)
                live = live_tile((tile, size), first, sizes[s])
                value = jnp.where(live, vector[turn, part, :], 0.0).astype(jnp.bfloat16)
                rounded[s, part, :] = value
                if turn == 0:
                    edge[0, part, :] = value
                if turn == sectors - 1:
                    other_edge[0, part, :] = value


def load_kernel(
    dims, wb, shift_hbm, size_hbm, left_hbm, right_hbm, vector_hbm,
    acc, left, right, start, shift_ref, size_ref, sems, row_sems, scalar_sems,
):
    sectors, terms, size, count, low, span = dims
    scalars = [
        pltpu.make_async_copy(shift_hbm, shift_ref, scalar_sems.at[0]),
        pltpu.make_async_copy(size_hbm, size_ref, scalar_sems.at[1]),
    ]
    for copy in scalars:
        copy.start()
    first = row_finder(count, low, span)(0, 0)
    rows = [
        pltpu.make_async_copy(vector_hbm.at[s, pl.ds(first, span), :], start.at[s], row_sems.at[s])
        for s in range(sectors)
    ]
    copies = {
        (turn, t): [
            pltpu.make_async_copy(
                hbm.at[sector_at(turn, sectors), t],
                vmem.at[sector_at(turn, sectors), t],
                sems.at[k, turn, t],
            )
            for k, (hbm, vmem) in enumerate(((left_hbm, left), (right_hbm, right)))
        ]
        for turn in range(sectors)
        for t in range(terms)
    }
    for pair in copies.values():
        for copy in pair:
            copy.start()
    for copy in rows:
        copy.start()
    acc[...] = jnp.zeros_like(acc)
    for copy in scalars:
        copy.wait()

    def arrived(t):
        for copy in copies[0, t]:
            copy.wait()

    add_inner(dims, sector_at(0, sectors), shift_ref, acc, left, right, wb, arrived)
    for s in range(sectors):
        rows[s].wait()
        live = live_tile((span, size), first, size_ref[s])
        start[s] = jnp.where(live, start[s], 0.0)
    for turn in range(1, sectors):
        for t in range(terms):
            for copy in copies[turn, t]:
                copy.wait()


def outer_kernel(dims, gathered, shift_ref, acc_ref, left, right, *refs):
    blocks, (send_ref, keep_ref, acc, wb) = refs[:-4], refs[-4:]
    acc[...] = acc_ref[...]
    add_outer(dims, 0, gathered, shift_ref, acc, left, right, blocks, wb)
    cut(dims, acc, send_ref, keep_ref)


def inner_kernel(dims, shift_ref, left, right, *refs):
    sectors = dims[0]
    pieces, (acc, own) = refs[:-2], refs[-2:]
    acc[...] = jnp.zeros_like(acc)
    for turn in range(sectors):
        place_rows(dims, own.at[sector_at(turn, sectors)], pieces[2 * turn : 2 * turn + 2])
    add_inner(dims, sector_at(0, sectors), shift_ref, acc, left, right, own)


def full_kernel(dims, turn, gathered, shift_ref, own, left, right, *refs):
    blocks, (send_ref, keep_ref, acc, wb) = refs[:-4], refs[-4:]
    acc[...] = jnp.zeros_like(acc)
    add_inner(dims, sector_at(turn, dims[0]), shift_ref, acc, left, right, own)
    add_outer(dims, turn, gathered, shift_ref, acc, left, right, blocks, wb)
    cut(dims, acc, send_ref, keep_ref)


def sums_kernel(dims, size_ref, vector_ref, wb, sums):
    sectors, size = dims[0], dims[2]
    sums[...] = jnp.zeros_like(sums)
    tile = min(64, size)
    for s in range(sectors):

        @pl.loop(0, size // tile)
        def _(n):
            first = pl.multiple_of(n * tile, tile)
            rows = pl.ds(first, tile)
            live = live_tile((tile, size), first, size_ref[s])
            start = jnp.where(live, vector_ref[s, rows, :], 0.0)
            shifted = wb[s, rows, :].astype(jnp.float32)
            for k, term in enumerate((shifted * shifted, shifted * start, start * start)):
                sums[k : k + 1, :] += jnp.sum(term, 0, keepdims=True)


def shift_kernel(dims, turn, scale, size_ref, start, left_row, right_row, *refs):
    sectors, terms, size, count, low, span = dims
    parts, (held_ref, shifted_ref, plus_ref, minus_ref) = refs[:-4], refs[-4:]
    s = sector_at(turn, sectors)
    first = row_finder(count, low, span)(0, 0)
    total = parts[0][...]
    for part in parts[1:]:
        total += part[...].astype(jnp.float32)
    mixed = jnp.where(live_tile((span, size), first, size_ref[s]), scale * total, 0.0)
    energy = energy_rows(left_row, right_row, s, first, span)
    begin = start[s]
    shifted = mixed + (energy - GUESS) * begin
    held_ref[...] = shifted.astype(jnp.bfloat16)
    shifted_ref[...] = shifted
    plus_ref[...] = energy * shifted
    minus_ref[...] = energy * begin + mixed


def finish_kernel(dims, cells, scale, size_ref, start, *refs):
    sectors, terms, size, count, low, span = dims
    shifted, plus, minus = [refs[k * sectors : (k + 1) * sectors] for k in range(3)]
    parts, refs = refs[3 * sectors : 3 * sectors + count * sectors], refs[3 * sectors + count * sectors :]
    tables, (next_ref, sigma_ref) = refs[:-2], refs[-2:]
    first = row_finder(count, low, span)(0, 0)
    sums = sum(table[...] for table in tables)
    shifted_sq, overlap, norm_sq = [
        jnp.sum(sums[k : k + 1, :], axis=1, keepdims=True) for k in range(3)
    ]
    correlation = overlap + GUESS * norm_sq
    ritz = (correlation / cells) / (norm_sq / cells + epsilon)
    delta = ritz - GUESS
    res_sq = shifted_sq - 2.0 * delta * overlap + delta * delta * norm_sq
    inverse = lax.rsqrt(res_sq / cells + epsilon)
    for turn in range(sectors):
        s = sector_at(turn, sectors)
        next_ref[s] = (shifted[turn][...] - delta * start[s]) * inverse
        total = parts[turn * count][...]
        for part in parts[turn * count + 1 : (turn + 1) * count]:
            total += part[...].astype(jnp.float32)
        mixed = jnp.where(live_tile((span, size), first, size_ref[s]), scale * total, 0.0)
        sigma_ref[s] = (plus[turn][...] - delta * minus[turn][...] + mixed) * inverse


SMEM = pl.BlockSpec(memory_space=pltpu.SMEM)
VMEM = pl.BlockSpec(memory_space=pltpu.VMEM)
HBM = pl.BlockSpec(memory_space=pltpu.HBM)
LIMIT = pltpu.CompilerParams(vmem_limit_bytes=24 * 2**20)


def call(kernel, out_shape, scalars, arrays, matrices=(), scratch=(), flops=2**20):
    matrices = [pltpu.with_memory_space_constraint(m, pltpu.HBM) for m in matrices]
    return pl.pallas_call(
        kernel,
        out_shape=out_shape,
        in_specs=[SMEM] * len(scalars) + [VMEM] * len(arrays) + [HBM] * len(matrices),
        out_specs=[VMEM] * len(out_shape),
        scratch_shapes=scratch,
        compiler_params=LIMIT,
        cost_estimate=pl.CostEstimate(flops=flops, bytes_accessed=flops // 256, transcendentals=0),
    )(*scalars, *arrays, *matrices)


def after_all(value, *others):
    return lax.optimization_barrier((value, *others))[0]


def on_device(
    lanczos_vector, left_block, right_block, left_energy, right_energy, sector_shifts, sector_sizes
):
    sectors, size = lanczos_vector.shape[:2]
    terms, ranks = left_block.shape[1], lax.axis_size("term")
    groups = lax.axis_size("sector")
    scale = float(terms * ranks) ** (-0.5)
    cells = float(sectors * groups * size * size)
    span = size // ranks
    low = 2 if ranks % 2 == 0 else 1
    count = ranks // low
    dims = (sectors, terms, size, count, low, span)
    turns = range(sectors)
    pair_flops = 4 * size**3
    rows = pltpu.VMEM((sectors, span, size), jnp.float32)
    square = pltpu.VMEM((size, size), jnp.float32)
    square_low = pltpu.VMEM((size, size), jnp.bfloat16)
    cut_shapes = [jax.ShapeDtypeStruct((count, span, size), d) for d in (jnp.bfloat16, jnp.float32)]
    pairs = [
        [p for i in range(start, groups - 1, 2) for p in ((i, i + 1), (i + 1, i))]
        for start in range(2)
    ]

    def halo(edge, which):
        return lax.ppermute(edge, "sector", pairs[which]) if pairs[which] else edge

    def low_sum(send, keep):
        if low == 1:
            return keep
        return keep + lax.ppermute(send, "term", pairs_low(ranks)).astype(jnp.float32)

    hops = range(count - 1, 0, -1)

    def high_parts(total):
        return [total[0]] + [
            lax.ppermute(total[k].astype(jnp.bfloat16), "term", pairs_high(ranks, low, k))
            for k in hops
        ]

    def gather_high(held):
        got = {k: lax.ppermute(held, "term", pairs_high(ranks, low, k)) for k in hops}
        return jnp.concatenate([held] + [got[k] for k in range(1, count)])

    def sector_cuts(acc, own, halos, gathered):
        return [
            call(
                functools.partial(outer_kernel, dims, gathered)
                if turn == 0
                else functools.partial(full_kernel, dims, turn, gathered),
                cut_shapes,
                (sector_shifts,),
                (own if turn else acc, left, right, *[halos[h] for h in halos_at(turn, sectors)]),
                scratch=[square, square_low],
                flops=terms * pair_flops // (1 if turn else 3),
            )
            for turn in turns
        ]

    with jax.named_scope("first"):
        parts = 2 if size % 256 == 0 else 1
        block = jax.ShapeDtypeStruct((1, size, size), jnp.bfloat16)
        rounded, *edges = call(
            round_kernel,
            [pltpu.VMEM(lanczos_vector.shape, jnp.bfloat16), block, block],
            (),
            (),
            (sector_sizes, lanczos_vector),
            [
                pltpu.VMEM(lanczos_vector.shape, jnp.float32),
                pltpu.SMEM((sectors,), jnp.int32),
                pltpu.SemaphoreType.DMA((sectors * parts + 1,)),
            ],
        )
        halos = [halo(edge, which) for which, edge in enumerate(edges)]
        matrices = pltpu.VMEM(left_block.shape, jnp.bfloat16)
        acc, left, right, start = call(
            functools.partial(load_kernel, dims),
            [square, matrices, matrices, rows],
            (),
            (rounded,),
            (sector_shifts, sector_sizes, left_block, right_block, lanczos_vector),
            [
                pltpu.SMEM((terms,), jnp.int32),
                pltpu.SMEM((sectors,), jnp.int32),
                pltpu.SemaphoreType.DMA((2, sectors, terms)),
                pltpu.SemaphoreType.DMA((sectors,)),
                pltpu.SemaphoreType.DMA((2,)),
            ],
            terms * pair_flops,
        )
        cuts = sector_cuts(acc, rounded, halos, False)
        totals = [low_sum(*c) for c in cuts]

    with jax.named_scope("gather"):
        shifted, plus, minus, pieces = [[None] * sectors for _ in range(4)]
        row = pltpu.VMEM((span, size), jnp.float32)
        parts = [high_parts(total) for total in totals]
        for turn in turns:
            held, shifted[turn], plus[turn], minus[turn] = call(
                functools.partial(shift_kernel, dims, turn, scale),
                [jax.ShapeDtypeStruct((span, size), jnp.bfloat16), row, row, row],
                (sector_sizes,),
                (start, left_energy, right_energy, *parts[turn]),
            )
            mine = gather_high(held[None])
            theirs = lax.ppermute(mine, "term", pairs_low(ranks)) if low > 1 else mine
            pieces[turn] = [mine, theirs]
        edges = [jnp.stack(pieces[0]), jnp.stack(pieces[-1])]
        edges[0] = after_all(edges[0], pieces[-1][1])
        halos = [halo(edge, which) for which, edge in enumerate(edges)]

    with jax.named_scope("second"):
        acc, own = call(
            functools.partial(inner_kernel, dims),
            [square, pltpu.VMEM((sectors, size, size), jnp.bfloat16)],
            (sector_shifts,),
            (left, right, *[piece for both in pieces for piece in both]),
            flops=terms * pair_flops,
        )
        cuts = sector_cuts(acc, own, halos, True)
        totals = [low_sum(*c) for c in cuts]

    with jax.named_scope("scalars"):
        (sums,) = call(
            functools.partial(sums_kernel, dims),
            [jax.ShapeDtypeStruct((8, size), jnp.float32)],
            (sector_sizes,),
            (lanczos_vector, after_all(own, *cuts[-1])),
        )
        parts = [high_parts(total) for total in totals]
        sums = after_all(sums, totals[-1], *parts[0])
        tables, reach = [sums], 1
        while reach < groups:
            if groups & (groups - 1):
                tables, reach = [lax.psum(sums, "sector")], groups
            else:
                sums, width = sum(tables), min(4, groups // reach)
                tables = [sums] + [
                    lax.ppermute(sums, "sector", [(i, i ^ (reach * k)) for i in range(groups)])
                    for k in range(1, width)
                ]
                reach *= width
        out = jax.ShapeDtypeStruct((sectors, span, size), jnp.float32)
        flat = [part for each in parts for part in each]
        return call(
            functools.partial(finish_kernel, dims, cells, scale),
            [out, out],
            (sector_sizes,),
            (start, *shifted, *plus, *minus, *flat, *tables),
        )


def solution(mesh):
    return jax.shard_map(
        on_device,
        mesh=mesh,
        in_specs=(
            P("sector", None, None),
            P("sector", "term", None, None),
            P("sector", "term", None, None),
            P("sector", None),
            P("sector", None),
            P("term"),
            P("sector"),
        ),
        out_specs=(P("sector", "term", None), P("sector", "term", None)),
        check_vma=False,
    )
```

```python
import functools
import jax
import jax.numpy as jnp
from jax import lax
from jax.experimental import pallas as pl
from jax.experimental.pallas import tpu as pltpu
from jax.sharding import PartitionSpec as P

epsilon = 1e-06
NT = (((1,), (1,)), ((), ()))
GUESS = 4.5


def other(hi, step, count):
    return hi ^ step if count & (count - 1) == 0 else (step - hi) % count


def traced_other(hi, step, count):
    return hi ^ step if count & (count - 1) == 0 else lax.rem(step - hi + count, count)


def pairs_low(size):
    return [(i, i ^ 1) for i in range(size)]


def pairs_high(size, low, step):
    count = size // low
    return [(i, other(i // low, step, count) * low + i % low) for i in range(size)]


def row_finder(count, low, span):
    rank = lax.axis_index("term")
    hi, lo = rank // low, lax.rem(rank, low)

    def row_of(step, far):
        digit = 1 - lo if far else lo
        return pl.multiple_of((traced_other(hi, step, count) * low + digit) * span, span)

    return row_of


def add_pair(acc, left, right, block):
    mixed = jnp.dot(left[...], block[...], preferred_element_type=jnp.float32)
    acc[...] += lax.dot_general(
        mixed.astype(jnp.bfloat16), right[...], NT, preferred_element_type=jnp.float32
    )


def sector_at(turn, sectors):
    odd = lax.rem(lax.axis_index("sector"), 2)
    return odd * turn + (1 - odd) * (sectors - 1 - turn)


def halos_at(turn, sectors):
    return ([0] if turn == 0 else []) + ([1] if turn == sectors - 1 else [])


def halo_side(halo):
    here, groups = lax.axis_index("sector"), lax.axis_size("sector")
    side = (1 - 2 * lax.rem(here, 2)) * (1 - 2 * halo)
    return side, (here + side >= 0) & (here + side < groups)


def add_inner(dims, s, shift_ref, acc, left, right, wb, before_term=lambda t: None):
    sectors, terms = dims[:2]
    for t in range(terms):
        before_term(t)
        partner = s + shift_ref[t]

        @pl.when((partner >= 0) & (partner < sectors))
        def _():
            add_pair(acc, left.at[s, t], right.at[s, t], wb.at[partner])


def place_rows(dims, wb, pieces):
    sectors, terms, size, count, low, span = dims
    row_of = row_finder(count, low, span)
    for far in range(low):
        for step in range(count):
            wb[pl.ds(row_of(step, far), span), :] = pieces[far][step]


def add_outer(dims, turn, gathered, shift_ref, acc, left, right, blocks, wb):
    sectors, terms = dims[:2]
    s = sector_at(turn, sectors)
    for block, halo in zip(blocks, halos_at(turn, sectors)):
        if gathered:
            place_rows(dims, wb, [block.at[0], block.at[1]])
            held = wb
        else:
            held = block
        side, there = halo_side(halo)
        for t in range(terms):

            @pl.when((shift_ref[t] == side) & there)
            def _():
                add_pair(acc, left.at[s, t], right.at[s, t], held)


def cut(dims, acc, send_ref, keep_ref):
    sectors, terms, size, count, low, span = dims
    row_of = row_finder(count, low, span)
    for step in range(count):
        if low > 1:
            send_ref[step] = acc[pl.ds(row_of(step, 1), span), :].astype(jnp.bfloat16)
        keep_ref[step] = acc[pl.ds(row_of(step, 0), span), :]


def live_tile(shape, first_row, limit):
    row = first_row + lax.broadcasted_iota(jnp.int32, shape, 0)
    return (row < limit) & (lax.broadcasted_iota(jnp.int32, shape, 1) < limit)


def energy_rows(left_row, right_row, s, first, span):
    shape = (span, left_row.shape[1])
    row = first + lax.broadcasted_iota(jnp.int32, shape, 0)
    here = row == lax.broadcasted_iota(jnp.int32, shape, 1)
    left = jnp.sum(jnp.where(here, left_row[pl.ds(s, 1), :], 0.0), axis=1, keepdims=True)
    return left + right_row[pl.ds(s, 1), :]


def round_kernel(size_hbm, vector_hbm, rounded, edge, other_edge, vector, sizes, sems):
    sectors, size = vector.shape[:2]
    parts = sems.shape[0] // sectors
    rows = size // parts
    tile = min(64, rows)
    limits = pltpu.make_async_copy(size_hbm, sizes, sems.at[sectors * parts])
    limits.start()
    copies = [
        pltpu.make_async_copy(
            vector_hbm.at[sector_at(turn, sectors), pl.ds(n * rows, rows), :],
            vector.at[turn, pl.ds(n * rows, rows), :],
            sems.at[turn * parts + n],
        )
        for turn in range(sectors)
        for n in range(parts)
    ]
    for copy in copies:
        copy.start()
    limits.wait()
    for turn in range(sectors):
        s = sector_at(turn, sectors)
        for n in range(parts):
            copies[turn * parts + n].wait()

            @pl.loop(0, rows // tile)
            def _(k):
                first = pl.multiple_of(n * rows + k * tile, tile)
                part = pl.ds(first, tile)
                live = live_tile((tile, size), first, sizes[s])
                value = jnp.where(live, vector[turn, part, :], 0.0).astype(jnp.bfloat16)
                rounded[s, part, :] = value
                if turn == 0:
                    edge[part, :] = value
                if turn == sectors - 1:
                    other_edge[part, :] = value


def load_kernel(
    dims, wb, shift_hbm, size_hbm, left_hbm, right_hbm, vector_hbm,
    acc, left, right, start, shift_ref, size_ref, sems, row_sems, scalar_sems,
):
    sectors, terms, size, count, low, span = dims
    scalars = [
        pltpu.make_async_copy(shift_hbm, shift_ref, scalar_sems.at[0]),
        pltpu.make_async_copy(size_hbm, size_ref, scalar_sems.at[1]),
    ]
    for copy in scalars:
        copy.start()
    first = row_finder(count, low, span)(0, 0)
    rows = [
        pltpu.make_async_copy(vector_hbm.at[s, pl.ds(first, span), :], start.at[s], row_sems.at[s])
        for s in range(sectors)
    ]
    copies = {
        (turn, t): [
            pltpu.make_async_copy(
                hbm.at[sector_at(turn, sectors), t],
                vmem.at[sector_at(turn, sectors), t],
                sems.at[k, turn, t],
            )
            for k, (hbm, vmem) in enumerate(((left_hbm, left), (right_hbm, right)))
        ]
        for turn in range(sectors)
        for t in range(terms)
    }
    for pair in copies.values():
        for copy in pair:
            copy.start()
    for copy in rows:
        copy.start()
    acc[...] = jnp.zeros_like(acc)
    for copy in scalars:
        copy.wait()

    def arrived(t):
        for copy in copies[0, t]:
            copy.wait()

    add_inner(dims, sector_at(0, sectors), shift_ref, acc, left, right, wb, arrived)
    for s in range(sectors):
        rows[s].wait()
        live = live_tile((span, size), first, size_ref[s])
        start[s] = jnp.where(live, start[s], 0.0)
    for turn in range(1, sectors):
        for t in range(terms):
            for copy in copies[turn, t]:
                copy.wait()


def outer_kernel(dims, gathered, shift_ref, acc_ref, left, right, *refs):
    blocks, (send_ref, keep_ref, acc, wb) = refs[:-4], refs[-4:]
    acc[...] = acc_ref[...]
    add_outer(dims, 0, gathered, shift_ref, acc, left, right, blocks, wb)
    cut(dims, acc, send_ref, keep_ref)


def self_kernel(dims, shift_ref, left, right, mine, theirs, acc, own):
    s = sector_at(0, dims[0])
    acc[...] = jnp.zeros_like(acc)
    place_rows(dims, own, [mine, theirs])
    for t in range(dims[1]):

        @pl.when(shift_ref[t] == 0)
        def _():
            add_pair(acc, left.at[s, t], right.at[s, t], own)


def inner_kernel(dims, shift_ref, acc_ref, first_block, left, right, *refs):
    sectors, terms = dims[:2]
    pieces, (acc, own) = refs[:-2], refs[-2:]
    acc[...] = acc_ref[...]
    s = sector_at(0, sectors)
    own[s] = first_block[...]
    for turn in range(1, sectors):
        place_rows(dims, own.at[sector_at(turn, sectors)], pieces[2 * turn - 2 : 2 * turn])
    for t in range(terms):
        partner = s + shift_ref[t]

        @pl.when((shift_ref[t] != 0) & (partner >= 0) & (partner < sectors))
        def _():
            add_pair(acc, left.at[s, t], right.at[s, t], own.at[partner])


def full_kernel(dims, turn, gathered, shift_ref, own, left, right, *refs):
    blocks, (send_ref, keep_ref, acc, wb) = refs[:-4], refs[-4:]
    acc[...] = jnp.zeros_like(acc)
    add_inner(dims, sector_at(turn, dims[0]), shift_ref, acc, left, right, own)
    add_outer(dims, turn, gathered, shift_ref, acc, left, right, blocks, wb)
    cut(dims, acc, send_ref, keep_ref)


def sums_kernel(dims, size_ref, vector_ref, wb, sums):
    sectors, size = dims[0], dims[2]
    sums[...] = jnp.zeros_like(sums)
    tile = min(64, size)
    for s in range(sectors):

        @pl.loop(0, size // tile)
        def _(n):
            first = pl.multiple_of(n * tile, tile)
            rows = pl.ds(first, tile)
            live = live_tile((tile, size), first, size_ref[s])
            start = jnp.where(live, vector_ref[s, rows, :], 0.0)
            shifted = wb[s, rows, :].astype(jnp.float32)
            for k, term in enumerate((shifted * shifted, shifted * start, start * start)):
                sums[k : k + 1, :] += jnp.sum(term, 0, keepdims=True)


def shift_kernel(dims, turn, scale, size_ref, start, left_row, right_row, *refs):
    sectors, terms, size, count, low, span = dims
    parts, (held_ref, shifted_ref, plus_ref, minus_ref) = refs[:-4], refs[-4:]
    s = sector_at(turn, sectors)
    first = row_finder(count, low, span)(0, 0)
    total = parts[0][...]
    for part in parts[1:]:
        total += part[...].astype(jnp.float32)
    mixed = jnp.where(live_tile((span, size), first, size_ref[s]), scale * total, 0.0)
    energy = energy_rows(left_row, right_row, s, first, span)
    begin = start[s]
    shifted = mixed + (energy - GUESS) * begin
    held_ref[...] = shifted.astype(jnp.bfloat16)
    shifted_ref[...] = shifted
    plus_ref[...] = energy * shifted
    minus_ref[...] = energy * begin + mixed


def finish_kernel(dims, cells, scale, size_ref, start, *refs):
    sectors, terms, size, count, low, span = dims
    shifted, plus, minus = [refs[k * sectors : (k + 1) * sectors] for k in range(3)]
    parts, refs = refs[3 * sectors : 3 * sectors + count * sectors], refs[3 * sectors + count * sectors :]
    tables, (next_ref, sigma_ref) = refs[:-2], refs[-2:]
    first = row_finder(count, low, span)(0, 0)
    sums = sum(table[...] for table in tables)
    shifted_sq, overlap, norm_sq = [
        jnp.sum(sums[k : k + 1, :], axis=1, keepdims=True) for k in range(3)
    ]
    correlation = overlap + GUESS * norm_sq
    ritz = (correlation / cells) / (norm_sq / cells + epsilon)
    delta = ritz - GUESS
    res_sq = shifted_sq - 2.0 * delta * overlap + delta * delta * norm_sq
    inverse = lax.rsqrt(res_sq / cells + epsilon)
    for turn in range(sectors):
        s = sector_at(turn, sectors)
        next_ref[s] = (shifted[turn][...] - delta * start[s]) * inverse
        total = parts[turn * count][...]
        for part in parts[turn * count + 1 : (turn + 1) * count]:
            total += part[...].astype(jnp.float32)
        mixed = jnp.where(live_tile((span, size), first, size_ref[s]), scale * total, 0.0)
        sigma_ref[s] = (plus[turn][...] - delta * minus[turn][...] + mixed) * inverse


SMEM = pl.BlockSpec(memory_space=pltpu.SMEM)
VMEM = pl.BlockSpec(memory_space=pltpu.VMEM)
HBM = pl.BlockSpec(memory_space=pltpu.HBM)
LIMIT = pltpu.CompilerParams(vmem_limit_bytes=24 * 2**20)


def call(kernel, out_shape, scalars, arrays, matrices=(), scratch=(), flops=2**20):
    matrices = [pltpu.with_memory_space_constraint(m, pltpu.HBM) for m in matrices]
    return pl.pallas_call(
        kernel,
        out_shape=out_shape,
        in_specs=[SMEM] * len(scalars) + [VMEM] * len(arrays) + [HBM] * len(matrices),
        out_specs=[VMEM] * len(out_shape),
        scratch_shapes=scratch,
        compiler_params=LIMIT,
        cost_estimate=pl.CostEstimate(flops=flops, bytes_accessed=flops // 256, transcendentals=0),
    )(*scalars, *arrays, *matrices)


def after_all(value, *others):
    return lax.optimization_barrier((value, *others))[0]


def on_device(
    lanczos_vector, left_block, right_block, left_energy, right_energy, sector_shifts, sector_sizes
):
    sectors, size = lanczos_vector.shape[:2]
    terms, ranks = left_block.shape[1], lax.axis_size("term")
    groups = lax.axis_size("sector")
    scale = float(terms * ranks) ** (-0.5)
    cells = float(sectors * groups * size * size)
    span = size // ranks
    low = 2 if ranks % 2 == 0 else 1
    count = ranks // low
    dims = (sectors, terms, size, count, low, span)
    turns = range(sectors)
    pair_flops = 4 * size**3
    rows = pltpu.VMEM((sectors, span, size), jnp.float32)
    square = pltpu.VMEM((size, size), jnp.float32)
    square_low = pltpu.VMEM((size, size), jnp.bfloat16)
    cut_shapes = [jax.ShapeDtypeStruct((count, span, size), d) for d in (jnp.bfloat16, jnp.float32)]
    pairs = [
        [p for i in range(start, groups - 1, 2) for p in ((i, i + 1), (i + 1, i))]
        for start in range(2)
    ]

    def halo(edge, which):
        return lax.ppermute(edge, "sector", pairs[which]) if pairs[which] else edge

    def low_sum(send, keep):
        if low == 1:
            return keep
        return keep + lax.ppermute(send, "term", pairs_low(ranks)).astype(jnp.float32)

    hops = range(count - 1, 0, -1)

    def high_parts(total):
        return [total[0]] + [
            lax.ppermute(total[k].astype(jnp.bfloat16), "term", pairs_high(ranks, low, k))
            for k in hops
        ]

    def gather_high(held, following):
        got = {
            k: lax.ppermute(
                after_all(held, following) if k == 1 else held, "term", pairs_high(ranks, low, k)
            )
            for k in hops
        }
        return jnp.concatenate([held] + [got[k] for k in range(1, count)])

    def first_cut(acc, halos, gathered):
        return call(
            functools.partial(outer_kernel, dims, gathered),
            cut_shapes,
            (sector_shifts,),
            (acc, left, right, *[halos[h] for h in halos_at(0, sectors)]),
            scratch=[square, square_low],
            flops=terms * pair_flops // 3,
        )

    def later_cut(turn, own, halos, gathered):
        return call(
            functools.partial(full_kernel, dims, turn, gathered),
            cut_shapes,
            (sector_shifts,),
            (own, left, right, *[halos[h] for h in halos_at(turn, sectors)]),
            scratch=[square, square_low],
            flops=terms * pair_flops,
        )

    with jax.named_scope("first"):
        parts = 2 if size % 256 == 0 else 1
        block = jax.ShapeDtypeStruct((size, size), jnp.bfloat16)
        rounded, *edges = call(
            round_kernel,
            [pltpu.VMEM(lanczos_vector.shape, jnp.bfloat16), block, block],
            (),
            (),
            (sector_sizes, lanczos_vector),
            [
                pltpu.VMEM(lanczos_vector.shape, jnp.float32),
                pltpu.SMEM((sectors,), jnp.int32),
                pltpu.SemaphoreType.DMA((sectors * parts + 1,)),
            ],
        )
        halos = [halo(edge, which) for which, edge in enumerate(edges)]
        matrices = pltpu.VMEM(left_block.shape, jnp.bfloat16)
        acc, left, right, start = call(
            functools.partial(load_kernel, dims),
            [square, matrices, matrices, rows],
            (),
            (rounded,),
            (sector_shifts, sector_sizes, left_block, right_block, lanczos_vector),
            [
                pltpu.SMEM((terms,), jnp.int32),
                pltpu.SMEM((sectors,), jnp.int32),
                pltpu.SemaphoreType.DMA((2, sectors, terms)),
                pltpu.SemaphoreType.DMA((sectors,)),
                pltpu.SemaphoreType.DMA((2,)),
            ],
            terms * pair_flops,
        )
        cuts = [first_cut(acc, halos, False)]
        cuts += [later_cut(turn, rounded, halos, False) for turn in turns[1:]]
        totals = [low_sum(*c) for c in cuts]

    with jax.named_scope("gather"):
        shifted, plus, minus, pieces = [[None] * sectors for _ in range(4)]
        row = pltpu.VMEM((span, size), jnp.float32)
        parts = [high_parts(total) for total in totals]
        held = [None] * sectors
        for turn in turns:
            held[turn], shifted[turn], plus[turn], minus[turn] = call(
                functools.partial(shift_kernel, dims, turn, scale),
                [jax.ShapeDtypeStruct((span, size), jnp.bfloat16), row, row, row],
                (sector_sizes,),
                (start, left_energy, right_energy, *parts[turn]),
            )
        for turn in turns:
            mine = gather_high(held[turn][None], held[min(turn + 1, sectors - 1)])
            theirs = lax.ppermute(mine, "term", pairs_low(ranks)) if low > 1 else mine
            pieces[turn] = [mine, theirs]

    with jax.named_scope("second"):
        acc, block = call(
            functools.partial(self_kernel, dims),
            [square, square_low],
            (sector_shifts,),
            (left, right, *pieces[0]),
            flops=terms * pair_flops // 3,
        )
        whole = after_all(jnp.stack(pieces[0]), pieces[-1][1], acc)
        halos = [halo(edge, n) for n, edge in enumerate((whole, jnp.stack(pieces[-1])))]
        acc, own = call(
            functools.partial(inner_kernel, dims),
            [square, pltpu.VMEM((sectors, size, size), jnp.bfloat16)],
            (sector_shifts,),
            (acc, block, left, right, *[piece for both in pieces[1:] for piece in both]),
            flops=terms * pair_flops // 3,
        )
        cuts = [first_cut(acc, halos, True)]
        (sums,) = call(
            functools.partial(sums_kernel, dims),
            [jax.ShapeDtypeStruct((8, size), jnp.float32)],
            (sector_sizes,),
            (lanczos_vector, after_all(own, *cuts[0])),
        )
        own = after_all(own, sums)
        cuts += [later_cut(turn, own, halos, True) for turn in turns[1:]]
        totals = [low_sum(*c) for c in cuts]

    with jax.named_scope("scalars"):
        parts = [high_parts(total) for total in totals]
        sums = after_all(sums, totals[-1], parts[0][-1])
        tables, reach = [sums], 1
        while reach < groups:
            if groups & (groups - 1):
                tables, reach = [lax.psum(sums, "sector")], groups
            else:
                sums, width = sum(tables), min(4, groups // reach)
                tables = [sums] + [
                    lax.ppermute(sums, "sector", [(i, i ^ (reach * k)) for i in range(groups)])
                    for k in range(1, width)
                ]
                reach *= width
        out = jax.ShapeDtypeStruct((sectors, span, size), jnp.float32)
        flat = [part for each in parts for part in each]
        return call(
            functools.partial(finish_kernel, dims, cells, scale),
            [out, out],
            (sector_sizes,),
            (start, *shifted, *plus, *minus, *flat, *tables),
        )


def solution(mesh):
    return jax.shard_map(
        on_device,
        mesh=mesh,
        in_specs=(
            P("sector", None, None),
            P("sector", "term", None, None),
            P("sector", "term", None, None),
            P("sector", None),
            P("sector", None),
            P("term"),
            P("sector"),
        ),
        out_specs=(P("sector", "term", None), P("sector", "term", None)),
        check_vma=False,
    )
```

```python
import functools
import jax
import jax.numpy as jnp
from jax import lax
from jax.experimental import pallas as pl
from jax.experimental.pallas import tpu as pltpu
from jax.sharding import PartitionSpec as P

epsilon = 1e-06
NT = (((1,), (1,)), ((), ()))
GUESS = 4.5


def other(hi, step, count):
    return hi ^ step if count & (count - 1) == 0 else (step - hi) % count


def traced_other(hi, step, count):
    return hi ^ step if count & (count - 1) == 0 else lax.rem(step - hi + count, count)


def pairs_low(size):
    return [(i, i ^ 1) for i in range(size)]


def pairs_high(size, low, step):
    count = size // low
    return [(i, other(i // low, step, count) * low + i % low) for i in range(size)]


def row_finder(count, low, span):
    rank = lax.axis_index("term")
    hi, lo = rank // low, lax.rem(rank, low)

    def row_of(step, far):
        digit = 1 - lo if far else lo
        return pl.multiple_of((traced_other(hi, step, count) * low + digit) * span, span)

    return row_of


def add_pair(acc, left, right, block):
    mixed = jnp.dot(left[...], block[...], preferred_element_type=jnp.float32)
    acc[...] += lax.dot_general(
        mixed.astype(jnp.bfloat16), right[...], NT, preferred_element_type=jnp.float32
    )


def sector_at(turn, sectors):
    odd = lax.rem(lax.axis_index("sector"), 2)
    return odd * turn + (1 - odd) * (sectors - 1 - turn)


def halos_at(turn, sectors):
    return ([0] if turn == 0 else []) + ([1] if turn == sectors - 1 else [])


def halo_side(halo):
    here, groups = lax.axis_index("sector"), lax.axis_size("sector")
    side = (1 - 2 * lax.rem(here, 2)) * (1 - 2 * halo)
    return side, (here + side >= 0) & (here + side < groups)


def add_inner(dims, s, shift_ref, acc, left, right, wb, before_term=lambda t: None):
    sectors, terms = dims[:2]
    for t in range(terms):
        before_term(t)
        partner = s + shift_ref[t]

        @pl.when((partner >= 0) & (partner < sectors))
        def _():
            add_pair(acc, left.at[s, t], right.at[s, t], wb.at[partner])


def place_rows(dims, wb, pieces):
    sectors, terms, size, count, low, span = dims
    row_of = row_finder(count, low, span)
    for far in range(low):
        for step in range(count):
            wb[pl.ds(row_of(step, far), span), :] = pieces[far][step]


def add_outer(dims, turn, gathered, shift_ref, acc, left, right, blocks, wb):
    sectors, terms = dims[:2]
    s = sector_at(turn, sectors)
    for block, halo in zip(blocks, halos_at(turn, sectors)):
        if gathered:
            place_rows(dims, wb, [block.at[0], block.at[1]])
            held = wb
        else:
            held = block
        side, there = halo_side(halo)
        for t in range(terms):

            @pl.when((shift_ref[t] == side) & there)
            def _():
                add_pair(acc, left.at[s, t], right.at[s, t], held)


def cut(dims, acc, send_ref, keep_ref):
    sectors, terms, size, count, low, span = dims
    row_of = row_finder(count, low, span)
    for step in range(count):
        if low > 1:
            send_ref[step] = acc[pl.ds(row_of(step, 1), span), :].astype(jnp.bfloat16)
        keep_ref[step] = acc[pl.ds(row_of(step, 0), span), :]


def live_tile(shape, first_row, limit):
    row = first_row + lax.broadcasted_iota(jnp.int32, shape, 0)
    return (row < limit) & (lax.broadcasted_iota(jnp.int32, shape, 1) < limit)


def energy_rows(left_row, right_row, s, first, span):
    shape = (span, left_row.shape[1])
    row = first + lax.broadcasted_iota(jnp.int32, shape, 0)
    here = row == lax.broadcasted_iota(jnp.int32, shape, 1)
    left = jnp.sum(jnp.where(here, left_row[pl.ds(s, 1), :], 0.0), axis=1, keepdims=True)
    return left + right_row[pl.ds(s, 1), :]


def round_kernel(size_hbm, vector_hbm, rounded, edge, other_edge, vector, sizes, sems):
    sectors, size = vector.shape[:2]
    parts = sems.shape[0] // sectors
    rows = size // parts
    tile = min(64, rows)
    limits = pltpu.make_async_copy(size_hbm, sizes, sems.at[sectors * parts])
    limits.start()
    copies = [
        pltpu.make_async_copy(
            vector_hbm.at[sector_at(turn, sectors), pl.ds(n * rows, rows), :],
            vector.at[turn, pl.ds(n * rows, rows), :],
            sems.at[turn * parts + n],
        )
        for turn in range(sectors)
        for n in range(parts)
    ]
    for copy in copies:
        copy.start()
    limits.wait()
    for turn in range(sectors):
        s = sector_at(turn, sectors)
        for n in range(parts):
            copies[turn * parts + n].wait()

            @pl.loop(0, rows // tile)
            def _(k):
                first = pl.multiple_of(n * rows + k * tile, tile)
                part = pl.ds(first, tile)
                live = live_tile((tile, size), first, sizes[s])
                value = jnp.where(live, vector[turn, part, :], 0.0).astype(jnp.bfloat16)
                rounded[s, part, :] = value
                if turn == 0:
                    edge[part, :] = value
                if turn == sectors - 1:
                    other_edge[part, :] = value


def load_kernel(
    dims, wb, shift_hbm, size_hbm, left_hbm, right_hbm, vector_hbm,
    acc, left, right, start, shift_ref, size_ref, sems, row_sems, scalar_sems,
):
    sectors, terms, size, count, low, span = dims
    scalars = [
        pltpu.make_async_copy(shift_hbm, shift_ref, scalar_sems.at[0]),
        pltpu.make_async_copy(size_hbm, size_ref, scalar_sems.at[1]),
    ]
    for copy in scalars:
        copy.start()
    first = row_finder(count, low, span)(0, 0)
    rows = [
        pltpu.make_async_copy(vector_hbm.at[s, pl.ds(first, span), :], start.at[s], row_sems.at[s])
        for s in range(sectors)
    ]
    copies = {
        (turn, t): [
            pltpu.make_async_copy(
                hbm.at[sector_at(turn, sectors), t],
                vmem.at[sector_at(turn, sectors), t],
                sems.at[k, turn, t],
            )
            for k, (hbm, vmem) in enumerate(((left_hbm, left), (right_hbm, right)))
        ]
        for turn in range(sectors)
        for t in range(terms)
    }
    for pair in copies.values():
        for copy in pair:
            copy.start()
    for copy in rows:
        copy.start()
    acc[...] = jnp.zeros_like(acc)
    for copy in scalars:
        copy.wait()

    def arrived(t):
        for copy in copies[0, t]:
            copy.wait()

    add_inner(dims, sector_at(0, sectors), shift_ref, acc, left, right, wb, arrived)
    for s in range(sectors):
        rows[s].wait()
        live = live_tile((span, size), first, size_ref[s])
        start[s] = jnp.where(live, start[s], 0.0)
    for turn in range(1, sectors):
        for t in range(terms):
            for copy in copies[turn, t]:
                copy.wait()


def outer_kernel(dims, gathered, shift_ref, acc_ref, left, right, *refs):
    blocks, (send_ref, keep_ref, acc, wb) = refs[:-4], refs[-4:]
    acc[...] = acc_ref[...]
    add_outer(dims, 0, gathered, shift_ref, acc, left, right, blocks, wb)
    cut(dims, acc, send_ref, keep_ref)


def self_kernel(dims, shift_ref, left, right, mine, theirs, acc, own):
    s = sector_at(0, dims[0])
    acc[...] = jnp.zeros_like(acc)
    place_rows(dims, own, [mine, theirs])
    for t in range(dims[1]):

        @pl.when(shift_ref[t] == 0)
        def _():
            add_pair(acc, left.at[s, t], right.at[s, t], own)


def inner_kernel(dims, shift_ref, acc_ref, first_block, left, right, *refs):
    sectors, terms = dims[:2]
    pieces, (acc, own) = refs[:-2], refs[-2:]
    acc[...] = acc_ref[...]
    s = sector_at(0, sectors)
    own[s] = first_block[...]
    for turn in range(1, sectors):
        place_rows(dims, own.at[sector_at(turn, sectors)], pieces[2 * turn - 2 : 2 * turn])
    for t in range(terms):
        partner = s + shift_ref[t]

        @pl.when((shift_ref[t] != 0) & (partner >= 0) & (partner < sectors))
        def _():
            add_pair(acc, left.at[s, t], right.at[s, t], own.at[partner])


def full_kernel(dims, turn, gathered, shift_ref, own, left, right, *refs):
    blocks, (send_ref, keep_ref, acc, wb) = refs[:-4], refs[-4:]
    acc[...] = jnp.zeros_like(acc)
    add_inner(dims, sector_at(turn, dims[0]), shift_ref, acc, left, right, own)
    add_outer(dims, turn, gathered, shift_ref, acc, left, right, blocks, wb)
    cut(dims, acc, send_ref, keep_ref)


def sums_kernel(dims, size_ref, vector_ref, wb, sums):
    sectors, size = dims[0], dims[2]
    sums[...] = jnp.zeros_like(sums)
    tile = min(64, size)
    for s in range(sectors):

        @pl.loop(0, size // tile)
        def _(n):
            first = pl.multiple_of(n * tile, tile)
            rows = pl.ds(first, tile)
            live = live_tile((tile, size), first, size_ref[s])
            start = jnp.where(live, vector_ref[s, rows, :], 0.0)
            shifted = wb[s, rows, :].astype(jnp.float32)
            for k, term in enumerate((shifted * shifted, shifted * start, start * start)):
                sums[k : k + 1, :] += jnp.sum(term, 0, keepdims=True)


def shift_kernel(dims, turn, scale, size_ref, start, left_row, right_row, *refs):
    sectors, terms, size, count, low, span = dims
    parts, (held_ref, shifted_ref, plus_ref, minus_ref) = refs[:-4], refs[-4:]
    s = sector_at(turn, sectors)
    first = row_finder(count, low, span)(0, 0)
    total = parts[0][...]
    for part in parts[1:]:
        total += part[...].astype(jnp.float32)
    mixed = jnp.where(live_tile((span, size), first, size_ref[s]), scale * total, 0.0)
    energy = energy_rows(left_row, right_row, s, first, span)
    begin = start[s]
    shifted = mixed + (energy - GUESS) * begin
    held_ref[...] = shifted.astype(jnp.bfloat16)
    shifted_ref[...] = shifted
    plus_ref[...] = energy * shifted
    minus_ref[...] = energy * begin + mixed


def finish_kernel(dims, cells, scale, size_ref, start, *refs):
    sectors, terms, size, count, low, span = dims
    shifted, plus, minus = [refs[k * sectors : (k + 1) * sectors] for k in range(3)]
    parts, refs = refs[3 * sectors : 3 * sectors + count * sectors], refs[3 * sectors + count * sectors :]
    tables, (next_ref, sigma_ref) = refs[:-2], refs[-2:]
    first = row_finder(count, low, span)(0, 0)
    sums = sum(table[...] for table in tables)
    shifted_sq, overlap, norm_sq = [
        jnp.sum(sums[k : k + 1, :], axis=1, keepdims=True) for k in range(3)
    ]
    correlation = overlap + GUESS * norm_sq
    ritz = (correlation / cells) / (norm_sq / cells + epsilon)
    delta = ritz - GUESS
    res_sq = shifted_sq - 2.0 * delta * overlap + delta * delta * norm_sq
    inverse = lax.rsqrt(res_sq / cells + epsilon)
    for turn in range(sectors):
        s = sector_at(turn, sectors)
        next_ref[s] = (shifted[turn][...] - delta * start[s]) * inverse
        total = parts[turn * count][...]
        for part in parts[turn * count + 1 : (turn + 1) * count]:
            total += part[...].astype(jnp.float32)
        mixed = jnp.where(live_tile((span, size), first, size_ref[s]), scale * total, 0.0)
        sigma_ref[s] = (plus[turn][...] - delta * minus[turn][...] + mixed) * inverse


SMEM = pl.BlockSpec(memory_space=pltpu.SMEM)
VMEM = pl.BlockSpec(memory_space=pltpu.VMEM)
HBM = pl.BlockSpec(memory_space=pltpu.HBM)
LIMIT = pltpu.CompilerParams(vmem_limit_bytes=24 * 2**20)


def call(kernel, out_shape, scalars, arrays, matrices=(), scratch=(), flops=2**20):
    matrices = [pltpu.with_memory_space_constraint(m, pltpu.HBM) for m in matrices]
    return pl.pallas_call(
        kernel,
        out_shape=out_shape,
        in_specs=[SMEM] * len(scalars) + [VMEM] * len(arrays) + [HBM] * len(matrices),
        out_specs=[VMEM] * len(out_shape),
        scratch_shapes=scratch,
        compiler_params=LIMIT,
        cost_estimate=pl.CostEstimate(flops=flops, bytes_accessed=flops // 256, transcendentals=0),
    )(*scalars, *arrays, *matrices)


def after_all(value, *others):
    return lax.optimization_barrier((value, *others))[0]


def on_device(
    lanczos_vector, left_block, right_block, left_energy, right_energy, sector_shifts, sector_sizes
):
    sectors, size = lanczos_vector.shape[:2]
    terms, ranks = left_block.shape[1], lax.axis_size("term")
    groups = lax.axis_size("sector")
    scale = float(terms * ranks) ** (-0.5)
    cells = float(sectors * groups * size * size)
    span = size // ranks
    low = 2 if ranks % 2 == 0 else 1
    count = ranks // low
    dims = (sectors, terms, size, count, low, span)
    turns = range(sectors)
    pair_flops = 4 * size**3
    rows = pltpu.VMEM((sectors, span, size), jnp.float32)
    square = pltpu.VMEM((size, size), jnp.float32)
    square_low = pltpu.VMEM((size, size), jnp.bfloat16)
    cut_shapes = [jax.ShapeDtypeStruct((count, span, size), d) for d in (jnp.bfloat16, jnp.float32)]
    pairs = [
        [p for i in range(start, groups - 1, 2) for p in ((i, i + 1), (i + 1, i))]
        for start in range(2)
    ]

    def halo(edge, which):
        return lax.ppermute(edge, "sector", pairs[which]) if pairs[which] else edge

    def low_sum(send, keep):
        if low == 1:
            return keep
        return keep + lax.ppermute(send, "term", pairs_low(ranks)).astype(jnp.float32)

    hops = range(count - 1, 0, -1)

    def high_parts(total):
        return [total[0]] + [
            lax.ppermute(total[k].astype(jnp.bfloat16), "term", pairs_high(ranks, low, k))
            for k in hops
        ]

    def gather_high(held):
        got = {k: lax.ppermute(held, "term", pairs_high(ranks, low, k)) for k in hops}
        return jnp.concatenate([held] + [got[k] for k in range(1, count)])

    def first_cut(acc, halos, gathered):
        return call(
            functools.partial(outer_kernel, dims, gathered),
            cut_shapes,
            (sector_shifts,),
            (acc, left, right, *[halos[h] for h in halos_at(0, sectors)]),
            scratch=[square, square_low],
            flops=terms * pair_flops // 3,
        )

    def later_cut(turn, own, halos, gathered):
        return call(
            functools.partial(full_kernel, dims, turn, gathered),
            cut_shapes,
            (sector_shifts,),
            (own, left, right, *[halos[h] for h in halos_at(turn, sectors)]),
            scratch=[square, square_low],
            flops=terms * pair_flops,
        )

    with jax.named_scope("first"):
        parts = 2 if size % 256 == 0 else 1
        block = jax.ShapeDtypeStruct((size, size), jnp.bfloat16)
        rounded, *edges = call(
            round_kernel,
            [pltpu.VMEM(lanczos_vector.shape, jnp.bfloat16), block, block],
            (),
            (),
            (sector_sizes, lanczos_vector),
            [
                pltpu.VMEM(lanczos_vector.shape, jnp.float32),
                pltpu.SMEM((sectors,), jnp.int32),
                pltpu.SemaphoreType.DMA((sectors * parts + 1,)),
            ],
        )
        halos = [halo(edge, which) for which, edge in enumerate(edges)]
        matrices = pltpu.VMEM(left_block.shape, jnp.bfloat16)
        acc, left, right, start = call(
            functools.partial(load_kernel, dims),
            [square, matrices, matrices, rows],
            (),
            (rounded,),
            (sector_shifts, sector_sizes, left_block, right_block, lanczos_vector),
            [
                pltpu.SMEM((terms,), jnp.int32),
                pltpu.SMEM((sectors,), jnp.int32),
                pltpu.SemaphoreType.DMA((2, sectors, terms)),
                pltpu.SemaphoreType.DMA((sectors,)),
                pltpu.SemaphoreType.DMA((2,)),
            ],
            terms * pair_flops,
        )
        cuts = [first_cut(acc, halos, False)]
        cuts += [later_cut(turn, rounded, halos, False) for turn in turns[1:]]
        totals = [low_sum(*c) for c in cuts]

    with jax.named_scope("gather"):
        shifted, plus, minus, pieces = [[None] * sectors for _ in range(4)]
        row = pltpu.VMEM((span, size), jnp.float32)
        parts = [high_parts(total) for total in totals]
        for turn in turns:
            held, shifted[turn], plus[turn], minus[turn] = call(
                functools.partial(shift_kernel, dims, turn, scale),
                [jax.ShapeDtypeStruct((span, size), jnp.bfloat16), row, row, row],
                (sector_sizes,),
                (start, left_energy, right_energy, *parts[turn]),
            )
            mine = gather_high(held[None])
            theirs = lax.ppermute(mine, "term", pairs_low(ranks)) if low > 1 else mine
            pieces[turn] = [mine, theirs]
    with jax.named_scope("second"):
        acc, block = call(
            functools.partial(self_kernel, dims),
            [square, square_low],
            (sector_shifts,),
            (left, right, *pieces[0]),
            flops=1,
        )
        whole = after_all(jnp.stack(pieces[0]), pieces[-1][1], acc)
        halos = [halo(edge, n) for n, edge in enumerate((whole, jnp.stack(pieces[-1])))]
        acc, own = call(
            functools.partial(inner_kernel, dims),
            [square, pltpu.VMEM((sectors, size, size), jnp.bfloat16)],
            (sector_shifts,),
            (acc, block, left, right, *[piece for both in pieces[1:] for piece in both]),
            flops=terms * pair_flops // 3,
        )
        cuts = [first_cut(acc, halos, True)]
        (sums,) = call(
            functools.partial(sums_kernel, dims),
            [jax.ShapeDtypeStruct((8, size), jnp.float32)],
            (sector_sizes,),
            (lanczos_vector, after_all(own, *cuts[0])),
        )
        own = after_all(own, sums)
        cuts += [later_cut(turn, own, halos, True) for turn in turns[1:]]
        totals = [low_sum(*c) for c in cuts]

    with jax.named_scope("scalars"):
        parts = [high_parts(total) for total in totals]
        sums = after_all(sums, totals[-1], parts[0][-1])
        tables, reach = [sums], 1
        while reach < groups:
            if groups & (groups - 1):
                tables, reach = [lax.psum(sums, "sector")], groups
            else:
                sums, width = sum(tables), min(4, groups // reach)
                tables = [sums] + [
                    lax.ppermute(sums, "sector", [(i, i ^ (reach * k)) for i in range(groups)])
                    for k in range(1, width)
                ]
                reach *= width
        out = jax.ShapeDtypeStruct((sectors, span, size), jnp.float32)
        flat = [part for each in parts for part in each]
        return call(
            functools.partial(finish_kernel, dims, cells, scale),
            [out, out],
            (sector_sizes,),
            (start, *shifted, *plus, *minus, *flat, *tables),
        )


def solution(mesh):
    return jax.shard_map(
        on_device,
        mesh=mesh,
        in_specs=(
            P("sector", None, None),
            P("sector", "term", None, None),
            P("sector", "term", None, None),
            P("sector", None),
            P("sector", None),
            P("term"),
            P("sector"),
        ),
        out_specs=(P("sector", "term", None), P("sector", "term", None)),
        check_vma=False,
    )
```

```python
import functools
import jax
import jax.numpy as jnp
from jax import lax
from jax.experimental import pallas as pl
from jax.experimental.pallas import tpu as pltpu
from jax.sharding import PartitionSpec as P

epsilon = 1e-06
NT = (((1,), (1,)), ((), ()))
GUESS = 4.5


def other(hi, step, count):
    return hi ^ step if count & (count - 1) == 0 else (step - hi) % count


def traced_other(hi, step, count):
    return hi ^ step if count & (count - 1) == 0 else lax.rem(step - hi + count, count)


def pairs_low(size):
    return [(i, i ^ 1) for i in range(size)]


def pairs_high(size, low, step):
    count = size // low
    return [(i, other(i // low, step, count) * low + i % low) for i in range(size)]


def gather_steps(count):
    return [1 << b for b in reversed(range(count.bit_length() - 1))] if count & (count - 1) == 0 else None


def gather_order(count):
    order = [0]
    for step in gather_steps(count) or ():
        order += [o ^ step for o in order]
    return order if gather_steps(count) else list(range(count))


def row_finder(count, low, span):
    rank = lax.axis_index("term")
    hi, lo = rank // low, lax.rem(rank, low)

    def row_of(step, far):
        digit = 1 - lo if far else lo
        return pl.multiple_of((traced_other(hi, step, count) * low + digit) * span, span)

    return row_of


def add_pair(acc, left, right, block):
    mixed = jnp.dot(left[...], block[...], preferred_element_type=jnp.float32)
    acc[...] += lax.dot_general(
        mixed.astype(jnp.bfloat16), right[...], NT, preferred_element_type=jnp.float32
    )


def sector_at(turn, sectors):
    odd = lax.rem(lax.axis_index("sector"), 2)
    return odd * turn + (1 - odd) * (sectors - 1 - turn)


def halos_at(turn, sectors):
    return ([0] if turn == 0 else []) + ([1] if turn == sectors - 1 else [])


def halo_side(halo):
    here, groups = lax.axis_index("sector"), lax.axis_size("sector")
    side = (1 - 2 * lax.rem(here, 2)) * (1 - 2 * halo)
    return side, (here + side >= 0) & (here + side < groups)


def add_inner(dims, s, shift_ref, acc, left, right, wb, before_term=lambda t: None):
    sectors, terms = dims[:2]
    for t in range(terms):
        before_term(t)
        partner = s + shift_ref[t]

        @pl.when((partner >= 0) & (partner < sectors))
        def _():
            add_pair(acc, left.at[s, t], right.at[s, t], wb.at[partner])


def place_rows(dims, wb, pieces):
    sectors, terms, size, count, low, span = dims
    row_of = row_finder(count, low, span)
    for far in range(low):
        for n, step in enumerate(gather_order(count)):
            wb[pl.ds(row_of(step, far), span), :] = pieces[far][n]


def add_outer(dims, turn, gathered, shift_ref, acc, left, right, blocks, wb):
    sectors, terms = dims[:2]
    s = sector_at(turn, sectors)
    for block, halo in zip(blocks, halos_at(turn, sectors)):
        if gathered:
            place_rows(dims, wb, [block.at[0], block.at[1]])
            held = wb
        else:
            held = block
        side, there = halo_side(halo)
        for t in range(terms):

            @pl.when((shift_ref[t] == side) & there)
            def _():
                add_pair(acc, left.at[s, t], right.at[s, t], held)


def cut(dims, acc, send_ref, keep_ref):
    sectors, terms, size, count, low, span = dims
    row_of = row_finder(count, low, span)
    for step in range(count):
        if low > 1:
            send_ref[step] = acc[pl.ds(row_of(step, 1), span), :].astype(jnp.bfloat16)
        keep_ref[step] = acc[pl.ds(row_of(step, 0), span), :]


def live_tile(shape, first_row, limit):
    row = first_row + lax.broadcasted_iota(jnp.int32, shape, 0)
    return (row < limit) & (lax.broadcasted_iota(jnp.int32, shape, 1) < limit)


def energy_rows(left_row, right_row, s, first, span):
    shape = (span, left_row.shape[1])
    row = first + lax.broadcasted_iota(jnp.int32, shape, 0)
    here = row == lax.broadcasted_iota(jnp.int32, shape, 1)
    left = jnp.sum(jnp.where(here, left_row[pl.ds(s, 1), :], 0.0), axis=1, keepdims=True)
    return left + right_row[pl.ds(s, 1), :]


def round_kernel(size_hbm, vector_hbm, rounded, edge, other_edge, vector, sizes, sems):
    sectors, size = vector.shape[:2]
    parts = sems.shape[0] // sectors
    rows = size // parts
    tile = min(64, rows)
    limits = pltpu.make_async_copy(size_hbm, sizes, sems.at[sectors * parts])
    limits.start()
    copies = [
        pltpu.make_async_copy(
            vector_hbm.at[sector_at(turn, sectors), pl.ds(n * rows, rows), :],
            vector.at[turn, pl.ds(n * rows, rows), :],
            sems.at[turn * parts + n],
        )
        for turn in range(sectors)
        for n in range(parts)
    ]
    for copy in copies:
        copy.start()
    limits.wait()
    for turn in range(sectors):
        s = sector_at(turn, sectors)
        for n in range(parts):
            copies[turn * parts + n].wait()

            @pl.loop(0, rows // tile)
            def _(k):
                first = pl.multiple_of(n * rows + k * tile, tile)
                part = pl.ds(first, tile)
                live = live_tile((tile, size), first, sizes[s])
                value = jnp.where(live, vector[turn, part, :], 0.0).astype(jnp.bfloat16)
                rounded[s, part, :] = value
                if turn == 0:
                    edge[part, :] = value
                if turn == sectors - 1:
                    other_edge[part, :] = value


def load_kernel(
    dims, wb, shift_hbm, size_hbm, left_hbm, right_hbm, vector_hbm,
    acc, left, right, start, shift_ref, size_ref, sems, row_sems, scalar_sems,
):
    sectors, terms, size, count, low, span = dims
    scalars = [
        pltpu.make_async_copy(shift_hbm, shift_ref, scalar_sems.at[0]),
        pltpu.make_async_copy(size_hbm, size_ref, scalar_sems.at[1]),
    ]
    for copy in scalars:
        copy.start()
    first = row_finder(count, low, span)(0, 0)
    rows = [
        pltpu.make_async_copy(vector_hbm.at[s, pl.ds(first, span), :], start.at[s], row_sems.at[s])
        for s in range(sectors)
    ]
    copies = {
        (turn, t): [
            pltpu.make_async_copy(
                hbm.at[sector_at(turn, sectors), t],
                vmem.at[sector_at(turn, sectors), t],
                sems.at[k, turn, t],
            )
            for k, (hbm, vmem) in enumerate(((left_hbm, left), (right_hbm, right)))
        ]
        for turn in range(sectors)
        for t in range(terms)
    }
    for pair in copies.values():
        for copy in pair:
            copy.start()
    for copy in rows:
        copy.start()
    acc[...] = jnp.zeros_like(acc)
    for copy in scalars:
        copy.wait()

    def arrived(t):
        for copy in copies[0, t]:
            copy.wait()

    add_inner(dims, sector_at(0, sectors), shift_ref, acc, left, right, wb, arrived)
    for s in range(sectors):
        rows[s].wait()
        live = live_tile((span, size), first, size_ref[s])
        start[s] = jnp.where(live, start[s], 0.0)
    for turn in range(1, sectors):
        for t in range(terms):
            for copy in copies[turn, t]:
                copy.wait()


def outer_kernel(dims, gathered, shift_ref, acc_ref, left, right, *refs):
    blocks, (send_ref, keep_ref, acc, wb) = refs[:-4], refs[-4:]
    acc[...] = acc_ref[...]
    add_outer(dims, 0, gathered, shift_ref, acc, left, right, blocks, wb)
    cut(dims, acc, send_ref, keep_ref)


def self_kernel(dims, shift_ref, left, right, mine, theirs, acc, own):
    s = sector_at(0, dims[0])
    acc[...] = jnp.zeros_like(acc)
    place_rows(dims, own, [mine, theirs])
    for t in range(dims[1]):

        @pl.when(shift_ref[t] == 0)
        def _():
            add_pair(acc, left.at[s, t], right.at[s, t], own)


def inner_kernel(dims, shift_ref, acc_ref, first_block, left, right, *refs):
    sectors, terms = dims[:2]
    pieces, (acc, own) = refs[:-2], refs[-2:]
    acc[...] = acc_ref[...]
    s = sector_at(0, sectors)
    own[s] = first_block[...]
    for turn in range(1, sectors):
        place_rows(dims, own.at[sector_at(turn, sectors)], pieces[2 * turn - 2 : 2 * turn])
    for t in range(terms):
        partner = s + shift_ref[t]

        @pl.when((shift_ref[t] != 0) & (partner >= 0) & (partner < sectors))
        def _():
            add_pair(acc, left.at[s, t], right.at[s, t], own.at[partner])


def full_kernel(dims, turn, gathered, shift_ref, own, left, right, *refs):
    blocks, (send_ref, keep_ref, acc, wb) = refs[:-4], refs[-4:]
    acc[...] = jnp.zeros_like(acc)
    add_inner(dims, sector_at(turn, dims[0]), shift_ref, acc, left, right, own)
    add_outer(dims, turn, gathered, shift_ref, acc, left, right, blocks, wb)
    cut(dims, acc, send_ref, keep_ref)


def sums_kernel(dims, size_ref, vector_ref, wb, sums):
    sectors, size = dims[0], dims[2]
    sums[...] = jnp.zeros_like(sums)
    tile = min(64, size)
    for s in range(sectors):

        @pl.loop(0, size // tile)
        def _(n):
            first = pl.multiple_of(n * tile, tile)
            rows = pl.ds(first, tile)
            live = live_tile((tile, size), first, size_ref[s])
            start = jnp.where(live, vector_ref[s, rows, :], 0.0)
            shifted = wb[s, rows, :].astype(jnp.float32)
            for k, term in enumerate((shifted * shifted, shifted * start, start * start)):
                sums[k : k + 1, :] += jnp.sum(term, 0, keepdims=True)


def shift_kernel(dims, turn, scale, size_ref, start, left_row, right_row, *refs):
    sectors, terms, size, count, low, span = dims
    parts, (held_ref, shifted_ref, plus_ref, minus_ref) = refs[:-4], refs[-4:]
    s = sector_at(turn, sectors)
    first = row_finder(count, low, span)(0, 0)
    total = parts[0][...]
    for part in parts[1:]:
        total += part[...].astype(jnp.float32)
    mixed = jnp.where(live_tile((span, size), first, size_ref[s]), scale * total, 0.0)
    energy = energy_rows(left_row, right_row, s, first, span)
    begin = start[s]
    shifted = mixed + (energy - GUESS) * begin
    held_ref[...] = shifted.astype(jnp.bfloat16)
    shifted_ref[...] = shifted
    plus_ref[...] = energy * shifted
    minus_ref[...] = energy * begin + mixed


def finish_kernel(dims, cells, scale, size_ref, start, *refs):
    sectors, terms, size, count, low, span = dims
    shifted, plus, minus = [refs[k * sectors : (k + 1) * sectors] for k in range(3)]
    parts, refs = refs[3 * sectors : 3 * sectors + count * sectors], refs[3 * sectors + count * sectors :]
    tables, (next_ref, sigma_ref) = refs[:-2], refs[-2:]
    first = row_finder(count, low, span)(0, 0)
    sums = sum(table[...] for table in tables)
    shifted_sq, overlap, norm_sq = [
        jnp.sum(sums[k : k + 1, :], axis=1, keepdims=True) for k in range(3)
    ]
    correlation = overlap + GUESS * norm_sq
    ritz = (correlation / cells) / (norm_sq / cells + epsilon)
    delta = ritz - GUESS
    res_sq = shifted_sq - 2.0 * delta * overlap + delta * delta * norm_sq
    inverse = lax.rsqrt(res_sq / cells + epsilon)
    for turn in range(sectors):
        s = sector_at(turn, sectors)
        next_ref[s] = (shifted[turn][...] - delta * start[s]) * inverse
        total = parts[turn * count][...]
        for part in parts[turn * count + 1 : (turn + 1) * count]:
            total += part[...].astype(jnp.float32)
        mixed = jnp.where(live_tile((span, size), first, size_ref[s]), scale * total, 0.0)
        sigma_ref[s] = (plus[turn][...] - delta * minus[turn][...] + mixed) * inverse


SMEM = pl.BlockSpec(memory_space=pltpu.SMEM)
VMEM = pl.BlockSpec(memory_space=pltpu.VMEM)
HBM = pl.BlockSpec(memory_space=pltpu.HBM)
LIMIT = pltpu.CompilerParams(vmem_limit_bytes=24 * 2**20)


def call(kernel, out_shape, scalars, arrays, matrices=(), scratch=(), flops=2**20):
    matrices = [pltpu.with_memory_space_constraint(m, pltpu.HBM) for m in matrices]
    return pl.pallas_call(
        kernel,
        out_shape=out_shape,
        in_specs=[SMEM] * len(scalars) + [VMEM] * len(arrays) + [HBM] * len(matrices),
        out_specs=[VMEM] * len(out_shape),
        scratch_shapes=scratch,
        compiler_params=LIMIT,
        cost_estimate=pl.CostEstimate(flops=flops, bytes_accessed=flops // 256, transcendentals=0),
    )(*scalars, *arrays, *matrices)


def after_all(value, *others):
    return lax.optimization_barrier((value, *others))[0]


def on_device(
    lanczos_vector, left_block, right_block, left_energy, right_energy, sector_shifts, sector_sizes
):
    sectors, size = lanczos_vector.shape[:2]
    terms, ranks = left_block.shape[1], lax.axis_size("term")
    groups = lax.axis_size("sector")
    scale = float(terms * ranks) ** (-0.5)
    cells = float(sectors * groups * size * size)
    span = size // ranks
    low = 2 if ranks % 2 == 0 else 1
    count = ranks // low
    dims = (sectors, terms, size, count, low, span)
    turns = range(sectors)
    pair_flops = 4 * size**3
    rows = pltpu.VMEM((sectors, span, size), jnp.float32)
    square = pltpu.VMEM((size, size), jnp.float32)
    square_low = pltpu.VMEM((size, size), jnp.bfloat16)
    cut_shapes = [jax.ShapeDtypeStruct((count, span, size), d) for d in (jnp.bfloat16, jnp.float32)]
    pairs = [
        [p for i in range(start, groups - 1, 2) for p in ((i, i + 1), (i + 1, i))]
        for start in range(2)
    ]

    def halo(edge, which):
        return lax.ppermute(edge, "sector", pairs[which]) if pairs[which] else edge

    def low_sum(send, keep):
        if low == 1:
            return keep
        return keep + lax.ppermute(send, "term", pairs_low(ranks)).astype(jnp.float32)

    hops = range(count - 1, 0, -1)

    def high_parts(total):
        return [total[0]] + [
            lax.ppermute(total[k].astype(jnp.bfloat16), "term", pairs_high(ranks, low, k))
            for k in hops
        ]

    def gather_high(held):
        steps = gather_steps(count)
        if steps is None:
            got = [lax.ppermute(held, "term", pairs_high(ranks, low, k)) for k in range(1, count)]
            return jnp.concatenate([held, *got])
        for step in steps:
            got = lax.ppermute(held, "term", pairs_high(ranks, low, step))
            held = jnp.concatenate([held, got])
        return held

    def first_cut(acc, halos, gathered):
        return call(
            functools.partial(outer_kernel, dims, gathered),
            cut_shapes,
            (sector_shifts,),
            (acc, left, right, *[halos[h] for h in halos_at(0, sectors)]),
            scratch=[square, square_low],
            flops=terms * pair_flops // 3,
        )

    def later_cut(turn, own, halos, gathered):
        return call(
            functools.partial(full_kernel, dims, turn, gathered),
            cut_shapes,
            (sector_shifts,),
            (own, left, right, *[halos[h] for h in halos_at(turn, sectors)]),
            scratch=[square, square_low],
            flops=terms * pair_flops,
        )

    with jax.named_scope("first"):
        parts = 2 if size % 256 == 0 else 1
        block = jax.ShapeDtypeStruct((size, size), jnp.bfloat16)
        rounded, *edges = call(
            round_kernel,
            [pltpu.VMEM(lanczos_vector.shape, jnp.bfloat16), block, block],
            (),
            (),
            (sector_sizes, lanczos_vector),
            [
                pltpu.VMEM(lanczos_vector.shape, jnp.float32),
                pltpu.SMEM((sectors,), jnp.int32),
                pltpu.SemaphoreType.DMA((sectors * parts + 1,)),
            ],
        )
        halos = [halo(edge, which) for which, edge in enumerate(edges)]
        matrices = pltpu.VMEM(left_block.shape, jnp.bfloat16)
        acc, left, right, start = call(
            functools.partial(load_kernel, dims),
            [square, matrices, matrices, rows],
            (),
            (rounded,),
            (sector_shifts, sector_sizes, left_block, right_block, lanczos_vector),
            [
                pltpu.SMEM((terms,), jnp.int32),
                pltpu.SMEM((sectors,), jnp.int32),
                pltpu.SemaphoreType.DMA((2, sectors, terms)),
                pltpu.SemaphoreType.DMA((sectors,)),
                pltpu.SemaphoreType.DMA((2,)),
            ],
            terms * pair_flops,
        )
        cuts = [first_cut(acc, halos, False)]
        cuts += [later_cut(turn, rounded, halos, False) for turn in turns[1:]]
        totals = [low_sum(*c) for c in cuts]

    with jax.named_scope("gather"):
        shifted, plus, minus, pieces = [[None] * sectors for _ in range(4)]
        row = pltpu.VMEM((span, size), jnp.float32)
        parts = [high_parts(total) for total in totals]
        for turn in turns:
            held, shifted[turn], plus[turn], minus[turn] = call(
                functools.partial(shift_kernel, dims, turn, scale),
                [jax.ShapeDtypeStruct((span, size), jnp.bfloat16), row, row, row],
                (sector_sizes,),
                (start, left_energy, right_energy, *parts[turn]),
            )
            mine = gather_high(held[None])
            theirs = lax.ppermute(mine, "term", pairs_low(ranks)) if low > 1 else mine
            pieces[turn] = [mine, theirs]
    with jax.named_scope("second"):
        acc, block = call(
            functools.partial(self_kernel, dims),
            [square, square_low],
            (sector_shifts,),
            (left, right, *pieces[0]),
            flops=1,
        )
        whole = after_all(jnp.stack(pieces[0]), pieces[-1][1], acc)
        halos = [halo(edge, n) for n, edge in enumerate((whole, jnp.stack(pieces[-1])))]
        acc, own = call(
            functools.partial(inner_kernel, dims),
            [square, pltpu.VMEM((sectors, size, size), jnp.bfloat16)],
            (sector_shifts,),
            (acc, block, left, right, *[piece for both in pieces[1:] for piece in both]),
            flops=terms * pair_flops // 3,
        )
        cuts = [first_cut(acc, halos, True)]
        (sums,) = call(
            functools.partial(sums_kernel, dims),
            [jax.ShapeDtypeStruct((8, size), jnp.float32)],
            (sector_sizes,),
            (lanczos_vector, after_all(own, *cuts[0])),
        )
        own = after_all(own, sums)
        cuts += [later_cut(turn, own, halos, True) for turn in turns[1:]]
        totals = [low_sum(*c) for c in cuts]

    with jax.named_scope("scalars"):
        parts = [high_parts(total) for total in totals]
        sums = after_all(sums, totals[-1], parts[0][-1])
        tables, reach = [sums], 1
        while reach < groups:
            if groups & (groups - 1):
                tables, reach = [lax.psum(sums, "sector")], groups
            else:
                sums, width = sum(tables), min(4, groups // reach)
                tables = [sums] + [
                    lax.ppermute(sums, "sector", [(i, i ^ (reach * k)) for i in range(groups)])
                    for k in range(1, width)
                ]
                reach *= width
        out = jax.ShapeDtypeStruct((sectors, span, size), jnp.float32)
        flat = [part for each in parts for part in each]
        return call(
            functools.partial(finish_kernel, dims, cells, scale),
            [out, out],
            (sector_sizes,),
            (start, *shifted, *plus, *minus, *flat, *tables),
        )


def solution(mesh):
    return jax.shard_map(
        on_device,
        mesh=mesh,
        in_specs=(
            P("sector", None, None),
            P("sector", "term", None, None),
            P("sector", "term", None, None),
            P("sector", None),
            P("sector", None),
            P("term"),
            P("sector"),
        ),
        out_specs=(P("sector", "term", None), P("sector", "term", None)),
        check_vma=False,
    )
```

```python
import functools
import jax
import jax.numpy as jnp
from jax import lax
from jax.experimental import pallas as pl
from jax.experimental.pallas import tpu as pltpu
from jax.sharding import PartitionSpec as P

epsilon = 1e-06
NT = (((1,), (1,)), ((), ()))
GUESS = 4.5


def other(hi, step, count):
    return hi ^ step if count & (count - 1) == 0 else (step - hi) % count


def traced_other(hi, step, count):
    return hi ^ step if count & (count - 1) == 0 else lax.rem(step - hi + count, count)


def pairs_low(size):
    return [(i, i ^ 1) for i in range(size)]


def pairs_high(size, low, step):
    count = size // low
    return [(i, other(i // low, step, count) * low + i % low) for i in range(size)]


def row_finder(count, low, span):
    rank = lax.axis_index("term")
    hi, lo = rank // low, lax.rem(rank, low)

    def row_of(step, far):
        digit = 1 - lo if far else lo
        return pl.multiple_of((traced_other(hi, step, count) * low + digit) * span, span)

    return row_of


def add_pair(acc, left, right, block):
    mixed = jnp.dot(left[...], block[...], preferred_element_type=jnp.float32)
    acc[...] += lax.dot_general(
        mixed.astype(jnp.bfloat16), right[...], NT, preferred_element_type=jnp.float32
    )


def sector_at(turn, sectors):
    odd = lax.rem(lax.axis_index("sector"), 2)
    return odd * turn + (1 - odd) * (sectors - 1 - turn)


def halos_at(turn, sectors):
    return ([0] if turn == 0 else []) + ([1] if turn == sectors - 1 else [])


def halo_side(halo):
    here, groups = lax.axis_index("sector"), lax.axis_size("sector")
    side = (1 - 2 * lax.rem(here, 2)) * (1 - 2 * halo)
    return side, (here + side >= 0) & (here + side < groups)


def add_pairs(dims, turn, shift_ref, acc, left, right, own, halos, arrived=None, skip_own=False):
    sectors, terms = dims[:2]
    s = sector_at(turn, sectors)
    for t in range(terms):
        if arrived is not None:
            arrived(t)
        partner = s + shift_ref[t]
        inside = (partner >= 0) & (partner < sectors)
        if skip_own:
            inside &= shift_ref[t] != 0

        @pl.when(inside)
        def _():
            add_pair(acc, left.at[t], right.at[t], own.at[partner])

        for block, halo in zip(halos, halos_at(turn, sectors)):
            side, there = halo_side(halo)

            @pl.when((shift_ref[t] == side) & there)
            def _():
                add_pair(acc, left.at[t], right.at[t], block)


def place_rows(dims, wb, pieces):
    sectors, terms, size, count, low, span = dims
    row_of = row_finder(count, low, span)
    for far in range(low):
        for step in range(count):
            wb[pl.ds(row_of(step, far), span), :] = pieces[far][step]


def cut(dims, acc, send_ref, keep_ref):
    sectors, terms, size, count, low, span = dims
    row_of = row_finder(count, low, span)
    for step in range(count):
        if low > 1:
            send_ref[step] = acc[pl.ds(row_of(step, 1), span), :].astype(jnp.bfloat16)
        keep_ref[step] = acc[pl.ds(row_of(step, 0), span), :]


def live_tile(shape, first_row, limit):
    row = first_row + lax.broadcasted_iota(jnp.int32, shape, 0)
    return (row < limit) & (lax.broadcasted_iota(jnp.int32, shape, 1) < limit)


def energy_rows(left_row, right_row, s, first, span):
    shape = (span, left_row.shape[1])
    row = first + lax.broadcasted_iota(jnp.int32, shape, 0)
    here = row == lax.broadcasted_iota(jnp.int32, shape, 1)
    left = jnp.sum(jnp.where(here, left_row[pl.ds(s, 1), :], 0.0), axis=1, keepdims=True)
    return left + right_row[pl.ds(s, 1), :]


def round_kernel(size_hbm, vector_hbm, rounded, edge, other_edge, vector, sizes, sems):
    sectors, size = vector.shape[:2]
    parts = sems.shape[0] // sectors
    rows = size // parts
    tile = min(64, rows)
    limits = pltpu.make_async_copy(size_hbm, sizes, sems.at[sectors * parts])
    limits.start()
    copies = [
        pltpu.make_async_copy(
            vector_hbm.at[sector_at(turn, sectors), pl.ds(n * rows, rows), :],
            vector.at[turn, pl.ds(n * rows, rows), :],
            sems.at[turn * parts + n],
        )
        for turn in range(sectors)
        for n in range(parts)
    ]
    for copy in copies:
        copy.start()
    limits.wait()
    for turn in range(sectors):
        s = sector_at(turn, sectors)
        for n in range(parts):
            copies[turn * parts + n].wait()

            @pl.loop(0, rows // tile)
            def _(k):
                first = pl.multiple_of(n * rows + k * tile, tile)
                part = pl.ds(first, tile)
                live = live_tile((tile, size), first, sizes[s])
                value = jnp.where(live, vector[turn, part, :], 0.0).astype(jnp.bfloat16)
                rounded[s, part, :] = value
                if turn == 0:
                    edge[part, :] = value
                if turn == sectors - 1:
                    other_edge[part, :] = value


def load_kernel(dims, turn, own, *refs):
    sectors, terms, size, count, low, span = dims
    blocks, refs = refs[: len(halos_at(turn, sectors))], refs[len(halos_at(turn, sectors)) :]
    shift_hbm, size_hbm, left_hbm, right_hbm, vector_hbm, send_ref, keep_ref, left, right, *refs = refs
    start, refs = (refs[0], refs[1:]) if turn == 0 else (None, refs)
    acc, shift_ref, size_ref, sems, row_sems, scalar_sems = refs
    s = sector_at(turn, sectors)
    scalars = [
        pltpu.make_async_copy(shift_hbm, shift_ref, scalar_sems.at[0]),
        pltpu.make_async_copy(size_hbm, size_ref, scalar_sems.at[1]),
    ]
    copies = [
        [
            pltpu.make_async_copy(hbm.at[s, t], vmem.at[t], sems.at[k, t])
            for k, (hbm, vmem) in enumerate(((left_hbm, left), (right_hbm, right)))
        ]
        for t in range(terms)
    ]
    first = row_finder(count, low, span)(0, 0)
    rows = [
        pltpu.make_async_copy(vector_hbm.at[e, pl.ds(first, span), :], start.at[e], row_sems.at[e])
        for e in range(sectors if turn == 0 else 0)
    ]
    for copy in scalars:
        copy.start()
    for pair in copies:
        for copy in pair:
            copy.start()
    for copy in rows:
        copy.start()
    acc[...] = jnp.zeros_like(acc)
    for copy in scalars:
        copy.wait()

    def arrived(t):
        for copy in copies[t]:
            copy.wait()

    add_pairs(dims, turn, shift_ref, acc, left, right, own, blocks, arrived)
    cut(dims, acc, send_ref, keep_ref)
    for e, copy in enumerate(rows):
        copy.wait()
        live = live_tile((span, size), first, size_ref[e])
        start[e] = jnp.where(live, start[e], 0.0)


def self_kernel(dims, shift_ref, left, right, mine, theirs, acc, own):
    acc[...] = jnp.zeros_like(acc)
    place_rows(dims, own, [mine, theirs])
    for t in range(dims[1]):

        @pl.when(shift_ref[t] == 0)
        def _():
            add_pair(acc, left.at[t], right.at[t], own)


def rest_kernel(dims, shift_ref, acc_ref, first_block, left, right, *refs):
    sectors = dims[0]
    pieces, refs = refs[: 2 * sectors - 2], refs[2 * sectors - 2 :]
    halos, (send_ref, keep_ref, own, acc, wb) = refs[:-5], refs[-5:]
    acc[...] = acc_ref[...]
    own[sector_at(0, sectors)] = first_block[...]
    for turn in range(1, sectors):
        place_rows(dims, own.at[sector_at(turn, sectors)], pieces[2 * turn - 2 : 2 * turn])
    for n, halo in enumerate(halos):
        place_rows(dims, wb.at[n], [halo.at[0], halo.at[1]])
    blocks = [wb.at[n] for n in range(len(halos))]
    add_pairs(dims, 0, shift_ref, acc, left, right, own, blocks, skip_own=True)
    cut(dims, acc, send_ref, keep_ref)


def full_kernel(dims, turn, shift_ref, own, left, right, *refs):
    halos, (send_ref, keep_ref, acc, wb) = refs[:-4], refs[-4:]
    acc[...] = jnp.zeros_like(acc)
    for n, halo in enumerate(halos):
        place_rows(dims, wb.at[n], [halo.at[0], halo.at[1]])
    blocks = [wb.at[n] for n in range(len(halos))]
    add_pairs(dims, turn, shift_ref, acc, left, right, own, blocks)
    cut(dims, acc, send_ref, keep_ref)


def sums_kernel(dims, turn, size_ref, vector_ref, block, sums):
    size = dims[2]
    s = sector_at(turn, dims[0])
    sums[...] = jnp.zeros_like(sums)
    tile = min(64, size)

    @pl.loop(0, size // tile)
    def _(n):
        first = pl.multiple_of(n * tile, tile)
        rows = pl.ds(first, tile)
        live = live_tile((tile, size), first, size_ref[s])
        start = jnp.where(live, vector_ref[s, rows, :], 0.0)
        shifted = (block[rows, :] if turn == 0 else block[s, rows, :]).astype(jnp.float32)
        for k, term in enumerate((shifted * shifted, shifted * start, start * start)):
            sums[k : k + 1, :] += jnp.sum(term, 0, keepdims=True)


def shift_kernel(dims, turn, scale, size_ref, start, left_row, right_row, *refs):
    sectors, terms, size, count, low, span = dims
    parts, (held_ref, shifted_ref, plus_ref, minus_ref) = refs[:-4], refs[-4:]
    s = sector_at(turn, sectors)
    first = row_finder(count, low, span)(0, 0)
    total = parts[0][...]
    for part in parts[1:]:
        total += part[...].astype(jnp.float32)
    mixed = jnp.where(live_tile((span, size), first, size_ref[s]), scale * total, 0.0)
    energy = energy_rows(left_row, right_row, s, first, span)
    begin = start[s]
    shifted = mixed + (energy - GUESS) * begin
    held_ref[...] = shifted.astype(jnp.bfloat16)
    shifted_ref[...] = shifted
    plus_ref[...] = energy * shifted
    minus_ref[...] = energy * begin + mixed


def finish_kernel(dims, cells, scale, size_ref, start, *refs):
    sectors, terms, size, count, low, span = dims
    shifted, plus, minus = [refs[k * sectors : (k + 1) * sectors] for k in range(3)]
    parts, refs = refs[3 * sectors : 3 * sectors + count * sectors], refs[3 * sectors + count * sectors :]
    tables, (next_ref, sigma_ref) = refs[:-2], refs[-2:]
    first = row_finder(count, low, span)(0, 0)
    sums = sum(table[...] for table in tables)
    shifted_sq, overlap, norm_sq = [
        jnp.sum(sums[k : k + 1, :], axis=1, keepdims=True) for k in range(3)
    ]
    correlation = overlap + GUESS * norm_sq
    ritz = (correlation / cells) / (norm_sq / cells + epsilon)
    delta = ritz - GUESS
    res_sq = shifted_sq - 2.0 * delta * overlap + delta * delta * norm_sq
    inverse = lax.rsqrt(res_sq / cells + epsilon)
    for turn in range(sectors):
        s = sector_at(turn, sectors)
        next_ref[s] = (shifted[turn][...] - delta * start[s]) * inverse
        total = parts[turn * count][...]
        for part in parts[turn * count + 1 : (turn + 1) * count]:
            total += part[...].astype(jnp.float32)
        mixed = jnp.where(live_tile((span, size), first, size_ref[s]), scale * total, 0.0)
        sigma_ref[s] = (plus[turn][...] - delta * minus[turn][...] + mixed) * inverse


SMEM = pl.BlockSpec(memory_space=pltpu.SMEM)
VMEM = pl.BlockSpec(memory_space=pltpu.VMEM)
HBM = pl.BlockSpec(memory_space=pltpu.HBM)
LIMIT = pltpu.CompilerParams(vmem_limit_bytes=24 * 2**20)


def call(kernel, out_shape, scalars, arrays, matrices=(), scratch=(), flops=2**20):
    matrices = [pltpu.with_memory_space_constraint(m, pltpu.HBM) for m in matrices]
    return pl.pallas_call(
        kernel,
        out_shape=out_shape,
        in_specs=[SMEM] * len(scalars) + [VMEM] * len(arrays) + [HBM] * len(matrices),
        out_specs=[VMEM] * len(out_shape),
        scratch_shapes=scratch,
        compiler_params=LIMIT,
        cost_estimate=pl.CostEstimate(flops=flops, bytes_accessed=flops // 256, transcendentals=0),
    )(*scalars, *arrays, *matrices)


def after_all(value, *others):
    return lax.optimization_barrier((value, *others))[0]


def on_device(
    lanczos_vector, left_block, right_block, left_energy, right_energy, sector_shifts, sector_sizes
):
    sectors, size = lanczos_vector.shape[:2]
    terms, ranks = left_block.shape[1], lax.axis_size("term")
    groups = lax.axis_size("sector")
    scale = float(terms * ranks) ** (-0.5)
    cells = float(sectors * groups * size * size)
    span = size // ranks
    low = 2 if ranks % 2 == 0 else 1
    count = ranks // low
    dims = (sectors, terms, size, count, low, span)
    turns = range(sectors)
    pair_flops = 4 * size**3
    rows = pltpu.VMEM((sectors, span, size), jnp.float32)
    square = pltpu.VMEM((size, size), jnp.float32)
    square_low = pltpu.VMEM((size, size), jnp.bfloat16)
    cut_shapes = [jax.ShapeDtypeStruct((count, span, size), d) for d in (jnp.bfloat16, jnp.float32)]
    pairs = [
        [p for i in range(start, groups - 1, 2) for p in ((i, i + 1), (i + 1, i))]
        for start in range(2)
    ]

    def halo(edge, which):
        return lax.ppermute(edge, "sector", pairs[which]) if pairs[which] else edge

    def low_sum(send, keep):
        if low == 1:
            return keep
        return keep + lax.ppermute(send, "term", pairs_low(ranks)).astype(jnp.float32)

    hops = range(count - 1, 0, -1)

    def high_parts(total):
        return [total[0]] + [
            lax.ppermute(total[k].astype(jnp.bfloat16), "term", pairs_high(ranks, low, k))
            for k in hops
        ]

    def gather_high(held):
        got = {k: lax.ppermute(held, "term", pairs_high(ranks, low, k)) for k in hops}
        return jnp.concatenate([held] + [got[k] for k in range(1, count)])

    with jax.named_scope("first"):
        parts = 2 if size % 256 == 0 else 1
        block = jax.ShapeDtypeStruct((size, size), jnp.bfloat16)
        rounded, *edges = call(
            round_kernel,
            [pltpu.VMEM(lanczos_vector.shape, jnp.bfloat16), block, block],
            (),
            (),
            (sector_sizes, lanczos_vector),
            [
                pltpu.VMEM(lanczos_vector.shape, jnp.float32),
                pltpu.SMEM((sectors,), jnp.int32),
                pltpu.SemaphoreType.DMA((sectors * parts + 1,)),
            ],
        )
        halos = [halo(edge, which) for which, edge in enumerate(edges)]
        matrices = pltpu.VMEM((terms, size, size), jnp.bfloat16)
        cuts, left, right = [], [None] * sectors, [None] * sectors
        for turn in turns:
            send, keep, left[turn], right[turn], *more = call(
                functools.partial(load_kernel, dims, turn),
                [*cut_shapes, matrices, matrices] + ([rows] if turn == 0 else []),
                (),
                (rounded, *[halos[h] for h in halos_at(turn, sectors)]),
                (sector_shifts, sector_sizes, left_block, right_block, lanczos_vector),
                [
                    square,
                    pltpu.SMEM((terms,), jnp.int32),
                    pltpu.SMEM((sectors,), jnp.int32),
                    pltpu.SemaphoreType.DMA((2, terms)),
                    pltpu.SemaphoreType.DMA((sectors,)),
                    pltpu.SemaphoreType.DMA((2,)),
                ],
                terms * pair_flops,
            )
            cuts.append((send, keep))
            start = more[0] if turn == 0 else start
        totals = [low_sum(*c) for c in cuts]

    with jax.named_scope("gather"):
        shifted, plus, minus, pieces = [[None] * sectors for _ in range(4)]
        row = pltpu.VMEM((span, size), jnp.float32)
        parts = [high_parts(total) for total in totals]
        for turn in turns:
            held, shifted[turn], plus[turn], minus[turn] = call(
                functools.partial(shift_kernel, dims, turn, scale),
                [jax.ShapeDtypeStruct((span, size), jnp.bfloat16), row, row, row],
                (sector_sizes,),
                (start, left_energy, right_energy, *parts[turn]),
            )
            mine = gather_high(held[None])
            theirs = lax.ppermute(mine, "term", pairs_low(ranks)) if low > 1 else mine
            pieces[turn] = [mine, theirs]
    def sector_sums(turn, block):
        return call(
            functools.partial(sums_kernel, dims, turn),
            [jax.ShapeDtypeStruct((8, size), jnp.float32)],
            (sector_sizes,),
            (lanczos_vector, block),
            flops=1,
        )[0]

    with jax.named_scope("second"):
        acc, block = call(
            functools.partial(self_kernel, dims),
            [square, square_low],
            (sector_shifts,),
            (left[0], right[0], *pieces[0]),
            flops=1,
        )
        sums = [sector_sums(0, block)]
        whole = after_all(jnp.stack(pieces[0]), pieces[-1][1], acc, sums[0])
        halos = [halo(edge, n) for n, edge in enumerate((whole, jnp.stack(pieces[-1])))]
        *first_cut, own = call(
            functools.partial(rest_kernel, dims),
            [*cut_shapes, pltpu.VMEM((sectors, size, size), jnp.bfloat16)],
            (sector_shifts,),
            (
                acc,
                block,
                left[0],
                right[0],
                *[piece for both in pieces[1:] for piece in both],
                *[halos[h] for h in halos_at(0, sectors)],
            ),
            scratch=[square, pltpu.VMEM((2, size, size), jnp.bfloat16)],
            flops=terms * pair_flops // 2,
        )
        cuts = [first_cut]
        for turn in turns[1:]:
            sums.append(sector_sums(turn, after_all(own, *first_cut)))
        own = after_all(own, *sums)
        for turn in turns[1:]:
            cuts.append(
                call(
                    functools.partial(full_kernel, dims, turn),
                    cut_shapes,
                    (sector_shifts,),
                    (own, left[turn], right[turn], *[halos[h] for h in halos_at(turn, sectors)]),
                    scratch=[square, pltpu.VMEM((2, size, size), jnp.bfloat16)],
                    flops=terms * pair_flops,
                )
            )
        totals = [low_sum(*c) for c in cuts]

    with jax.named_scope("scalars"):
        parts = [high_parts(total) for total in totals]
        sums = after_all(sum(sums), totals[-1], parts[0][-1])
        tables, reach = [sums], 1
        while reach < groups:
            if groups & (groups - 1):
                tables, reach = [lax.psum(sums, "sector")], groups
            else:
                sums, width = sum(tables), min(4, groups // reach)
                tables = [sums] + [
                    lax.ppermute(sums, "sector", [(i, i ^ (reach * k)) for i in range(groups)])
                    for k in range(1, width)
                ]
                reach *= width
        out = jax.ShapeDtypeStruct((sectors, span, size), jnp.float32)
        flat = [part for each in parts for part in each]
        return call(
            functools.partial(finish_kernel, dims, cells, scale),
            [out, out],
            (sector_sizes,),
            (start, *shifted, *plus, *minus, *flat, *tables),
        )


def solution(mesh):
    return jax.shard_map(
        on_device,
        mesh=mesh,
        in_specs=(
            P("sector", None, None),
            P("sector", "term", None, None),
            P("sector", "term", None, None),
            P("sector", None),
            P("sector", None),
            P("term"),
            P("sector"),
        ),
        out_specs=(P("sector", "term", None), P("sector", "term", None)),
        check_vma=False,
    )
```

```python
import functools
import jax
import jax.numpy as jnp
from jax import lax
from jax.experimental import pallas as pl
from jax.experimental.pallas import tpu as pltpu
from jax.sharding import PartitionSpec as P

epsilon = 1e-06
NT = (((1,), (1,)), ((), ()))
GUESS = 4.5


def other(hi, step, count):
    return hi ^ step if count & (count - 1) == 0 else (step - hi) % count


def traced_other(hi, step, count):
    return hi ^ step if count & (count - 1) == 0 else lax.rem(step - hi + count, count)


def pairs_low(size):
    return [(i, i ^ 1) for i in range(size)]


def pairs_high(size, low, step):
    count = size // low
    return [(i, other(i // low, step, count) * low + i % low) for i in range(size)]


def row_finder(count, low, span):
    rank = lax.axis_index("term")
    hi, lo = rank // low, lax.rem(rank, low)

    def row_of(step, far):
        digit = 1 - lo if far else lo
        return pl.multiple_of((traced_other(hi, step, count) * low + digit) * span, span)

    return row_of


def add_pair(acc, left, right, block):
    mixed = jnp.dot(left[...], block[...], preferred_element_type=jnp.float32)
    acc[...] += lax.dot_general(
        mixed.astype(jnp.bfloat16), right[...], NT, preferred_element_type=jnp.float32
    )


def sector_at(turn, sectors):
    odd = lax.rem(lax.axis_index("sector"), 2)
    return odd * turn + (1 - odd) * (sectors - 1 - turn)


def halos_at(turn, sectors):
    return ([0] if turn == 0 else []) + ([1] if turn == sectors - 1 else [])


def halo_side(halo):
    here, groups = lax.axis_index("sector"), lax.axis_size("sector")
    side = (1 - 2 * lax.rem(here, 2)) * (1 - 2 * halo)
    return side, (here + side >= 0) & (here + side < groups)


def add_pairs(dims, turn, shift_ref, acc, left, right, own, halos, arrived=None, skip_own=False):
    sectors, terms = dims[:2]
    s = sector_at(turn, sectors)
    for t in range(terms):
        if arrived is not None:
            arrived(t)
        partner = s + shift_ref[t]
        inside = (partner >= 0) & (partner < sectors)
        if skip_own:
            inside &= shift_ref[t] != 0

        @pl.when(inside)
        def _():
            add_pair(acc, left.at[t], right.at[t], own.at[partner])

        for block, halo in zip(halos, halos_at(turn, sectors)):
            side, there = halo_side(halo)

            @pl.when((shift_ref[t] == side) & there)
            def _():
                add_pair(acc, left.at[t], right.at[t], block)


def place_rows(dims, wb, pieces):
    sectors, terms, size, count, low, span = dims
    row_of = row_finder(count, low, span)
    for far in range(low):
        for step in range(count):
            wb[pl.ds(row_of(step, far), span), :] = pieces[far][step]


def cut(dims, acc, send_ref, keep_ref):
    sectors, terms, size, count, low, span = dims
    row_of = row_finder(count, low, span)
    for step in range(count):
        if low > 1:
            send_ref[step] = acc[pl.ds(row_of(step, 1), span), :].astype(jnp.bfloat16)
        keep_ref[step] = acc[pl.ds(row_of(step, 0), span), :]


def live_tile(shape, first_row, limit):
    row = first_row + lax.broadcasted_iota(jnp.int32, shape, 0)
    return (row < limit) & (lax.broadcasted_iota(jnp.int32, shape, 1) < limit)


def energy_rows(left_row, right_row, s, first, span):
    shape = (span, left_row.shape[1])
    row = first + lax.broadcasted_iota(jnp.int32, shape, 0)
    here = row == lax.broadcasted_iota(jnp.int32, shape, 1)
    left = jnp.sum(jnp.where(here, left_row[pl.ds(s, 1), :], 0.0), axis=1, keepdims=True)
    return left + right_row[pl.ds(s, 1), :]


def round_kernel(size_hbm, vector_hbm, rounded, edge, other_edge, vector, sizes, sems):
    sectors, size = vector.shape[:2]
    parts = sems.shape[0] // sectors
    rows = size // parts
    tile = min(64, rows)
    limits = pltpu.make_async_copy(size_hbm, sizes, sems.at[sectors * parts])
    limits.start()
    copies = [
        pltpu.make_async_copy(
            vector_hbm.at[sector_at(turn, sectors), pl.ds(n * rows, rows), :],
            vector.at[turn, pl.ds(n * rows, rows), :],
            sems.at[turn * parts + n],
        )
        for turn in range(sectors)
        for n in range(parts)
    ]
    for copy in copies:
        copy.start()
    limits.wait()
    for turn in range(sectors):
        s = sector_at(turn, sectors)
        for n in range(parts):
            copies[turn * parts + n].wait()

            @pl.loop(0, rows // tile)
            def _(k):
                first = pl.multiple_of(n * rows + k * tile, tile)
                part = pl.ds(first, tile)
                live = live_tile((tile, size), first, sizes[s])
                value = jnp.where(live, vector[turn, part, :], 0.0).astype(jnp.bfloat16)
                rounded[s, part, :] = value
                if turn == 0:
                    edge[part, :] = value
                if turn == sectors - 1:
                    other_edge[part, :] = value


def load_kernel(dims, turn, own, *refs):
    sectors, terms, size, count, low, span = dims
    blocks, refs = refs[: len(halos_at(turn, sectors))], refs[len(halos_at(turn, sectors)) :]
    shift_hbm, size_hbm, left_hbm, right_hbm, vector_hbm, send_ref, keep_ref, left, right, *refs = refs
    start, refs = (refs[0], refs[1:]) if turn == 0 else (None, refs)
    acc, shift_ref, size_ref, sems, row_sems, scalar_sems = refs
    s = sector_at(turn, sectors)
    scalars = [
        pltpu.make_async_copy(shift_hbm, shift_ref, scalar_sems.at[0]),
        pltpu.make_async_copy(size_hbm, size_ref, scalar_sems.at[1]),
    ]
    copies = [
        [
            pltpu.make_async_copy(hbm.at[s, t], vmem.at[t], sems.at[k, t])
            for k, (hbm, vmem) in enumerate(((left_hbm, left), (right_hbm, right)))
        ]
        for t in range(terms)
    ]
    first = row_finder(count, low, span)(0, 0)
    rows = [
        pltpu.make_async_copy(vector_hbm.at[e, pl.ds(first, span), :], start.at[e], row_sems.at[e])
        for e in range(sectors if turn == 0 else 0)
    ]
    for copy in scalars:
        copy.start()
    for pair in copies:
        for copy in pair:
            copy.start()
    for copy in rows:
        copy.start()
    acc[...] = jnp.zeros_like(acc)
    for copy in scalars:
        copy.wait()

    def arrived(t):
        for copy in copies[t]:
            copy.wait()

    add_pairs(dims, turn, shift_ref, acc, left, right, own, blocks, arrived)
    cut(dims, acc, send_ref, keep_ref)
    for e, copy in enumerate(rows):
        copy.wait()
        live = live_tile((span, size), first, size_ref[e])
        start[e] = jnp.where(live, start[e], 0.0)


def self_kernel(dims, shift_ref, left, right, mine, theirs, acc, own):
    acc[...] = jnp.zeros_like(acc)
    place_rows(dims, own, [mine, theirs])
    for t in range(dims[1]):

        @pl.when(shift_ref[t] == 0)
        def _():
            add_pair(acc, left.at[t], right.at[t], own)


def rest_kernel(dims, shift_ref, acc_ref, first_block, left, right, *refs):
    sectors = dims[0]
    pieces, refs = refs[: 2 * sectors - 2], refs[2 * sectors - 2 :]
    halos, (send_ref, keep_ref, own, acc, wb) = refs[:-5], refs[-5:]
    acc[...] = acc_ref[...]
    own[sector_at(0, sectors)] = first_block[...]
    for turn in range(1, sectors):
        place_rows(dims, own.at[sector_at(turn, sectors)], pieces[2 * turn - 2 : 2 * turn])
    for n, halo in enumerate(halos):
        place_rows(dims, wb.at[n], [halo.at[0], halo.at[1]])
    blocks = [wb.at[n] for n in range(len(halos))]
    add_pairs(dims, 0, shift_ref, acc, left, right, own, blocks, skip_own=True)
    cut(dims, acc, send_ref, keep_ref)


def full_kernel(dims, turn, shift_ref, own, left, right, *refs):
    halos, (send_ref, keep_ref, acc, wb) = refs[:-4], refs[-4:]
    acc[...] = jnp.zeros_like(acc)
    for n, halo in enumerate(halos):
        place_rows(dims, wb.at[n], [halo.at[0], halo.at[1]])
    blocks = [wb.at[n] for n in range(len(halos))]
    add_pairs(dims, turn, shift_ref, acc, left, right, own, blocks)
    cut(dims, acc, send_ref, keep_ref)


def sums_kernel(dims, turn, size_ref, vector_ref, block, sums):
    size = dims[2]
    s = sector_at(turn, dims[0])
    sums[...] = jnp.zeros_like(sums)
    tile = min(64, size)

    @pl.loop(0, size // tile)
    def _(n):
        first = pl.multiple_of(n * tile, tile)
        rows = pl.ds(first, tile)
        live = live_tile((tile, size), first, size_ref[s])
        start = jnp.where(live, vector_ref[s, rows, :], 0.0)
        shifted = (block[rows, :] if turn == 0 else block[s, rows, :]).astype(jnp.float32)
        for k, term in enumerate((shifted * shifted, shifted * start, start * start)):
            sums[k : k + 1, :] += jnp.sum(term, 0, keepdims=True)


def shift_kernel(dims, turn, scale, size_ref, start, left_row, right_row, *refs):
    sectors, terms, size, count, low, span = dims
    parts, (held_ref, shifted_ref, plus_ref, minus_ref) = refs[:-4], refs[-4:]
    s = sector_at(turn, sectors)
    first = row_finder(count, low, span)(0, 0)
    total = parts[0][...]
    for part in parts[1:]:
        total += part[...].astype(jnp.float32)
    mixed = jnp.where(live_tile((span, size), first, size_ref[s]), scale * total, 0.0)
    energy = energy_rows(left_row, right_row, s, first, span)
    begin = start[s]
    shifted = mixed + (energy - GUESS) * begin
    held_ref[...] = shifted.astype(jnp.bfloat16)
    shifted_ref[...] = shifted
    plus_ref[...] = energy * shifted
    minus_ref[...] = energy * begin + mixed


def finish_kernel(dims, cells, scale, size_ref, start, *refs):
    sectors, terms, size, count, low, span = dims
    shifted, plus, minus = [refs[k * sectors : (k + 1) * sectors] for k in range(3)]
    parts, refs = refs[3 * sectors : 3 * sectors + count * sectors], refs[3 * sectors + count * sectors :]
    tables, (next_ref, sigma_ref) = refs[:-2], refs[-2:]
    first = row_finder(count, low, span)(0, 0)
    sums = sum(table[...] for table in tables)
    shifted_sq, overlap, norm_sq = [
        jnp.sum(sums[k : k + 1, :], axis=1, keepdims=True) for k in range(3)
    ]
    correlation = overlap + GUESS * norm_sq
    ritz = (correlation / cells) / (norm_sq / cells + epsilon)
    delta = ritz - GUESS
    res_sq = shifted_sq - 2.0 * delta * overlap + delta * delta * norm_sq
    inverse = lax.rsqrt(res_sq / cells + epsilon)
    for turn in range(sectors):
        s = sector_at(turn, sectors)
        next_ref[s] = (shifted[turn][...] - delta * start[s]) * inverse
        total = parts[turn * count][...]
        for part in parts[turn * count + 1 : (turn + 1) * count]:
            total += part[...].astype(jnp.float32)
        mixed = jnp.where(live_tile((span, size), first, size_ref[s]), scale * total, 0.0)
        sigma_ref[s] = (plus[turn][...] - delta * minus[turn][...] + mixed) * inverse


SMEM = pl.BlockSpec(memory_space=pltpu.SMEM)
VMEM = pl.BlockSpec(memory_space=pltpu.VMEM)
HBM = pl.BlockSpec(memory_space=pltpu.HBM)
LIMIT = pltpu.CompilerParams(vmem_limit_bytes=24 * 2**20)


def call(kernel, out_shape, scalars, arrays, matrices=(), scratch=(), flops=2**20):
    matrices = [pltpu.with_memory_space_constraint(m, pltpu.HBM) for m in matrices]
    return pl.pallas_call(
        kernel,
        out_shape=out_shape,
        in_specs=[SMEM] * len(scalars) + [VMEM] * len(arrays) + [HBM] * len(matrices),
        out_specs=[VMEM] * len(out_shape),
        scratch_shapes=scratch,
        compiler_params=LIMIT,
        cost_estimate=pl.CostEstimate(flops=flops, bytes_accessed=flops // 256, transcendentals=0),
    )(*scalars, *arrays, *matrices)


def after_all(value, *others):
    return lax.optimization_barrier((value, *others))[0]


def on_device(
    lanczos_vector, left_block, right_block, left_energy, right_energy, sector_shifts, sector_sizes
):
    sectors, size = lanczos_vector.shape[:2]
    terms, ranks = left_block.shape[1], lax.axis_size("term")
    groups = lax.axis_size("sector")
    scale = float(terms * ranks) ** (-0.5)
    cells = float(sectors * groups * size * size)
    span = size // ranks
    low = 2 if ranks % 2 == 0 else 1
    count = ranks // low
    dims = (sectors, terms, size, count, low, span)
    turns = range(sectors)
    pair_flops = 4 * size**3
    rows = pltpu.VMEM((sectors, span, size), jnp.float32)
    square = pltpu.VMEM((size, size), jnp.float32)
    square_low = pltpu.VMEM((size, size), jnp.bfloat16)
    cut_shapes = [jax.ShapeDtypeStruct((count, span, size), d) for d in (jnp.bfloat16, jnp.float32)]
    pairs = [
        [p for i in range(start, groups - 1, 2) for p in ((i, i + 1), (i + 1, i))]
        for start in range(2)
    ]

    def halo(edge, which):
        return lax.ppermute(edge, "sector", pairs[which]) if pairs[which] else edge

    def low_sum(send, keep):
        if low == 1:
            return keep
        return keep + lax.ppermute(send, "term", pairs_low(ranks)).astype(jnp.float32)

    hops = range(1, count)

    def high_parts(total):
        return [total[0]] + [
            lax.ppermute(total[k].astype(jnp.bfloat16), "term", pairs_high(ranks, low, k))
            for k in hops
        ]

    def gather_high(held):
        got = {k: lax.ppermute(held, "term", pairs_high(ranks, low, k)) for k in hops}
        return jnp.concatenate([held] + [got[k] for k in range(1, count)])

    with jax.named_scope("first"):
        parts = 2 if size % 256 == 0 else 1
        block = jax.ShapeDtypeStruct((size, size), jnp.bfloat16)
        rounded, *edges = call(
            round_kernel,
            [pltpu.VMEM(lanczos_vector.shape, jnp.bfloat16), block, block],
            (),
            (),
            (sector_sizes, lanczos_vector),
            [
                pltpu.VMEM(lanczos_vector.shape, jnp.float32),
                pltpu.SMEM((sectors,), jnp.int32),
                pltpu.SemaphoreType.DMA((sectors * parts + 1,)),
            ],
        )
        halos = [halo(edge, which) for which, edge in enumerate(edges)]
        matrices = pltpu.VMEM((terms, size, size), jnp.bfloat16)
        cuts, left, right = [], [None] * sectors, [None] * sectors
        for turn in turns:
            send, keep, left[turn], right[turn], *more = call(
                functools.partial(load_kernel, dims, turn),
                [*cut_shapes, matrices, matrices] + ([rows] if turn == 0 else []),
                (),
                (rounded, *[halos[h] for h in halos_at(turn, sectors)]),
                (sector_shifts, sector_sizes, left_block, right_block, lanczos_vector),
                [
                    square,
                    pltpu.SMEM((terms,), jnp.int32),
                    pltpu.SMEM((sectors,), jnp.int32),
                    pltpu.SemaphoreType.DMA((2, terms)),
                    pltpu.SemaphoreType.DMA((sectors,)),
                    pltpu.SemaphoreType.DMA((2,)),
                ],
                terms * pair_flops,
            )
            cuts.append((send, keep))
            start = more[0] if turn == 0 else start
        totals = [low_sum(*c) for c in cuts]

    with jax.named_scope("gather"):
        shifted, plus, minus, pieces = [[None] * sectors for _ in range(4)]
        row = pltpu.VMEM((span, size), jnp.float32)
        parts = [high_parts(total) for total in totals]
        for turn in turns:
            held, shifted[turn], plus[turn], minus[turn] = call(
                functools.partial(shift_kernel, dims, turn, scale),
                [jax.ShapeDtypeStruct((span, size), jnp.bfloat16), row, row, row],
                (sector_sizes,),
                (start, left_energy, right_energy, *parts[turn]),
            )
            mine = gather_high(held[None])
            theirs = lax.ppermute(mine, "term", pairs_low(ranks)) if low > 1 else mine
            pieces[turn] = [mine, theirs]
    def sector_sums(turn, block):
        return call(
            functools.partial(sums_kernel, dims, turn),
            [jax.ShapeDtypeStruct((8, size), jnp.float32)],
            (sector_sizes,),
            (lanczos_vector, block),
            flops=1,
        )[0]

    with jax.named_scope("second"):
        acc, block = call(
            functools.partial(self_kernel, dims),
            [square, square_low],
            (sector_shifts,),
            (left[0], right[0], *pieces[0]),
            flops=1,
        )
        sums = [sector_sums(0, block)]
        whole = after_all(jnp.stack(pieces[0]), pieces[-1][1], acc, sums[0])
        halos = [halo(edge, n) for n, edge in enumerate((whole, jnp.stack(pieces[-1])))]
        *first_cut, own = call(
            functools.partial(rest_kernel, dims),
            [*cut_shapes, pltpu.VMEM((sectors, size, size), jnp.bfloat16)],
            (sector_shifts,),
            (
                acc,
                block,
                left[0],
                right[0],
                *[piece for both in pieces[1:] for piece in both],
                *[halos[h] for h in halos_at(0, sectors)],
            ),
            scratch=[square, pltpu.VMEM((2, size, size), jnp.bfloat16)],
            flops=terms * pair_flops // 2,
        )
        cuts = [first_cut]
        for turn in turns[1:]:
            sums.append(sector_sums(turn, after_all(own, *first_cut)))
        own = after_all(own, *sums)
        for turn in turns[1:]:
            cuts.append(
                call(
                    functools.partial(full_kernel, dims, turn),
                    cut_shapes,
                    (sector_shifts,),
                    (own, left[turn], right[turn], *[halos[h] for h in halos_at(turn, sectors)]),
                    scratch=[square, pltpu.VMEM((2, size, size), jnp.bfloat16)],
                    flops=terms * pair_flops,
                )
            )
        totals = [low_sum(*c) for c in cuts]

    with jax.named_scope("scalars"):
        parts = [high_parts(total) for total in totals]
        sums = after_all(sum(sums), totals[-1], parts[0][min(1, count - 1)])
        tables, reach = [sums], 1
        while reach < groups:
            if groups & (groups - 1):
                tables, reach = [lax.psum(sums, "sector")], groups
            else:
                sums, width = sum(tables), min(4, groups // reach)
                tables = [sums] + [
                    lax.ppermute(sums, "sector", [(i, i ^ (reach * k)) for i in range(groups)])
                    for k in range(1, width)
                ]
                reach *= width
        out = jax.ShapeDtypeStruct((sectors, span, size), jnp.float32)
        flat = [part for each in parts for part in each]
        return call(
            functools.partial(finish_kernel, dims, cells, scale),
            [out, out],
            (sector_sizes,),
            (start, *shifted, *plus, *minus, *flat, *tables),
        )


def solution(mesh):
    return jax.shard_map(
        on_device,
        mesh=mesh,
        in_specs=(
            P("sector", None, None),
            P("sector", "term", None, None),
            P("sector", "term", None, None),
            P("sector", None),
            P("sector", None),
            P("term"),
            P("sector"),
        ),
        out_specs=(P("sector", "term", None), P("sector", "term", None)),
        check_vma=False,
    )
```

```python
import functools
import jax
import jax.numpy as jnp
from jax import lax
from jax.experimental import pallas as pl
from jax.experimental.pallas import tpu as pltpu
from jax.sharding import PartitionSpec as P

epsilon = 1e-06
NT = (((1,), (1,)), ((), ()))
GUESS = 4.5


def other(hi, step, count):
    return hi ^ step if count & (count - 1) == 0 else (step - hi) % count


def traced_other(hi, step, count):
    return hi ^ step if count & (count - 1) == 0 else lax.rem(step - hi + count, count)


def pairs_low(size):
    return [(i, i ^ 1) for i in range(size)]


def pairs_high(size, low, step):
    count = size // low
    return [(i, other(i // low, step, count) * low + i % low) for i in range(size)]


def row_finder(count, low, span):
    rank = lax.axis_index("term")
    hi, lo = rank // low, lax.rem(rank, low)

    def row_of(step, far):
        digit = 1 - lo if far else lo
        return pl.multiple_of((traced_other(hi, step, count) * low + digit) * span, span)

    return row_of


def add_pair(dims, far, acc, left, right, block):
    count, low, span = dims[3:]
    row_of = row_finder(count, low, span)
    rows = [left[pl.ds(row_of(step, far), span), :] for step in range(count)]
    mixed = jnp.dot(jnp.concatenate(rows), block[...], preferred_element_type=jnp.float32)
    acc[...] += lax.dot_general(
        mixed.astype(jnp.bfloat16), right[...], NT, preferred_element_type=jnp.float32
    )


def sector_at(turn, sectors):
    odd = lax.rem(lax.axis_index("sector"), 2)
    return odd * turn + (1 - odd) * (sectors - 1 - turn)


def halos_at(turn, sectors):
    return ([0] if turn == 0 else []) + ([1] if turn == sectors - 1 else [])


def halo_side(halo):
    here, groups = lax.axis_index("sector"), lax.axis_size("sector")
    side = (1 - 2 * lax.rem(here, 2)) * (1 - 2 * halo)
    return side, (here + side >= 0) & (here + side < groups)


def add_pairs(
    dims, turn, far, shift_ref, acc, left, right, own, halos, arrived=None, skip_own=False
):
    sectors, terms = dims[:2]
    s = sector_at(turn, sectors)
    for t in range(terms):
        if arrived is not None:
            arrived(t)
        partner = s + shift_ref[t]
        inside = (partner >= 0) & (partner < sectors)
        if skip_own:
            inside &= shift_ref[t] != 0

        @pl.when(inside)
        def _():
            add_pair(dims, far, acc, left.at[t], right.at[t], own.at[partner])

        for block, halo in zip(halos, halos_at(turn, sectors)):
            side, there = halo_side(halo)

            @pl.when((shift_ref[t] == side) & there)
            def _():
                add_pair(dims, far, acc, left.at[t], right.at[t], block)


def place_rows(dims, wb, pieces):
    sectors, terms, size, count, low, span = dims
    row_of = row_finder(count, low, span)
    for far in range(low):
        for step in range(count):
            wb[pl.ds(row_of(step, far), span), :] = pieces[far][step]


def live_tile(shape, first_row, limit):
    row = first_row + lax.broadcasted_iota(jnp.int32, shape, 0)
    return (row < limit) & (lax.broadcasted_iota(jnp.int32, shape, 1) < limit)


def energy_rows(left_row, right_row, s, first, span):
    shape = (span, left_row.shape[1])
    row = first + lax.broadcasted_iota(jnp.int32, shape, 0)
    here = row == lax.broadcasted_iota(jnp.int32, shape, 1)
    left = jnp.sum(jnp.where(here, left_row[pl.ds(s, 1), :], 0.0), axis=1, keepdims=True)
    return left + right_row[pl.ds(s, 1), :]


def round_kernel(size_hbm, vector_hbm, rounded, edge, other_edge, vector, sizes, sems):
    sectors, size = vector.shape[:2]
    parts = sems.shape[0] // sectors
    rows = size // parts
    tile = min(64, rows)
    limits = pltpu.make_async_copy(size_hbm, sizes, sems.at[sectors * parts])
    limits.start()
    copies = [
        pltpu.make_async_copy(
            vector_hbm.at[sector_at(turn, sectors), pl.ds(n * rows, rows), :],
            vector.at[turn, pl.ds(n * rows, rows), :],
            sems.at[turn * parts + n],
        )
        for turn in range(sectors)
        for n in range(parts)
    ]
    for copy in copies:
        copy.start()
    limits.wait()
    for turn in range(sectors):
        s = sector_at(turn, sectors)
        for n in range(parts):
            copies[turn * parts + n].wait()

            @pl.loop(0, rows // tile)
            def _(k):
                first = pl.multiple_of(n * rows + k * tile, tile)
                part = pl.ds(first, tile)
                live = live_tile((tile, size), first, sizes[s])
                value = jnp.where(live, vector[turn, part, :], 0.0).astype(jnp.bfloat16)
                rounded[s, part, :] = value
                if turn == 0:
                    edge[part, :] = value
                if turn == sectors - 1:
                    other_edge[part, :] = value


def load_kernel(dims, turn, own, *refs):
    sectors, terms, size, count, low, span = dims
    blocks, refs = refs[: len(halos_at(turn, sectors))], refs[len(halos_at(turn, sectors)) :]
    shift_hbm, size_hbm, left_hbm, right_hbm, vector_hbm, send_ref, left, right, *refs = refs
    start, refs = (refs[0], refs[1:]) if turn == 0 else (None, refs)
    acc, shift_ref, size_ref, sems, row_sems, scalar_sems = refs
    s = sector_at(turn, sectors)
    scalars = [
        pltpu.make_async_copy(shift_hbm, shift_ref, scalar_sems.at[0]),
        pltpu.make_async_copy(size_hbm, size_ref, scalar_sems.at[1]),
    ]
    copies = [
        [
            pltpu.make_async_copy(hbm.at[s, t], vmem.at[t], sems.at[k, t])
            for k, (hbm, vmem) in enumerate(((left_hbm, left), (right_hbm, right)))
        ]
        for t in range(terms)
    ]
    first = row_finder(count, low, span)(0, 0)
    rows = [
        pltpu.make_async_copy(vector_hbm.at[e, pl.ds(first, span), :], start.at[e], row_sems.at[e])
        for e in range(sectors if turn == 0 else 0)
    ]
    for copy in scalars:
        copy.start()
    for pair in copies[:2]:
        for copy in pair:
            copy.start()
    acc[...] = jnp.zeros_like(acc)
    for copy in scalars:
        copy.wait()

    def arrived(t):
        for copy in copies[t]:
            copy.wait()
        for pair in copies[t + 2 : t + 3]:
            for copy in pair:
                copy.start()
        if t == terms - 1:
            for copy in rows:
                copy.start()

    add_pairs(dims, turn, low - 1, shift_ref, acc, left, right, own, blocks, arrived)
    send_ref[...] = acc[...].astype(send_ref.dtype)
    for e, copy in enumerate(rows):
        copy.wait()
        live = live_tile((span, size), first, size_ref[e])
        start[e] = jnp.where(live, start[e], 0.0)


def keep_kernel(dims, turn, began, shift_ref, own, left, right, *refs):
    blocks, keep_ref = refs[: len(halos_at(turn, dims[0]))], refs[-1]
    keep_ref[...] = refs[-2][...] if began else jnp.zeros_like(keep_ref)
    add_pairs(dims, turn, 0, shift_ref, keep_ref, left, right, own, blocks, skip_own=began)


def self_kernel(dims, shift_ref, left, right, mine, theirs, own, *accs):
    place_rows(dims, own, [mine, theirs])
    for far, acc in enumerate(accs):
        acc[...] = jnp.zeros_like(acc)
        for t in range(dims[1]):

            @pl.when(shift_ref[t] == 0)
            def _():
                add_pair(dims, far, acc, left.at[t], right.at[t], own)


def send_kernel(dims, turn, shift_ref, left, right, *refs):
    sectors, low = dims[0], dims[4]
    refs, (acc,) = refs[:-1], refs[-1:]
    halos, refs = refs[: len(halos_at(turn, sectors))], refs[len(halos_at(turn, sectors)) :]
    if turn == 0:
        began, first_block, *pieces = refs[: 2 * sectors]
        send_ref, blocks, own = refs[2 * sectors :]
        acc[...] = began[...]
        own[sector_at(0, sectors)] = first_block[...]
        for n in range(1, sectors):
            place_rows(dims, own.at[sector_at(n, sectors)], pieces[2 * n - 2 : 2 * n])
    else:
        own, send_ref, blocks = refs
        acc[...] = jnp.zeros_like(acc)
    for n, halo in enumerate(halos):
        place_rows(dims, blocks.at[n], [halo.at[0], halo.at[1]])
    held = [blocks.at[n] for n in range(len(halos))]
    add_pairs(dims, turn, low - 1, shift_ref, acc, left, right, own, held, skip_own=turn == 0)
    send_ref[...] = acc[...].astype(send_ref.dtype)


def sums_kernel(dims, turn, size_ref, vector_ref, block, sums):
    size = dims[2]
    s = sector_at(turn, dims[0])
    sums[...] = jnp.zeros_like(sums)
    tile = min(64, size)

    @pl.loop(0, size // tile)
    def _(n):
        first = pl.multiple_of(n * tile, tile)
        rows = pl.ds(first, tile)
        live = live_tile((tile, size), first, size_ref[s])
        start = jnp.where(live, vector_ref[s, rows, :], 0.0)
        shifted = (block[rows, :] if turn == 0 else block[s, rows, :]).astype(jnp.float32)
        for k, term in enumerate((shifted * shifted, shifted * start, start * start)):
            sums[k : k + 1, :] += jnp.sum(term, 0, keepdims=True)


def shift_kernel(dims, turn, scale, size_ref, start, left_row, right_row, *refs):
    sectors, terms, size, count, low, span = dims
    parts, (held_ref, shifted_ref, plus_ref, minus_ref) = refs[:-4], refs[-4:]
    s = sector_at(turn, sectors)
    first = row_finder(count, low, span)(0, 0)
    total = parts[0][...]
    for part in parts[1:]:
        total += part[...].astype(jnp.float32)
    mixed = jnp.where(live_tile((span, size), first, size_ref[s]), scale * total, 0.0)
    energy = energy_rows(left_row, right_row, s, first, span)
    begin = start[s]
    shifted = mixed + (energy - GUESS) * begin
    held_ref[...] = shifted.astype(jnp.bfloat16)
    shifted_ref[...] = shifted
    plus_ref[...] = energy * shifted
    minus_ref[...] = energy * begin + mixed


def finish_kernel(dims, cells, scale, size_ref, start, *refs):
    sectors, terms, size, count, low, span = dims
    shifted, plus, minus = [refs[k * sectors : (k + 1) * sectors] for k in range(3)]
    parts, refs = refs[3 * sectors : 3 * sectors + count * sectors], refs[3 * sectors + count * sectors :]
    tables, (next_ref, sigma_ref) = refs[:-2], refs[-2:]
    first = row_finder(count, low, span)(0, 0)
    sums = sum(table[...] for table in tables)
    shifted_sq, overlap, norm_sq = [
        jnp.sum(sums[k : k + 1, :], axis=1, keepdims=True) for k in range(3)
    ]
    correlation = overlap + GUESS * norm_sq
    ritz = (correlation / cells) / (norm_sq / cells + epsilon)
    delta = ritz - GUESS
    res_sq = shifted_sq - 2.0 * delta * overlap + delta * delta * norm_sq
    inverse = lax.rsqrt(res_sq / cells + epsilon)
    for turn in range(sectors):
        s = sector_at(turn, sectors)
        next_ref[s] = (shifted[turn][...] - delta * start[s]) * inverse
        total = parts[turn * count][...]
        for part in parts[turn * count + 1 : (turn + 1) * count]:
            total += part[...].astype(jnp.float32)
        mixed = jnp.where(live_tile((span, size), first, size_ref[s]), scale * total, 0.0)
        sigma_ref[s] = (plus[turn][...] - delta * minus[turn][...] + mixed) * inverse


SMEM = pl.BlockSpec(memory_space=pltpu.SMEM)
VMEM = pl.BlockSpec(memory_space=pltpu.VMEM)
HBM = pl.BlockSpec(memory_space=pltpu.HBM)
LIMIT = pltpu.CompilerParams(vmem_limit_bytes=24 * 2**20)


def call(kernel, out_shape, scalars, arrays, matrices=(), scratch=(), flops=2**20):
    matrices = [pltpu.with_memory_space_constraint(m, pltpu.HBM) for m in matrices]
    return pl.pallas_call(
        kernel,
        out_shape=out_shape,
        in_specs=[SMEM] * len(scalars) + [VMEM] * len(arrays) + [HBM] * len(matrices),
        out_specs=[VMEM] * len(out_shape),
        scratch_shapes=scratch,
        compiler_params=LIMIT,
        cost_estimate=pl.CostEstimate(flops=flops, bytes_accessed=flops // 256, transcendentals=0),
    )(*scalars, *arrays, *matrices)


def after_all(value, *others):
    return lax.optimization_barrier((value, *others))[0]


def on_device(
    lanczos_vector, left_block, right_block, left_energy, right_energy, sector_shifts, sector_sizes
):
    sectors, size = lanczos_vector.shape[:2]
    terms, ranks = left_block.shape[1], lax.axis_size("term")
    groups = lax.axis_size("sector")
    scale = float(terms * ranks) ** (-0.5)
    cells = float(sectors * groups * size * size)
    span = size // ranks
    low = 2 if ranks % 2 == 0 else 1
    count = ranks // low
    dims = (sectors, terms, size, count, low, span)
    turns = range(sectors)
    pair_flops = 4 * size**3
    rows = pltpu.VMEM((sectors, span, size), jnp.float32)
    square = pltpu.VMEM((size, size), jnp.float32)
    square_low = pltpu.VMEM((size, size), jnp.bfloat16)
    part = pltpu.VMEM((count * span, size), jnp.float32)
    kept = jax.ShapeDtypeStruct((count * span, size), jnp.float32)
    sent = jax.ShapeDtypeStruct(kept.shape, jnp.bfloat16 if low > 1 else jnp.float32)
    pairs = [
        [p for i in range(start, groups - 1, 2) for p in ((i, i + 1), (i + 1, i))]
        for start in range(2)
    ]

    def halo(edge, which):
        return lax.ppermute(edge, "sector", pairs[which]) if pairs[which] else edge

    def low_sum(send, keep):
        total = send
        if low > 1:
            got = lax.ppermute(send, "term", pairs_low(ranks))
            arrived.append(got)
            total = keep + got.astype(jnp.float32)
        return total.reshape(count, span, size)

    arrived = []

    def keep_rows(turn, own, blocks, began=()):
        if low == 1:
            return None
        return call(
            functools.partial(keep_kernel, dims, turn, bool(began)),
            [kept],
            (sector_shifts,),
            (own, left[turn], right[turn], *blocks, *began),
            flops=terms * pair_flops // 2,
        )[0]

    hops = range(count - 1, 0, -1)

    def high_parts(total):
        return [total[0]] + [
            lax.ppermute(total[k].astype(jnp.bfloat16), "term", pairs_high(ranks, low, k))
            for k in hops
        ]

    def gather_high(held):
        got = {k: lax.ppermute(held, "term", pairs_high(ranks, low, k)) for k in hops}
        return jnp.concatenate([held] + [got[k] for k in range(1, count)])

    with jax.named_scope("first"):
        parts = 2 if size % 256 == 0 else 1
        block = jax.ShapeDtypeStruct((size, size), jnp.bfloat16)
        rounded, *edges = call(
            round_kernel,
            [pltpu.VMEM(lanczos_vector.shape, jnp.bfloat16), block, block],
            (),
            (),
            (sector_sizes, lanczos_vector),
            [
                pltpu.VMEM(lanczos_vector.shape, jnp.float32),
                pltpu.SMEM((sectors,), jnp.int32),
                pltpu.SemaphoreType.DMA((sectors * parts + 1,)),
            ],
        )
        halos = [halo(edge, which) for which, edge in enumerate(edges)]
        matrices = pltpu.VMEM((terms, size, size), jnp.bfloat16)
        cuts, totals, left, right = [], [], [None] * sectors, [None] * sectors
        for turn in turns:
            blocks = [halos[h] for h in halos_at(turn, sectors)]
            ahead = [c for c in cuts[-1:] if low > 1]
            send, left[turn], right[turn], *more = call(
                functools.partial(load_kernel, dims, turn),
                [sent, matrices, matrices] + ([rows] if turn == 0 else []),
                (),
                (after_all(rounded, *[keep for _, keep in ahead]), *blocks),
                (sector_shifts, sector_sizes, left_block, right_block, lanczos_vector),
                [
                    part,
                    pltpu.SMEM((terms,), jnp.int32),
                    pltpu.SMEM((sectors,), jnp.int32),
                    pltpu.SemaphoreType.DMA((2, terms)),
                    pltpu.SemaphoreType.DMA((sectors,)),
                    pltpu.SemaphoreType.DMA((2,)),
                ],
                terms * pair_flops // 2,
            )
            cuts.append((send, keep_rows(turn, after_all(rounded, *arrived[-1:]), blocks)))
            totals.append(low_sum(*cuts[-1]))
            start = more[0] if turn == 0 else start

    with jax.named_scope("gather"):
        shifted, plus, minus, pieces = [[None] * sectors for _ in range(4)]
        row = pltpu.VMEM((span, size), jnp.float32)
        parts = [high_parts(total) for total in totals]
        for turn in turns:
            held, shifted[turn], plus[turn], minus[turn] = call(
                functools.partial(shift_kernel, dims, turn, scale),
                [jax.ShapeDtypeStruct((span, size), jnp.bfloat16), row, row, row],
                (sector_sizes,),
                (start, left_energy, right_energy, *parts[turn]),
            )
            mine = gather_high(held[None])
            theirs = lax.ppermute(mine, "term", pairs_low(ranks)) if low > 1 else mine
            pieces[turn] = [mine, theirs]
    def sector_sums(turn, block):
        return call(
            functools.partial(sums_kernel, dims, turn),
            [jax.ShapeDtypeStruct((8, size), jnp.float32)],
            (sector_sizes,),
            (lanczos_vector, block),
            flops=1,
        )[0]

    with jax.named_scope("second"):
        block, *began = call(
            functools.partial(self_kernel, dims),
            [square_low] + [part] * low,
            (sector_shifts,),
            (left[0], right[0], *pieces[0]),
            flops=1,
        )
        sums = [sector_sums(0, block)]
        whole = after_all(jnp.stack(pieces[0]), pieces[-1][1], *began, sums[0])
        halos = [halo(edge, n) for n, edge in enumerate((whole, jnp.stack(pieces[-1])))]
        blocks = [halos[h] for h in halos_at(0, sectors)]
        placed = pltpu.VMEM((2, size, size), jnp.bfloat16)
        send, beside, own = call(
            functools.partial(send_kernel, dims, 0),
            [sent, placed, pltpu.VMEM((sectors, size, size), jnp.bfloat16)],
            (sector_shifts,),
            (
                left[0],
                right[0],
                *blocks,
                began[-1],
                block,
                *[piece for both in pieces[1:] for piece in both],
            ),
            scratch=[part],
            flops=terms * pair_flops // 4,
        )
        cuts = [(send, keep_rows(0, own, [beside[n] for n in range(len(blocks))], began[:1]))]
        for turn in turns[1:]:
            sums.append(sector_sums(turn, after_all(own, send)))
        totals = [low_sum(*cuts[0])]
        for turn in turns[1:]:
            if low > 1:
                own = after_all(own, *sums, cuts[-1][1])
            blocks = [halos[h] for h in halos_at(turn, sectors)]
            send, beside = call(
                functools.partial(send_kernel, dims, turn),
                [sent, placed],
                (sector_shifts,),
                (left[turn], right[turn], *blocks, own),
                scratch=[part],
                flops=terms * pair_flops // 2,
            )
            blocks = [beside[n] for n in range(len(blocks))]
            cuts.append((send, keep_rows(turn, after_all(own, *arrived[-1:]), blocks)))
            totals.append(low_sum(*cuts[-1]))

    with jax.named_scope("scalars"):
        parts = [high_parts(total) for total in totals]
        sums = after_all(sum(sums), totals[-1], parts[0][-1])
        tables, reach = [sums], 1
        while reach < groups:
            if groups & (groups - 1):
                tables, reach = [lax.psum(sums, "sector")], groups
            else:
                sums, width = sum(tables), min(4, groups // reach)
                tables = [sums] + [
                    lax.ppermute(sums, "sector", [(i, i ^ (reach * k)) for i in range(groups)])
                    for k in range(1, width)
                ]
                reach *= width
        out = jax.ShapeDtypeStruct((sectors, span, size), jnp.float32)
        flat = [part for each in parts for part in each]
        return call(
            functools.partial(finish_kernel, dims, cells, scale),
            [out, out],
            (sector_sizes,),
            (start, *shifted, *plus, *minus, *flat, *tables),
        )


def solution(mesh):
    return jax.shard_map(
        on_device,
        mesh=mesh,
        in_specs=(
            P("sector", None, None),
            P("sector", "term", None, None),
            P("sector", "term", None, None),
            P("sector", None),
            P("sector", None),
            P("term"),
            P("sector"),
        ),
        out_specs=(P("sector", "term", None), P("sector", "term", None)),
        check_vma=False,
    )
```

```python
import functools
import jax
import jax.numpy as jnp
from jax import lax
from jax.experimental import pallas as pl
from jax.experimental.pallas import tpu as pltpu
from jax.sharding import PartitionSpec as P

epsilon = 1e-06
NT = (((1,), (1,)), ((), ()))
GUESS = 4.5


def other(hi, step, count):
    return hi ^ step if count & (count - 1) == 0 else (step - hi) % count


def traced_other(hi, step, count):
    return hi ^ step if count & (count - 1) == 0 else lax.rem(step - hi + count, count)


def pairs_low(size):
    return [(i, i ^ 1) for i in range(size)]


def pairs_high(size, low, step):
    count = size // low
    return [(i, other(i // low, step, count) * low + i % low) for i in range(size)]


def row_finder(count, low, span):
    rank = lax.axis_index("term")
    hi, lo = rank // low, lax.rem(rank, low)

    def row_of(step, far):
        digit = 1 - lo if far else lo
        return pl.multiple_of((traced_other(hi, step, count) * low + digit) * span, span)

    return row_of


def add_pair(acc, left, right, block):
    mixed = jnp.dot(left[...], block[...], preferred_element_type=jnp.float32)
    acc[...] += lax.dot_general(
        mixed.astype(jnp.bfloat16), right[...], NT, preferred_element_type=jnp.float32
    )


def sector_at(turn, sectors):
    odd = lax.rem(lax.axis_index("sector"), 2)
    return odd * turn + (1 - odd) * (sectors - 1 - turn)


def halos_at(turn, sectors):
    return ([0] if turn == 0 else []) + ([1] if turn == sectors - 1 else [])


def halo_side(halo):
    here, groups = lax.axis_index("sector"), lax.axis_size("sector")
    side = (1 - 2 * lax.rem(here, 2)) * (1 - 2 * halo)
    return side, (here + side >= 0) & (here + side < groups)


def add_pairs(dims, turn, shift_ref, acc, left, right, own, halos, arrived=None, skip_own=False):
    sectors, terms = dims[:2]
    s = sector_at(turn, sectors)
    for t in range(terms):
        if arrived is not None:
            arrived(t)
        partner = s + shift_ref[t]
        inside = (partner >= 0) & (partner < sectors)
        if skip_own:
            inside &= shift_ref[t] != 0

        @pl.when(inside)
        def _():
            add_pair(acc, left.at[t], right.at[t], own.at[partner])

        for block, halo in zip(halos, halos_at(turn, sectors)):
            side, there = halo_side(halo)

            @pl.when((shift_ref[t] == side) & there)
            def _():
                add_pair(acc, left.at[t], right.at[t], block)


def place_rows(dims, wb, pieces):
    sectors, terms, size, count, low, span = dims
    row_of = row_finder(count, low, span)
    for far in range(low):
        for step in range(count):
            wb[pl.ds(row_of(step, far), span), :] = pieces[far][step]


def cut(dims, acc, send_ref, keep_ref):
    sectors, terms, size, count, low, span = dims
    row_of = row_finder(count, low, span)
    for step in range(count):
        if low > 1:
            send_ref[step] = acc[pl.ds(row_of(step, 1), span), :].astype(jnp.bfloat16)
        keep_ref[step] = acc[pl.ds(row_of(step, 0), span), :]


def live_tile(shape, first_row, limit):
    row = first_row + lax.broadcasted_iota(jnp.int32, shape, 0)
    return (row < limit) & (lax.broadcasted_iota(jnp.int32, shape, 1) < limit)


def energy_rows(left_row, right_row, s, first, span):
    shape = (span, left_row.shape[1])
    row = first + lax.broadcasted_iota(jnp.int32, shape, 0)
    here = row == lax.broadcasted_iota(jnp.int32, shape, 1)
    left = jnp.sum(jnp.where(here, left_row[pl.ds(s, 1), :], 0.0), axis=1, keepdims=True)
    return left + right_row[pl.ds(s, 1), :]


def round_kernel(size_hbm, vector_hbm, rounded, edge, other_edge, vector, sizes, sems):
    sectors, size = vector.shape[:2]
    parts = sems.shape[0] // sectors
    rows = size // parts
    tile = min(64, rows)
    limits = pltpu.make_async_copy(size_hbm, sizes, sems.at[sectors * parts])
    limits.start()
    copies = [
        pltpu.make_async_copy(
            vector_hbm.at[sector_at(turn, sectors), pl.ds(n * rows, rows), :],
            vector.at[turn, pl.ds(n * rows, rows), :],
            sems.at[turn * parts + n],
        )
        for turn in range(sectors)
        for n in range(parts)
    ]
    for copy in copies:
        copy.start()
    limits.wait()
    for turn in range(sectors):
        s = sector_at(turn, sectors)
        for n in range(parts):
            copies[turn * parts + n].wait()

            @pl.loop(0, rows // tile)
            def _(k):
                first = pl.multiple_of(n * rows + k * tile, tile)
                part = pl.ds(first, tile)
                live = live_tile((tile, size), first, sizes[s])
                value = jnp.where(live, vector[turn, part, :], 0.0).astype(jnp.bfloat16)
                rounded[s, part, :] = value
                if turn == 0:
                    edge[part, :] = value
                if turn == sectors - 1:
                    other_edge[part, :] = value


def load_kernel(dims, turn, own, *refs):
    sectors, terms, size, count, low, span = dims
    blocks, refs = refs[: len(halos_at(turn, sectors))], refs[len(halos_at(turn, sectors)) :]
    shift_hbm, size_hbm, left_hbm, right_hbm, vector_hbm, send_ref, keep_ref, left, right, *refs = refs
    start, refs = (refs[0], refs[1:]) if turn == 0 else (None, refs)
    acc, shift_ref, size_ref, sems, row_sems, scalar_sems = refs
    s = sector_at(turn, sectors)
    scalars = [
        pltpu.make_async_copy(shift_hbm, shift_ref, scalar_sems.at[0]),
        pltpu.make_async_copy(size_hbm, size_ref, scalar_sems.at[1]),
    ]
    copies = [
        [
            pltpu.make_async_copy(hbm.at[s, t], vmem.at[t], sems.at[k, t])
            for k, (hbm, vmem) in enumerate(((left_hbm, left), (right_hbm, right)))
        ]
        for t in range(terms)
    ]
    first = row_finder(count, low, span)(0, 0)
    rows = [
        pltpu.make_async_copy(vector_hbm.at[e, pl.ds(first, span), :], start.at[e], row_sems.at[e])
        for e in range(sectors if turn == 0 else 0)
    ]
    for copy in scalars:
        copy.start()
    for pair in copies:
        for copy in pair:
            copy.start()
    for copy in rows:
        copy.start()
    acc[...] = jnp.zeros_like(acc)
    for copy in scalars:
        copy.wait()

    def arrived(t):
        for copy in copies[t]:
            copy.wait()

    add_pairs(dims, turn, shift_ref, acc, left, right, own, blocks, arrived)
    cut(dims, acc, send_ref, keep_ref)
    for e, copy in enumerate(rows):
        copy.wait()
        live = live_tile((span, size), first, size_ref[e])
        start[e] = jnp.where(live, start[e], 0.0)


def self_kernel(dims, shift_ref, left, right, mine, theirs, acc, own):
    acc[...] = jnp.zeros_like(acc)
    place_rows(dims, own, [mine, theirs])
    for t in range(dims[1]):

        @pl.when(shift_ref[t] == 0)
        def _():
            add_pair(acc, left.at[t], right.at[t], own)


def rest_kernel(dims, shift_ref, acc_ref, first_block, left, right, *refs):
    sectors = dims[0]
    pieces, refs = refs[: 2 * sectors - 2], refs[2 * sectors - 2 :]
    halos, (send_ref, keep_ref, own, acc, wb) = refs[:-5], refs[-5:]
    acc[...] = acc_ref[...]
    own[sector_at(0, sectors)] = first_block[...]
    for turn in range(1, sectors):
        place_rows(dims, own.at[sector_at(turn, sectors)], pieces[2 * turn - 2 : 2 * turn])
    for n, halo in enumerate(halos):
        place_rows(dims, wb.at[n], [halo.at[0], halo.at[1]])
    blocks = [wb.at[n] for n in range(len(halos))]
    add_pairs(dims, 0, shift_ref, acc, left, right, own, blocks, skip_own=True)
    cut(dims, acc, send_ref, keep_ref)


def full_kernel(dims, turn, shift_ref, own, left, right, *refs):
    halos, (send_ref, keep_ref, acc, wb) = refs[:-4], refs[-4:]
    acc[...] = jnp.zeros_like(acc)
    for n, halo in enumerate(halos):
        place_rows(dims, wb.at[n], [halo.at[0], halo.at[1]])
    blocks = [wb.at[n] for n in range(len(halos))]
    add_pairs(dims, turn, shift_ref, acc, left, right, own, blocks)
    cut(dims, acc, send_ref, keep_ref)


def sums_kernel(dims, turn, size_ref, vector_ref, block, sums):
    size = dims[2]
    s = sector_at(turn, dims[0])
    sums[...] = jnp.zeros_like(sums)
    tile = min(64, size)

    @pl.loop(0, size // tile)
    def _(n):
        first = pl.multiple_of(n * tile, tile)
        rows = pl.ds(first, tile)
        live = live_tile((tile, size), first, size_ref[s])
        start = jnp.where(live, vector_ref[s, rows, :], 0.0)
        shifted = (block[rows, :] if turn == 0 else block[s, rows, :]).astype(jnp.float32)
        for k, term in enumerate((shifted * shifted, shifted * start, start * start)):
            sums[k : k + 1, :] += jnp.sum(term, 0, keepdims=True)


def shift_kernel(dims, turn, scale, size_ref, start, left_row, right_row, *refs):
    sectors, terms, size, count, low, span = dims
    parts, (held_ref, shifted_ref, plus_ref, minus_ref) = refs[:-4], refs[-4:]
    s = sector_at(turn, sectors)
    first = row_finder(count, low, span)(0, 0)
    total = parts[0][...]
    for part in parts[1:]:
        total += part[...].astype(jnp.float32)
    mixed = jnp.where(live_tile((span, size), first, size_ref[s]), scale * total, 0.0)
    energy = energy_rows(left_row, right_row, s, first, span)
    begin = start[s]
    shifted = mixed + (energy - GUESS) * begin
    held_ref[...] = shifted.astype(jnp.bfloat16)
    shifted_ref[...] = shifted
    plus_ref[...] = energy * shifted
    minus_ref[...] = energy * begin + mixed


def finish_kernel(dims, cells, scale, size_ref, start, *refs):
    sectors, terms, size, count, low, span = dims
    shifted, plus, minus = [refs[k * sectors : (k + 1) * sectors] for k in range(3)]
    totals, refs = refs[3 * sectors : 4 * sectors], refs[4 * sectors :]
    tables, (next_ref, sigma_ref) = refs[:-2], refs[-2:]
    first = row_finder(count, low, span)(0, 0)
    sums = sum(table[...] for table in tables)
    shifted_sq, overlap, norm_sq = [
        jnp.sum(sums[k : k + 1, :], axis=1, keepdims=True) for k in range(3)
    ]
    correlation = overlap + GUESS * norm_sq
    ritz = (correlation / cells) / (norm_sq / cells + epsilon)
    delta = ritz - GUESS
    res_sq = shifted_sq - 2.0 * delta * overlap + delta * delta * norm_sq
    inverse = lax.rsqrt(res_sq / cells + epsilon)
    for turn in range(sectors):
        s = sector_at(turn, sectors)
        next_ref[s] = (shifted[turn][...] - delta * start[s]) * inverse
        mixed = jnp.where(live_tile((span, size), first, size_ref[s]), scale * totals[turn][...], 0.0)
        sigma_ref[s] = (plus[turn][...] - delta * minus[turn][...] + mixed) * inverse


SMEM = pl.BlockSpec(memory_space=pltpu.SMEM)
VMEM = pl.BlockSpec(memory_space=pltpu.VMEM)
HBM = pl.BlockSpec(memory_space=pltpu.HBM)
LIMIT = pltpu.CompilerParams(vmem_limit_bytes=24 * 2**20)


def call(kernel, out_shape, scalars, arrays, matrices=(), scratch=(), flops=2**20):
    matrices = [pltpu.with_memory_space_constraint(m, pltpu.HBM) for m in matrices]
    return pl.pallas_call(
        kernel,
        out_shape=out_shape,
        in_specs=[SMEM] * len(scalars) + [VMEM] * len(arrays) + [HBM] * len(matrices),
        out_specs=[VMEM] * len(out_shape),
        scratch_shapes=scratch,
        compiler_params=LIMIT,
        cost_estimate=pl.CostEstimate(flops=flops, bytes_accessed=flops // 256, transcendentals=0),
    )(*scalars, *arrays, *matrices)


def after_all(value, *others):
    return lax.optimization_barrier((value, *others))[0]


def on_device(
    lanczos_vector, left_block, right_block, left_energy, right_energy, sector_shifts, sector_sizes
):
    sectors, size = lanczos_vector.shape[:2]
    terms, ranks = left_block.shape[1], lax.axis_size("term")
    groups = lax.axis_size("sector")
    scale = float(terms * ranks) ** (-0.5)
    cells = float(sectors * groups * size * size)
    span = size // ranks
    low = 2 if ranks % 2 == 0 else 1
    count = ranks // low
    dims = (sectors, terms, size, count, low, span)
    turns = range(sectors)
    pair_flops = 4 * size**3
    rows = pltpu.VMEM((sectors, span, size), jnp.float32)
    square = pltpu.VMEM((size, size), jnp.float32)
    square_low = pltpu.VMEM((size, size), jnp.bfloat16)
    cut_shapes = [jax.ShapeDtypeStruct((count, span, size), d) for d in (jnp.bfloat16, jnp.float32)]
    pairs = [
        [p for i in range(start, groups - 1, 2) for p in ((i, i + 1), (i + 1, i))]
        for start in range(2)
    ]

    def halo(edge, which):
        return lax.ppermute(edge, "sector", pairs[which]) if pairs[which] else edge

    received = []

    def low_sum(send, keep):
        received.append(send)
        if low == 1:
            return keep
        received.append(lax.ppermute(send, "term", pairs_low(ranks)))
        return keep + received[-1].astype(jnp.float32)

    hops = range(count - 1, 0, -1)

    def high_parts(total):
        return [total[0]] + [
            lax.ppermute(total[k].astype(jnp.bfloat16), "term", pairs_high(ranks, low, k))
            for k in hops
        ]

    def gather_high(held):
        got = {k: lax.ppermute(held, "term", pairs_high(ranks, low, k)) for k in hops}
        return jnp.concatenate([held] + [got[k] for k in range(1, count)])

    with jax.named_scope("first"):
        parts = 2 if size % 256 == 0 else 1
        block = jax.ShapeDtypeStruct((size, size), jnp.bfloat16)
        rounded, *edges = call(
            round_kernel,
            [pltpu.VMEM(lanczos_vector.shape, jnp.bfloat16), block, block],
            (),
            (),
            (sector_sizes, lanczos_vector),
            [
                pltpu.VMEM(lanczos_vector.shape, jnp.float32),
                pltpu.SMEM((sectors,), jnp.int32),
                pltpu.SemaphoreType.DMA((sectors * parts + 1,)),
            ],
        )
        halos = [halo(edge, which) for which, edge in enumerate(edges)]
        matrices = pltpu.VMEM((terms, size, size), jnp.bfloat16)
        cuts, left, right = [], [None] * sectors, [None] * sectors
        for turn in turns:
            send, keep, left[turn], right[turn], *more = call(
                functools.partial(load_kernel, dims, turn),
                [*cut_shapes, matrices, matrices] + ([rows] if turn == 0 else []),
                (),
                (
                    after_all(rounded, *[send for send, _ in cuts[-1:]]),
                    *[halos[h] for h in halos_at(turn, sectors)],
                ),
                (sector_shifts, sector_sizes, left_block, right_block, lanczos_vector),
                [
                    square,
                    pltpu.SMEM((terms,), jnp.int32),
                    pltpu.SMEM((sectors,), jnp.int32),
                    pltpu.SemaphoreType.DMA((2, terms)),
                    pltpu.SemaphoreType.DMA((sectors,)),
                    pltpu.SemaphoreType.DMA((2,)),
                ],
                terms * pair_flops,
            )
            cuts.append((send, keep))
            start = more[0] if turn == 0 else start
        totals = [low_sum(*c) for c in cuts]

    with jax.named_scope("gather"):
        shifted, plus, minus, pieces = [[None] * sectors for _ in range(4)]
        row = pltpu.VMEM((span, size), jnp.float32)
        parts = [high_parts(total) for total in totals]
        for turn in turns:
            held, shifted[turn], plus[turn], minus[turn] = call(
                functools.partial(shift_kernel, dims, turn, scale),
                [jax.ShapeDtypeStruct((span, size), jnp.bfloat16), row, row, row],
                (sector_sizes,),
                (start, left_energy, right_energy, *parts[turn]),
            )
            mine = theirs = gather_high(held[None])
            if low > 1:
                theirs = lax.ppermute(held, "term", pairs_low(ranks))[None]
                if count > 1:
                    late = lax.ppermute(mine[1:], "term", pairs_low(ranks))
                    theirs = jnp.concatenate([theirs, late])
            pieces[turn] = [mine, theirs]
    def sector_sums(turn, block):
        return call(
            functools.partial(sums_kernel, dims, turn),
            [jax.ShapeDtypeStruct((8, size), jnp.float32)],
            (sector_sizes,),
            (lanczos_vector, block),
            flops=1,
        )[0]

    with jax.named_scope("second"):
        acc, block = call(
            functools.partial(self_kernel, dims),
            [square, square_low],
            (sector_shifts,),
            (left[0], right[0], *pieces[0]),
            flops=1,
        )
        sums = [sector_sums(0, block)]
        whole = after_all(jnp.stack(pieces[0]), pieces[-1][1], acc, sums[0])
        halos = [halo(edge, n) for n, edge in enumerate((whole, jnp.stack(pieces[-1])))]
        *first_cut, own = call(
            functools.partial(rest_kernel, dims),
            [*cut_shapes, pltpu.VMEM((sectors, size, size), jnp.bfloat16)],
            (sector_shifts,),
            (
                acc,
                block,
                left[0],
                right[0],
                *[piece for both in pieces[1:] for piece in both],
                *[halos[h] for h in halos_at(0, sectors)],
            ),
            scratch=[square, pltpu.VMEM((2, size, size), jnp.bfloat16)],
            flops=terms * pair_flops // 2,
        )
        cuts = [first_cut]
        for turn in turns[1:]:
            sums.append(sector_sums(turn, after_all(own, *first_cut)))
        own = after_all(own, *sums)
        for turn in turns[1:]:
            cuts.append(
                call(
                    functools.partial(full_kernel, dims, turn),
                    cut_shapes,
                    (sector_shifts,),
                    (own, left[turn], right[turn], *[halos[h] for h in halos_at(turn, sectors)]),
                    scratch=[square, pltpu.VMEM((2, size, size), jnp.bfloat16)],
                    flops=terms * pair_flops,
                )
            )
        totals = [low_sum(*cuts[0])]
        for send, *kept_rows in cuts[1:]:
            totals.append(low_sum(after_all(send, received[-1]), *kept_rows))

    with jax.named_scope("scalars"):
        parts = [high_parts(total) for total in totals]
        sums = after_all(sum(sums), totals[-1], parts[0][-1])
        tables, reach = [sums], 1
        while reach < groups:
            if groups & (groups - 1):
                tables, reach = [lax.psum(sums, "sector")], groups
            else:
                sums, width = sum(tables), min(4, groups // reach)
                tables = [sums] + [
                    lax.ppermute(sums, "sector", [(i, i ^ (reach * k)) for i in range(groups)])
                    for k in range(1, width)
                ]
                reach *= width
        out = jax.ShapeDtypeStruct((sectors, span, size), jnp.float32)
        flat = [sum(part.astype(jnp.float32) for part in each) for each in parts]
        return call(
            functools.partial(finish_kernel, dims, cells, scale),
            [out, out],
            (sector_sizes,),
            (start, *shifted, *plus, *minus, *flat, *tables),
        )


def solution(mesh):
    return jax.shard_map(
        on_device,
        mesh=mesh,
        in_specs=(
            P("sector", None, None),
            P("sector", "term", None, None),
            P("sector", "term", None, None),
            P("sector", None),
            P("sector", None),
            P("term"),
            P("sector"),
        ),
        out_specs=(P("sector", "term", None), P("sector", "term", None)),
        check_vma=False,
    )
```

```python
import functools
import jax
import jax.numpy as jnp
from jax import lax
from jax.experimental import pallas as pl
from jax.experimental.pallas import tpu as pltpu
from jax.sharding import PartitionSpec as P

epsilon = 1e-06
NT = (((1,), (1,)), ((), ()))
GUESS = 4.5


def other(hi, step, count):
    return hi ^ step if count & (count - 1) == 0 else (step - hi) % count


def traced_other(hi, step, count):
    return hi ^ step if count & (count - 1) == 0 else lax.rem(step - hi + count, count)


def pairs_low(size):
    return [(i, i ^ 1) for i in range(size)]


def pairs_high(size, low, step):
    count = size // low
    return [(i, other(i // low, step, count) * low + i % low) for i in range(size)]


def row_finder(count, low, span):
    rank = lax.axis_index("term")
    hi, lo = rank // low, lax.rem(rank, low)

    def row_of(step, far):
        digit = 1 - lo if far else lo
        return pl.multiple_of((traced_other(hi, step, count) * low + digit) * span, span)

    return row_of


def add_pair(acc, left, right, block):
    mixed = jnp.dot(left[...], block[...], preferred_element_type=jnp.float32)
    acc[...] += lax.dot_general(
        mixed.astype(jnp.bfloat16), right[...], NT, preferred_element_type=jnp.float32
    )


def sector_at(turn, sectors):
    odd = lax.rem(lax.axis_index("sector"), 2)
    return odd * turn + (1 - odd) * (sectors - 1 - turn)


def halos_at(turn, sectors):
    return ([0] if turn == 0 else []) + ([1] if turn == sectors - 1 else [])


def halo_side(halo):
    here, groups = lax.axis_index("sector"), lax.axis_size("sector")
    side = (1 - 2 * lax.rem(here, 2)) * (1 - 2 * halo)
    return side, (here + side >= 0) & (here + side < groups)


def add_pairs(dims, turn, shift_ref, acc, left, right, own, halos, arrived=None, skip_own=False):
    sectors, terms = dims[:2]
    s = sector_at(turn, sectors)
    for t in range(terms):
        if arrived is not None:
            arrived(t)
        partner = s + shift_ref[t]
        inside = (partner >= 0) & (partner < sectors)
        if skip_own:
            inside &= shift_ref[t] != 0

        @pl.when(inside)
        def _():
            add_pair(acc, left.at[t], right.at[t], own.at[partner])

        for block, halo in zip(halos, halos_at(turn, sectors)):
            side, there = halo_side(halo)

            @pl.when((shift_ref[t] == side) & there)
            def _():
                add_pair(acc, left.at[t], right.at[t], block)


def place_rows(dims, wb, pieces):
    sectors, terms, size, count, low, span = dims
    row_of = row_finder(count, low, span)
    for far in range(low):
        for step in range(count):
            wb[pl.ds(row_of(step, far), span), :] = pieces[far][step]


def cut(dims, acc, send_ref, keep_ref):
    sectors, terms, size, count, low, span = dims
    row_of = row_finder(count, low, span)
    for step in range(count):
        if low > 1:
            send_ref[step] = acc[pl.ds(row_of(step, 1), span), :].astype(jnp.bfloat16)
        keep_ref[step] = acc[pl.ds(row_of(step, 0), span), :]


def place_halos(dims, turn, wb, refs):
    refs, blocks = list(refs), []
    for n, halo in enumerate(halos_at(turn, dims[0])):
        pieces = [refs.pop(0) for _ in range(halo + 1)]
        place_rows(dims, wb.at[n], pieces if halo else [pieces[0].at[0], pieces[0].at[1]])
        blocks.append(wb.at[n])
    return blocks


def live_tile(shape, first_row, limit):
    row = first_row + lax.broadcasted_iota(jnp.int32, shape, 0)
    return (row < limit) & (lax.broadcasted_iota(jnp.int32, shape, 1) < limit)


def energy_rows(left_row, right_row, s, first, span):
    shape = (span, left_row.shape[1])
    row = first + lax.broadcasted_iota(jnp.int32, shape, 0)
    here = row == lax.broadcasted_iota(jnp.int32, shape, 1)
    left = jnp.sum(jnp.where(here, left_row[pl.ds(s, 1), :], 0.0), axis=1, keepdims=True)
    return left + right_row[pl.ds(s, 1), :]


def round_kernel(size_hbm, vector_hbm, rounded, edge, upper, lower, vector, sizes, sems):
    sectors, size = vector.shape[:2]
    parts = sems.shape[0] // sectors
    rows = size // parts
    tile = min(64, rows)
    limits = pltpu.make_async_copy(size_hbm, sizes, sems.at[sectors * parts])
    limits.start()
    copies = [
        pltpu.make_async_copy(
            vector_hbm.at[sector_at(turn, sectors), pl.ds(n * rows, rows), :],
            vector.at[turn, pl.ds(n * rows, rows), :],
            sems.at[turn * parts + n],
        )
        for turn in range(sectors)
        for n in range(parts)
    ]
    for copy in copies:
        copy.start()
    limits.wait()
    for turn in range(sectors):
        s = sector_at(turn, sectors)
        for n in range(parts):
            copies[turn * parts + n].wait()

            @pl.loop(0, rows // tile)
            def _(k):
                first = pl.multiple_of(n * rows + k * tile, tile)
                part = pl.ds(first, tile)
                live = live_tile((tile, size), first, sizes[s])
                value = jnp.where(live, vector[turn, part, :], 0.0).astype(jnp.bfloat16)
                rounded[s, part, :] = value
                if turn == 0:
                    edge[part, :] = value
                if turn == sectors - 1:
                    if n < parts // 2:
                        upper[part, :] = value
                    else:
                        lower[pl.ds(first - size // 2, tile), :] = value


def load_kernel(dims, turn, own, *refs):
    sectors, terms, size, count, low, span = dims
    pieces = {h: h + 1 for h in halos_at(turn, sectors)}
    blocks, refs = refs[: sum(pieces.values())], refs[sum(pieces.values()) :]
    shift_hbm, size_hbm, left_hbm, right_hbm, vector_hbm, send_ref, keep_ref, left, right, *refs = refs
    start, refs = (refs[0], refs[1:]) if turn == 0 else (None, refs)
    acc, wb, shift_ref, size_ref, sems, row_sems, scalar_sems = refs
    s = sector_at(turn, sectors)
    scalars = [
        pltpu.make_async_copy(shift_hbm, shift_ref, scalar_sems.at[0]),
        pltpu.make_async_copy(size_hbm, size_ref, scalar_sems.at[1]),
    ]
    copies = [
        [
            pltpu.make_async_copy(hbm.at[s, t], vmem.at[t], sems.at[k, t])
            for k, (hbm, vmem) in enumerate(((left_hbm, left), (right_hbm, right)))
        ]
        for t in range(terms)
    ]
    first = row_finder(count, low, span)(0, 0)
    rows = [
        pltpu.make_async_copy(vector_hbm.at[e, pl.ds(first, span), :], start.at[e], row_sems.at[e])
        for e in range(sectors if turn == 0 else 0)
    ]
    for copy in scalars:
        copy.start()
    for pair in copies:
        for copy in pair:
            copy.start()
    for copy in rows:
        copy.start()
    acc[...] = jnp.zeros_like(acc)
    if 1 in pieces:
        for n, half in enumerate(blocks[-2:]):
            wb[pl.ds(n * (size // 2), size // 2), :] = half[...]
        blocks = [*blocks[:-2], wb]
    for copy in scalars:
        copy.wait()

    def arrived(t):
        for copy in copies[t]:
            copy.wait()

    add_pairs(dims, turn, shift_ref, acc, left, right, own, blocks, arrived)
    cut(dims, acc, send_ref, keep_ref)
    for e, copy in enumerate(rows):
        copy.wait()
        live = live_tile((span, size), first, size_ref[e])
        start[e] = jnp.where(live, start[e], 0.0)


def self_kernel(dims, shift_ref, left, right, mine, theirs, acc, own):
    acc[...] = jnp.zeros_like(acc)
    place_rows(dims, own, [mine, theirs])
    for t in range(dims[1]):

        @pl.when(shift_ref[t] == 0)
        def _():
            add_pair(acc, left.at[t], right.at[t], own)


def rest_kernel(dims, shift_ref, acc_ref, first_block, left, right, *refs):
    sectors = dims[0]
    pieces, refs = refs[: 2 * sectors - 2], refs[2 * sectors - 2 :]
    halos, (send_ref, keep_ref, own, acc, wb) = refs[:-5], refs[-5:]
    acc[...] = acc_ref[...]
    own[sector_at(0, sectors)] = first_block[...]
    for turn in range(1, sectors):
        place_rows(dims, own.at[sector_at(turn, sectors)], pieces[2 * turn - 2 : 2 * turn])
    blocks = place_halos(dims, 0, wb, halos)
    add_pairs(dims, 0, shift_ref, acc, left, right, own, blocks, skip_own=True)
    cut(dims, acc, send_ref, keep_ref)


def full_kernel(dims, turn, shift_ref, own, left, right, *refs):
    halos, (send_ref, keep_ref, acc, wb) = refs[:-4], refs[-4:]
    acc[...] = jnp.zeros_like(acc)
    blocks = place_halos(dims, turn, wb, halos)
    add_pairs(dims, turn, shift_ref, acc, left, right, own, blocks)
    cut(dims, acc, send_ref, keep_ref)


def sums_kernel(dims, turn, size_ref, vector_ref, block, sums):
    size = dims[2]
    s = sector_at(turn, dims[0])
    sums[...] = jnp.zeros_like(sums)
    tile = min(64, size)

    @pl.loop(0, size // tile)
    def _(n):
        first = pl.multiple_of(n * tile, tile)
        rows = pl.ds(first, tile)
        live = live_tile((tile, size), first, size_ref[s])
        start = jnp.where(live, vector_ref[s, rows, :], 0.0)
        shifted = (block[rows, :] if turn == 0 else block[s, rows, :]).astype(jnp.float32)
        for k, term in enumerate((shifted * shifted, shifted * start, start * start)):
            sums[k : k + 1, :] += jnp.sum(term, 0, keepdims=True)


def shift_kernel(dims, turn, scale, size_ref, start, left_row, right_row, *refs):
    sectors, terms, size, count, low, span = dims
    parts, (held_ref, shifted_ref, plus_ref, minus_ref) = refs[:-4], refs[-4:]
    s = sector_at(turn, sectors)
    first = row_finder(count, low, span)(0, 0)
    total = parts[0][...]
    for part in parts[1:]:
        total += part[...].astype(jnp.float32)
    mixed = jnp.where(live_tile((span, size), first, size_ref[s]), scale * total, 0.0)
    energy = energy_rows(left_row, right_row, s, first, span)
    begin = start[s]
    shifted = mixed + (energy - GUESS) * begin
    held_ref[...] = shifted.astype(jnp.bfloat16)
    shifted_ref[...] = shifted
    plus_ref[...] = energy * shifted
    minus_ref[...] = energy * begin + mixed


def finish_kernel(dims, cells, scale, size_ref, start, *refs):
    sectors, terms, size, count, low, span = dims
    shifted, plus, minus = [refs[k * sectors : (k + 1) * sectors] for k in range(3)]
    totals, refs = refs[3 * sectors : 4 * sectors], refs[4 * sectors :]
    tables, (next_ref, sigma_ref) = refs[:-2], refs[-2:]
    first = row_finder(count, low, span)(0, 0)
    sums = sum(table[...] for table in tables)
    shifted_sq, overlap, norm_sq = [
        jnp.sum(sums[k : k + 1, :], axis=1, keepdims=True) for k in range(3)
    ]
    correlation = overlap + GUESS * norm_sq
    ritz = (correlation / cells) / (norm_sq / cells + epsilon)
    delta = ritz - GUESS
    res_sq = shifted_sq - 2.0 * delta * overlap + delta * delta * norm_sq
    inverse = lax.rsqrt(res_sq / cells + epsilon)
    for turn in range(sectors):
        s = sector_at(turn, sectors)
        next_ref[s] = (shifted[turn][...] - delta * start[s]) * inverse
        mixed = jnp.where(live_tile((span, size), first, size_ref[s]), scale * totals[turn][...], 0.0)
        sigma_ref[s] = (plus[turn][...] - delta * minus[turn][...] + mixed) * inverse


SMEM = pl.BlockSpec(memory_space=pltpu.SMEM)
VMEM = pl.BlockSpec(memory_space=pltpu.VMEM)
HBM = pl.BlockSpec(memory_space=pltpu.HBM)
LIMIT = pltpu.CompilerParams(vmem_limit_bytes=24 * 2**20)


def call(kernel, out_shape, scalars, arrays, matrices=(), scratch=(), flops=2**20):
    matrices = [pltpu.with_memory_space_constraint(m, pltpu.HBM) for m in matrices]
    return pl.pallas_call(
        kernel,
        out_shape=out_shape,
        in_specs=[SMEM] * len(scalars) + [VMEM] * len(arrays) + [HBM] * len(matrices),
        out_specs=[VMEM] * len(out_shape),
        scratch_shapes=scratch,
        compiler_params=LIMIT,
        cost_estimate=pl.CostEstimate(flops=flops, bytes_accessed=flops // 256, transcendentals=0),
    )(*scalars, *arrays, *matrices)


def after_all(value, *others):
    return lax.optimization_barrier((value, *others))[0]


def on_device(
    lanczos_vector, left_block, right_block, left_energy, right_energy, sector_shifts, sector_sizes
):
    sectors, size = lanczos_vector.shape[:2]
    terms, ranks = left_block.shape[1], lax.axis_size("term")
    groups = lax.axis_size("sector")
    scale = float(terms * ranks) ** (-0.5)
    cells = float(sectors * groups * size * size)
    span = size // ranks
    low = 2 if ranks % 2 == 0 else 1
    count = ranks // low
    dims = (sectors, terms, size, count, low, span)
    turns = range(sectors)
    pair_flops = 4 * size**3
    rows = pltpu.VMEM((sectors, span, size), jnp.float32)
    square = pltpu.VMEM((size, size), jnp.float32)
    square_low = pltpu.VMEM((size, size), jnp.bfloat16)
    cut_shapes = [jax.ShapeDtypeStruct((count, span, size), d) for d in (jnp.bfloat16, jnp.float32)]
    pairs = [
        [p for i in range(start, groups - 1, 2) for p in ((i, i + 1), (i + 1, i))]
        for start in range(2)
    ]

    def halo(edge, which):
        return lax.ppermute(edge, "sector", pairs[which]) if pairs[which] else edge

    received = []

    def low_sum(send, keep):
        received.append(send)
        if low == 1:
            return keep
        received.append(lax.ppermute(send, "term", pairs_low(ranks)))
        return keep + received[-1].astype(jnp.float32)

    hops = range(count - 1, 0, -1)

    def high_parts(total):
        return [total[0]] + [
            lax.ppermute(total[k].astype(jnp.bfloat16), "term", pairs_high(ranks, low, k))
            for k in hops
        ]

    def gather_high(held):
        got = {k: lax.ppermute(held, "term", pairs_high(ranks, low, k)) for k in hops}
        return jnp.concatenate([held] + [got[k] for k in range(1, count)])

    with jax.named_scope("first"):
        parts = 2
        block = jax.ShapeDtypeStruct((size, size), jnp.bfloat16)
        half = jax.ShapeDtypeStruct((size // 2, size), jnp.bfloat16)
        rounded, edge, *halves = call(
            round_kernel,
            [pltpu.VMEM(lanczos_vector.shape, jnp.bfloat16), block, half, half],
            (),
            (),
            (sector_sizes, lanczos_vector),
            [
                pltpu.VMEM(lanczos_vector.shape, jnp.float32),
                pltpu.SMEM((sectors,), jnp.int32),
                pltpu.SemaphoreType.DMA((sectors * parts + 1,)),
            ],
        )
        halos = [[halo(edge, 0)], [halo(edge, 1) for edge in halves]]
        matrices = pltpu.VMEM((terms, size, size), jnp.bfloat16)
        cuts, left, right = [], [None] * sectors, [None] * sectors
        for turn in turns:
            send, keep, left[turn], right[turn], *more = call(
                functools.partial(load_kernel, dims, turn),
                [*cut_shapes, matrices, matrices] + ([rows] if turn == 0 else []),
                (),
                (
                    after_all(rounded, *[send for send, _ in cuts[-1:]]),
                    *[piece for h in halos_at(turn, sectors) for piece in halos[h]],
                ),
                (sector_shifts, sector_sizes, left_block, right_block, lanczos_vector),
                [
                    square,
                    square_low,
                    pltpu.SMEM((terms,), jnp.int32),
                    pltpu.SMEM((sectors,), jnp.int32),
                    pltpu.SemaphoreType.DMA((2, terms)),
                    pltpu.SemaphoreType.DMA((sectors,)),
                    pltpu.SemaphoreType.DMA((2,)),
                ],
                terms * pair_flops,
            )
            cuts.append((send, keep))
            start = more[0] if turn == 0 else start
        totals = [low_sum(*c) for c in cuts]

    with jax.named_scope("gather"):
        shifted, plus, minus, pieces = [[None] * sectors for _ in range(4)]
        row = pltpu.VMEM((span, size), jnp.float32)
        parts = [high_parts(total) for total in totals]
        for turn in turns:
            held, shifted[turn], plus[turn], minus[turn] = call(
                functools.partial(shift_kernel, dims, turn, scale),
                [jax.ShapeDtypeStruct((span, size), jnp.bfloat16), row, row, row],
                (sector_sizes,),
                (start, left_energy, right_energy, *parts[turn]),
            )
            mine = gather_high(held[None])
            theirs = lax.ppermute(mine, "term", pairs_low(ranks)) if low > 1 else mine
            pieces[turn] = [mine, theirs]
    def sector_sums(turn, block):
        return call(
            functools.partial(sums_kernel, dims, turn),
            [jax.ShapeDtypeStruct((8, size), jnp.float32)],
            (sector_sizes,),
            (lanczos_vector, block),
            flops=1,
        )[0]

    with jax.named_scope("second"):
        acc, block = call(
            functools.partial(self_kernel, dims),
            [square, square_low],
            (sector_shifts,),
            (left[0], right[0], *pieces[0]),
            flops=1,
        )
        sums = [sector_sums(0, block)]
        whole = after_all(jnp.stack(pieces[0]), pieces[-1][1], acc, sums[0])
        halos = [[halo(whole, 0)], [halo(piece, 1) for piece in pieces[-1]]]
        *first_cut, own = call(
            functools.partial(rest_kernel, dims),
            [*cut_shapes, pltpu.VMEM((sectors, size, size), jnp.bfloat16)],
            (sector_shifts,),
            (
                acc,
                block,
                left[0],
                right[0],
                *[piece for both in pieces[1:] for piece in both],
                *[piece for h in halos_at(0, sectors) for piece in halos[h]],
            ),
            scratch=[square, pltpu.VMEM((2, size, size), jnp.bfloat16)],
            flops=terms * pair_flops // 2,
        )
        cuts = [first_cut]
        for turn in turns[1:]:
            sums.append(sector_sums(turn, after_all(own, *first_cut)))
        own = after_all(own, *sums)
        for turn in turns[1:]:
            cuts.append(
                call(
                    functools.partial(full_kernel, dims, turn),
                    cut_shapes,
                    (sector_shifts,),
                    (
                        own,
                        left[turn],
                        right[turn],
                        *[piece for h in halos_at(turn, sectors) for piece in halos[h]],
                    ),
                    scratch=[square, pltpu.VMEM((2, size, size), jnp.bfloat16)],
                    flops=terms * pair_flops,
                )
            )
        totals = [low_sum(*cuts[0])]
        for send, *kept_rows in cuts[1:]:
            totals.append(low_sum(after_all(send, received[-1]), *kept_rows))

    with jax.named_scope("scalars"):
        parts = [high_parts(total) for total in totals]
        sums = after_all(sum(sums), totals[-1], parts[0][-1])
        tables, reach = [sums], 1
        while reach < groups:
            if groups & (groups - 1):
                tables, reach = [lax.psum(sums, "sector")], groups
            else:
                sums, width = sum(tables), min(4, groups // reach)
                tables = [sums] + [
                    lax.ppermute(sums, "sector", [(i, i ^ (reach * k)) for i in range(groups)])
                    for k in range(1, width)
                ]
                reach *= width
        out = jax.ShapeDtypeStruct((sectors, span, size), jnp.float32)
        flat = [sum(part.astype(jnp.float32) for part in each) for each in parts]
        return call(
            functools.partial(finish_kernel, dims, cells, scale),
            [out, out],
            (sector_sizes,),
            (start, *shifted, *plus, *minus, *flat, *tables),
        )


def solution(mesh):
    return jax.shard_map(
        on_device,
        mesh=mesh,
        in_specs=(
            P("sector", None, None),
            P("sector", "term", None, None),
            P("sector", "term", None, None),
            P("sector", None),
            P("sector", None),
            P("term"),
            P("sector"),
        ),
        out_specs=(P("sector", "term", None), P("sector", "term", None)),
        check_vma=False,
    )
```

```python
import functools
import jax
import jax.numpy as jnp
from jax import lax
from jax.experimental import pallas as pl
from jax.experimental.pallas import tpu as pltpu
from jax.sharding import PartitionSpec as P

epsilon = 1e-06
NT = (((1,), (1,)), ((), ()))
GUESS = 4.5


def other(hi, step, count):
    return hi ^ step if count & (count - 1) == 0 else (step - hi) % count


def traced_other(hi, step, count):
    return hi ^ step if count & (count - 1) == 0 else lax.rem(step - hi + count, count)


def pairs_low(size):
    return [(i, i ^ 1) for i in range(size)]


def pairs_high(size, low, step):
    count = size // low
    return [(i, other(i // low, step, count) * low + i % low) for i in range(size)]


def row_finder(count, low, span):
    rank = lax.axis_index("term")
    hi, lo = rank // low, lax.rem(rank, low)

    def row_of(step, far):
        digit = 1 - lo if far else lo
        return pl.multiple_of((traced_other(hi, step, count) * low + digit) * span, span)

    return row_of


def add_pair(acc, left, right, block):
    mixed = jnp.dot(left[...], block[...], preferred_element_type=jnp.float32)
    acc[...] += lax.dot_general(
        mixed.astype(jnp.bfloat16), right[...], NT, preferred_element_type=jnp.float32
    )


def sector_at(turn, sectors):
    odd = lax.rem(lax.axis_index("sector"), 2)
    return odd * turn + (1 - odd) * (sectors - 1 - turn)


def halos_at(turn, sectors):
    return ([0] if turn == 0 else []) + ([1] if turn == sectors - 1 else [])


def halo_side(halo):
    here, groups = lax.axis_index("sector"), lax.axis_size("sector")
    side = (1 - 2 * lax.rem(here, 2)) * (1 - 2 * halo)
    return side, (here + side >= 0) & (here + side < groups)


def add_pairs(dims, turn, shift_ref, acc, left, right, own, halos, arrived=None, skip_own=False):
    sectors, terms = dims[:2]
    s = sector_at(turn, sectors)
    for t in range(terms):
        if arrived is not None:
            arrived(t)
        partner = s + shift_ref[t]
        inside = (partner >= 0) & (partner < sectors)
        if skip_own:
            inside &= shift_ref[t] != 0

        @pl.when(inside)
        def _():
            add_pair(acc, left.at[t], right.at[t], own.at[partner])

        for block, halo in zip(halos, halos_at(turn, sectors)):
            side, there = halo_side(halo)

            @pl.when((shift_ref[t] == side) & there)
            def _():
                add_pair(acc, left.at[t], right.at[t], block)


def place_rows(dims, wb, pieces):
    sectors, terms, size, count, low, span = dims
    row_of = row_finder(count, low, span)
    for far in range(low):
        for step in range(count):
            wb[pl.ds(row_of(step, far), span), :] = pieces[far][step]


def cut(dims, acc, send_ref, keep_ref):
    sectors, terms, size, count, low, span = dims
    row_of = row_finder(count, low, span)
    for step in range(count):
        if low > 1:
            send_ref[step] = acc[pl.ds(row_of(step, 1), span), :].astype(jnp.bfloat16)
        keep_ref[step] = acc[pl.ds(row_of(step, 0), span), :]


def live_tile(shape, first_row, limit):
    row = first_row + lax.broadcasted_iota(jnp.int32, shape, 0)
    return (row < limit) & (lax.broadcasted_iota(jnp.int32, shape, 1) < limit)


def energy_rows(left_row, right_row, s, first, span):
    shape = (span, left_row.shape[1])
    row = first + lax.broadcasted_iota(jnp.int32, shape, 0)
    here = row == lax.broadcasted_iota(jnp.int32, shape, 1)
    left = jnp.sum(jnp.where(here, left_row[pl.ds(s, 1), :], 0.0), axis=1, keepdims=True)
    return left + right_row[pl.ds(s, 1), :]


def round_kernel(size_hbm, vector_hbm, rounded, edge, other_edge, vector, sizes, sems):
    sectors, size = vector.shape[:2]
    parts = sems.shape[0] // sectors
    rows = size // parts
    tile = min(64, rows)
    limits = pltpu.make_async_copy(size_hbm, sizes, sems.at[sectors * parts])
    limits.start()
    copies = [
        pltpu.make_async_copy(
            vector_hbm.at[sector_at(turn, sectors), pl.ds(n * rows, rows), :],
            vector.at[turn, pl.ds(n * rows, rows), :],
            sems.at[turn * parts + n],
        )
        for turn in range(sectors)
        for n in range(parts)
    ]
    for copy in copies:
        copy.start()
    limits.wait()
    for turn in range(sectors):
        s = sector_at(turn, sectors)
        for n in range(parts):
            copies[turn * parts + n].wait()

            @pl.loop(0, rows // tile)
            def _(k):
                first = pl.multiple_of(n * rows + k * tile, tile)
                part = pl.ds(first, tile)
                live = live_tile((tile, size), first, sizes[s])
                value = jnp.where(live, vector[turn, part, :], 0.0).astype(jnp.bfloat16)
                rounded[s, part, :] = value
                if turn == 0:
                    edge[part, :] = value
                if turn == sectors - 1:
                    other_edge[part, :] = value


def load_kernel(dims, turn, own, *refs):
    sectors, terms, size, count, low, span = dims
    blocks, refs = refs[: len(halos_at(turn, sectors))], refs[len(halos_at(turn, sectors)) :]
    shift_hbm, size_hbm, left_hbm, right_hbm, vector_hbm, send_ref, keep_ref, left, right, *refs = refs
    start, refs = (refs[0], refs[1:]) if turn == 0 else (None, refs)
    acc, shift_ref, size_ref, sems, row_sems, scalar_sems = refs
    s = sector_at(turn, sectors)
    scalars = [
        pltpu.make_async_copy(shift_hbm, shift_ref, scalar_sems.at[0]),
        pltpu.make_async_copy(size_hbm, size_ref, scalar_sems.at[1]),
    ]
    copies = [
        [
            pltpu.make_async_copy(hbm.at[s, t, part, :], vmem.at[t, part, :], sems.at[k, t, n])
            for k, (hbm, vmem) in enumerate(((left_hbm, left), (right_hbm, right)))
            for n, part in enumerate((pl.ds(0, size // 2), pl.ds(size // 2, size // 2)))
        ]
        for t in range(terms)
    ]
    first = row_finder(count, low, span)(0, 0)
    rows = [
        pltpu.make_async_copy(vector_hbm.at[e, pl.ds(first, span), :], start.at[e], row_sems.at[e])
        for e in range(sectors if turn == 0 else 0)
    ]
    for copy in scalars:
        copy.start()
    for pair in copies:
        for copy in pair:
            copy.start()
    for copy in rows:
        copy.start()
    acc[...] = jnp.zeros_like(acc)
    for copy in scalars:
        copy.wait()

    def arrived(t):
        for copy in copies[t]:
            copy.wait()

    add_pairs(dims, turn, shift_ref, acc, left, right, own, blocks, arrived)
    cut(dims, acc, send_ref, keep_ref)
    for e, copy in enumerate(rows):
        copy.wait()
        live = live_tile((span, size), first, size_ref[e])
        start[e] = jnp.where(live, start[e], 0.0)


def self_kernel(dims, shift_ref, left, right, mine, theirs, acc, own):
    acc[...] = jnp.zeros_like(acc)
    place_rows(dims, own, [mine, theirs])
    for t in range(dims[1]):

        @pl.when(shift_ref[t] == 0)
        def _():
            add_pair(acc, left.at[t], right.at[t], own)


def rest_kernel(dims, shift_ref, acc_ref, first_block, left, right, *refs):
    sectors = dims[0]
    pieces, refs = refs[: 2 * sectors - 2], refs[2 * sectors - 2 :]
    halos, (send_ref, keep_ref, own, acc, wb) = refs[:-5], refs[-5:]
    acc[...] = acc_ref[...]
    own[sector_at(0, sectors)] = first_block[...]
    for turn in range(1, sectors):
        place_rows(dims, own.at[sector_at(turn, sectors)], pieces[2 * turn - 2 : 2 * turn])
    for n, halo in enumerate(halos):
        place_rows(dims, wb.at[n], [halo.at[0], halo.at[1]])
    blocks = [wb.at[n] for n in range(len(halos))]
    add_pairs(dims, 0, shift_ref, acc, left, right, own, blocks, skip_own=True)
    cut(dims, acc, send_ref, keep_ref)


def full_kernel(dims, turn, shift_ref, own, left, right, *refs):
    halos, (send_ref, keep_ref, acc, wb) = refs[:-4], refs[-4:]
    acc[...] = jnp.zeros_like(acc)
    for n, halo in enumerate(halos):
        place_rows(dims, wb.at[n], [halo.at[0], halo.at[1]])
    blocks = [wb.at[n] for n in range(len(halos))]
    add_pairs(dims, turn, shift_ref, acc, left, right, own, blocks)
    cut(dims, acc, send_ref, keep_ref)


def sums_kernel(dims, turn, size_ref, vector_ref, block, sums):
    size = dims[2]
    s = sector_at(turn, dims[0])
    sums[...] = jnp.zeros_like(sums)
    tile = min(64, size)

    @pl.loop(0, size // tile)
    def _(n):
        first = pl.multiple_of(n * tile, tile)
        rows = pl.ds(first, tile)
        live = live_tile((tile, size), first, size_ref[s])
        start = jnp.where(live, vector_ref[s, rows, :], 0.0)
        shifted = (block[rows, :] if turn == 0 else block[s, rows, :]).astype(jnp.float32)
        for k, term in enumerate((shifted * shifted, shifted * start, start * start)):
            sums[k : k + 1, :] += jnp.sum(term, 0, keepdims=True)


def shift_kernel(dims, turn, scale, size_ref, start, left_row, right_row, *refs):
    sectors, terms, size, count, low, span = dims
    parts, (held_ref, shifted_ref, plus_ref, minus_ref) = refs[:-4], refs[-4:]
    s = sector_at(turn, sectors)
    first = row_finder(count, low, span)(0, 0)
    total = parts[0][...]
    for part in parts[1:]:
        total += part[...].astype(jnp.float32)
    mixed = jnp.where(live_tile((span, size), first, size_ref[s]), scale * total, 0.0)
    energy = energy_rows(left_row, right_row, s, first, span)
    begin = start[s]
    shifted = mixed + (energy - GUESS) * begin
    held_ref[...] = shifted.astype(jnp.bfloat16)
    shifted_ref[...] = shifted
    plus_ref[...] = energy * shifted
    minus_ref[...] = energy * begin + mixed


def finish_kernel(dims, cells, scale, size_ref, start, *refs):
    sectors, terms, size, count, low, span = dims
    shifted, plus, minus = [refs[k * sectors : (k + 1) * sectors] for k in range(3)]
    parts, refs = refs[3 * sectors : 3 * sectors + count * sectors], refs[3 * sectors + count * sectors :]
    tables, (next_ref, sigma_ref) = refs[:-2], refs[-2:]
    first = row_finder(count, low, span)(0, 0)
    sums = sum(table[...] for table in tables)
    shifted_sq, overlap, norm_sq = [
        jnp.sum(sums[k : k + 1, :], axis=1, keepdims=True) for k in range(3)
    ]
    correlation = overlap + GUESS * norm_sq
    ritz = (correlation / cells) / (norm_sq / cells + epsilon)
    delta = ritz - GUESS
    res_sq = shifted_sq - 2.0 * delta * overlap + delta * delta * norm_sq
    inverse = lax.rsqrt(res_sq / cells + epsilon)
    for turn in range(sectors):
        s = sector_at(turn, sectors)
        next_ref[s] = (shifted[turn][...] - delta * start[s]) * inverse
        total = parts[turn * count][...]
        for part in parts[turn * count + 1 : (turn + 1) * count]:
            total += part[...].astype(jnp.float32)
        mixed = jnp.where(live_tile((span, size), first, size_ref[s]), scale * total, 0.0)
        sigma_ref[s] = (plus[turn][...] - delta * minus[turn][...] + mixed) * inverse


SMEM = pl.BlockSpec(memory_space=pltpu.SMEM)
VMEM = pl.BlockSpec(memory_space=pltpu.VMEM)
HBM = pl.BlockSpec(memory_space=pltpu.HBM)
LIMIT = pltpu.CompilerParams(vmem_limit_bytes=24 * 2**20)


def call(kernel, out_shape, scalars, arrays, matrices=(), scratch=(), flops=2**20):
    matrices = [pltpu.with_memory_space_constraint(m, pltpu.HBM) for m in matrices]
    return pl.pallas_call(
        kernel,
        out_shape=out_shape,
        in_specs=[SMEM] * len(scalars) + [VMEM] * len(arrays) + [HBM] * len(matrices),
        out_specs=[VMEM] * len(out_shape),
        scratch_shapes=scratch,
        compiler_params=LIMIT,
        cost_estimate=pl.CostEstimate(flops=flops, bytes_accessed=flops // 256, transcendentals=0),
    )(*scalars, *arrays, *matrices)


def after_all(value, *others):
    return lax.optimization_barrier((value, *others))[0]


def on_device(
    lanczos_vector, left_block, right_block, left_energy, right_energy, sector_shifts, sector_sizes
):
    sectors, size = lanczos_vector.shape[:2]
    terms, ranks = left_block.shape[1], lax.axis_size("term")
    groups = lax.axis_size("sector")
    scale = float(terms * ranks) ** (-0.5)
    cells = float(sectors * groups * size * size)
    span = size // ranks
    low = 2 if ranks % 2 == 0 else 1
    count = ranks // low
    dims = (sectors, terms, size, count, low, span)
    turns = range(sectors)
    pair_flops = 4 * size**3
    rows = pltpu.VMEM((sectors, span, size), jnp.float32)
    square = pltpu.VMEM((size, size), jnp.float32)
    square_low = pltpu.VMEM((size, size), jnp.bfloat16)
    cut_shapes = [jax.ShapeDtypeStruct((count, span, size), d) for d in (jnp.bfloat16, jnp.float32)]
    pairs = [
        [p for i in range(start, groups - 1, 2) for p in ((i, i + 1), (i + 1, i))]
        for start in range(2)
    ]

    def halo(edge, which):
        return lax.ppermute(edge, "sector", pairs[which]) if pairs[which] else edge

    def low_sum(send, keep):
        if low == 1:
            return keep
        return keep + lax.ppermute(send, "term", pairs_low(ranks)).astype(jnp.float32)

    hops = range(count - 1, 0, -1)

    def high_parts(total):
        return [total[0]] + [
            lax.ppermute(total[k].astype(jnp.bfloat16), "term", pairs_high(ranks, low, k))
            for k in hops
        ]

    def gather_high(held):
        got = {k: lax.ppermute(held, "term", pairs_high(ranks, low, k)) for k in hops}
        return jnp.concatenate([held] + [got[k] for k in range(1, count)])

    with jax.named_scope("first"):
        parts = 2 if size % 256 == 0 else 1
        block = jax.ShapeDtypeStruct((size, size), jnp.bfloat16)
        rounded, *edges = call(
            round_kernel,
            [pltpu.VMEM(lanczos_vector.shape, jnp.bfloat16), block, block],
            (),
            (),
            (sector_sizes, lanczos_vector),
            [
                pltpu.VMEM(lanczos_vector.shape, jnp.float32),
                pltpu.SMEM((sectors,), jnp.int32),
                pltpu.SemaphoreType.DMA((sectors * parts + 1,)),
            ],
        )
        halos = [halo(edge, which) for which, edge in enumerate(edges)]
        matrices = pltpu.VMEM((terms, size, size), jnp.bfloat16)
        cuts, left, right = [], [None] * sectors, [None] * sectors
        for turn in turns:
            send, keep, left[turn], right[turn], *more = call(
                functools.partial(load_kernel, dims, turn),
                [*cut_shapes, matrices, matrices] + ([rows] if turn == 0 else []),
                (),
                (rounded, *[halos[h] for h in halos_at(turn, sectors)]),
                (sector_shifts, sector_sizes, left_block, right_block, lanczos_vector),
                [
                    square,
                    pltpu.SMEM((terms,), jnp.int32),
                    pltpu.SMEM((sectors,), jnp.int32),
                    pltpu.SemaphoreType.DMA((2, terms, 2)),
                    pltpu.SemaphoreType.DMA((sectors,)),
                    pltpu.SemaphoreType.DMA((2,)),
                ],
                terms * pair_flops,
            )
            cuts.append((send, keep))
            start = more[0] if turn == 0 else start
        totals = [low_sum(*c) for c in cuts]

    with jax.named_scope("gather"):
        shifted, plus, minus, pieces = [[None] * sectors for _ in range(4)]
        row = pltpu.VMEM((span, size), jnp.float32)
        parts = [high_parts(total) for total in totals]
        for turn in turns:
            held, shifted[turn], plus[turn], minus[turn] = call(
                functools.partial(shift_kernel, dims, turn, scale),
                [jax.ShapeDtypeStruct((span, size), jnp.bfloat16), row, row, row],
                (sector_sizes,),
                (start, left_energy, right_energy, *parts[turn]),
            )
            mine = gather_high(held[None])
            theirs = lax.ppermute(mine, "term", pairs_low(ranks)) if low > 1 else mine
            pieces[turn] = [mine, theirs]
    def sector_sums(turn, block):
        return call(
            functools.partial(sums_kernel, dims, turn),
            [jax.ShapeDtypeStruct((8, size), jnp.float32)],
            (sector_sizes,),
            (lanczos_vector, block),
            flops=1,
        )[0]

    with jax.named_scope("second"):
        acc, block = call(
            functools.partial(self_kernel, dims),
            [square, square_low],
            (sector_shifts,),
            (left[0], right[0], *pieces[0]),
            flops=1,
        )
        sums = [sector_sums(0, block)]
        whole = after_all(jnp.stack(pieces[0]), pieces[-1][1], acc, sums[0])
        halos = [halo(edge, n) for n, edge in enumerate((whole, jnp.stack(pieces[-1])))]
        *first_cut, own = call(
            functools.partial(rest_kernel, dims),
            [*cut_shapes, pltpu.VMEM((sectors, size, size), jnp.bfloat16)],
            (sector_shifts,),
            (
                acc,
                block,
                left[0],
                right[0],
                *[piece for both in pieces[1:] for piece in both],
                *[halos[h] for h in halos_at(0, sectors)],
            ),
            scratch=[square, pltpu.VMEM((2, size, size), jnp.bfloat16)],
            flops=terms * pair_flops // 2,
        )
        cuts = [first_cut]
        for turn in turns[1:]:
            sums.append(sector_sums(turn, after_all(own, *first_cut)))
        own = after_all(own, *sums)
        for turn in turns[1:]:
            cuts.append(
                call(
                    functools.partial(full_kernel, dims, turn),
                    cut_shapes,
                    (sector_shifts,),
                    (own, left[turn], right[turn], *[halos[h] for h in halos_at(turn, sectors)]),
                    scratch=[square, pltpu.VMEM((2, size, size), jnp.bfloat16)],
                    flops=terms * pair_flops,
                )
            )
        totals = [low_sum(*c) for c in cuts]

    with jax.named_scope("scalars"):
        parts = [high_parts(total) for total in totals]
        sums = after_all(sum(sums), totals[-1], parts[0][-1])
        tables, reach = [sums], 1
        while reach < groups:
            if groups & (groups - 1):
                tables, reach = [lax.psum(sums, "sector")], groups
            else:
                sums, width = sum(tables), min(4, groups // reach)
                tables = [sums] + [
                    lax.ppermute(sums, "sector", [(i, i ^ (reach * k)) for i in range(groups)])
                    for k in range(1, width)
                ]
                reach *= width
        out = jax.ShapeDtypeStruct((sectors, span, size), jnp.float32)
        flat = [part for each in parts for part in each]
        return call(
            functools.partial(finish_kernel, dims, cells, scale),
            [out, out],
            (sector_sizes,),
            (start, *shifted, *plus, *minus, *flat, *tables),
        )


def solution(mesh):
    return jax.shard_map(
        on_device,
        mesh=mesh,
        in_specs=(
            P("sector", None, None),
            P("sector", "term", None, None),
            P("sector", "term", None, None),
            P("sector", None),
            P("sector", None),
            P("term"),
            P("sector"),
        ),
        out_specs=(P("sector", "term", None), P("sector", "term", None)),
        check_vma=False,
    )
```

```python
import functools
import jax
import jax.numpy as jnp
from jax import lax
from jax.experimental import pallas as pl
from jax.experimental.pallas import tpu as pltpu
from jax.sharding import PartitionSpec as P

epsilon = 1e-06
NT = (((1,), (1,)), ((), ()))
GUESS = 4.5


def other(hi, step, count):
    return hi ^ step if count & (count - 1) == 0 else (step - hi) % count


def traced_other(hi, step, count):
    return hi ^ step if count & (count - 1) == 0 else lax.rem(step - hi + count, count)


def pairs_low(size):
    return [(i, i ^ 1) for i in range(size)]


def pairs_high(size, low, step):
    count = size // low
    return [(i, other(i // low, step, count) * low + i % low) for i in range(size)]


def row_finder(count, low, span):
    rank = lax.axis_index("term")
    hi, lo = rank // low, lax.rem(rank, low)

    def row_of(step, far):
        digit = 1 - lo if far else lo
        return pl.multiple_of((traced_other(hi, step, count) * low + digit) * span, span)

    return row_of


def add_pair(acc, left, right, block):
    mixed = jnp.dot(left[...], block[...], preferred_element_type=jnp.float32)
    acc[...] += lax.dot_general(
        mixed.astype(jnp.bfloat16), right[...], NT, preferred_element_type=jnp.float32
    )


def add_small_pair(acc, left, right, block):
    half = block.shape[0] // 2
    mixed = jnp.dot(left[:, :half], block[:half, :half], preferred_element_type=jnp.float32)
    acc[...] += lax.dot_general(
        mixed.astype(jnp.bfloat16), right[:, :half], NT, preferred_element_type=jnp.float32
    )


def sector_at(turn, sectors):
    odd = lax.rem(lax.axis_index("sector"), 2)
    return odd * turn + (1 - odd) * (sectors - 1 - turn)


def halos_at(turn, sectors):
    return ([0] if turn == 0 else []) + ([1] if turn == sectors - 1 else [])


def halo_side(halo):
    here, groups = lax.axis_index("sector"), lax.axis_size("sector")
    side = (1 - 2 * lax.rem(here, 2)) * (1 - 2 * halo)
    return side, (here + side >= 0) & (here + side < groups)


def add_pairs(
    dims, turn, shift_ref, size_ref, acc, left, right, own, halos, arrived=None, skip_own=False
):
    sectors, terms = dims[:2]
    s = sector_at(turn, sectors)
    for t in range(terms):
        if arrived is not None:
            arrived(t)
        partner = s + shift_ref[t]
        inside = (partner >= 0) & (partner < sectors)
        if skip_own:
            inside &= shift_ref[t] != 0

        small = size_ref[jnp.clip(partner, 0, sectors - 1)] <= dims[2] // 2

        @pl.when(inside & small)
        def _():
            add_small_pair(acc, left.at[t], right.at[t], own.at[partner])

        @pl.when(inside & jnp.logical_not(small))
        def _():
            add_pair(acc, left.at[t], right.at[t], own.at[partner])

        for block, halo in zip(halos, halos_at(turn, sectors)):
            side, there = halo_side(halo)

            @pl.when((shift_ref[t] == side) & there)
            def _():
                add_pair(acc, left.at[t], right.at[t], block)


def place_rows(dims, wb, pieces):
    sectors, terms, size, count, low, span = dims
    row_of = row_finder(count, low, span)
    for far in range(low):
        for step in range(count):
            wb[pl.ds(row_of(step, far), span), :] = pieces[far][step]


def cut(dims, acc, send_ref, keep_ref):
    sectors, terms, size, count, low, span = dims
    row_of = row_finder(count, low, span)
    for step in range(count):
        if low > 1:
            send_ref[step] = acc[pl.ds(row_of(step, 1), span), :].astype(jnp.bfloat16)
        keep_ref[step] = acc[pl.ds(row_of(step, 0), span), :]


def live_tile(shape, first_row, limit):
    row = first_row + lax.broadcasted_iota(jnp.int32, shape, 0)
    return (row < limit) & (lax.broadcasted_iota(jnp.int32, shape, 1) < limit)


def energy_rows(left_row, right_row, s, first, span):
    shape = (span, left_row.shape[1])
    row = first + lax.broadcasted_iota(jnp.int32, shape, 0)
    here = row == lax.broadcasted_iota(jnp.int32, shape, 1)
    left = jnp.sum(jnp.where(here, left_row[pl.ds(s, 1), :], 0.0), axis=1, keepdims=True)
    return left + right_row[pl.ds(s, 1), :]


def round_kernel(size_hbm, vector_hbm, rounded, edge, other_edge, vector, sizes, sems):
    sectors, size = vector.shape[:2]
    parts = sems.shape[0] // sectors
    rows = size // parts
    tile = min(64, rows)
    limits = pltpu.make_async_copy(size_hbm, sizes, sems.at[sectors * parts])
    limits.start()
    copies = [
        pltpu.make_async_copy(
            vector_hbm.at[sector_at(turn, sectors), pl.ds(n * rows, rows), :],
            vector.at[turn, pl.ds(n * rows, rows), :],
            sems.at[turn * parts + n],
        )
        for turn in range(sectors)
        for n in range(parts)
    ]
    for copy in copies:
        copy.start()
    limits.wait()
    for turn in range(sectors):
        s = sector_at(turn, sectors)
        for n in range(parts):
            copies[turn * parts + n].wait()

            @pl.loop(0, rows // tile)
            def _(k):
                first = pl.multiple_of(n * rows + k * tile, tile)
                part = pl.ds(first, tile)
                live = live_tile((tile, size), first, sizes[s])
                value = jnp.where(live, vector[turn, part, :], 0.0).astype(jnp.bfloat16)
                rounded[s, part, :] = value
                if turn == 0:
                    edge[part, :] = value
                if turn == sectors - 1:
                    other_edge[part, :] = value


def load_kernel(dims, turn, own, *refs):
    sectors, terms, size, count, low, span = dims
    blocks, refs = refs[: len(halos_at(turn, sectors))], refs[len(halos_at(turn, sectors)) :]
    shift_hbm, size_hbm, left_hbm, right_hbm, vector_hbm, send_ref, keep_ref, left, right, *refs = refs
    start, refs = (refs[0], refs[1:]) if turn == 0 else (None, refs)
    acc, shift_ref, size_ref, sems, row_sems, scalar_sems = refs
    s = sector_at(turn, sectors)
    scalars = [
        pltpu.make_async_copy(shift_hbm, shift_ref, scalar_sems.at[0]),
        pltpu.make_async_copy(size_hbm, size_ref, scalar_sems.at[1]),
    ]
    copies = [
        [
            pltpu.make_async_copy(hbm.at[s, t, part, :], vmem.at[t, part, :], sems.at[k, t, n])
            for k, (hbm, vmem) in enumerate(((left_hbm, left), (right_hbm, right)))
            for n, part in enumerate((pl.ds(0, size // 2), pl.ds(size // 2, size // 2)))
        ]
        for t in range(terms)
    ]
    first = row_finder(count, low, span)(0, 0)
    rows = [
        pltpu.make_async_copy(vector_hbm.at[e, pl.ds(first, span), :], start.at[e], row_sems.at[e])
        for e in range(sectors if turn == 0 else 0)
    ]
    for copy in scalars:
        copy.start()
    for pair in copies:
        for copy in pair:
            copy.start()
    for copy in rows:
        copy.start()
    acc[...] = jnp.zeros_like(acc)
    for copy in scalars:
        copy.wait()

    def arrived(t):
        for copy in copies[t]:
            copy.wait()

    add_pairs(dims, turn, shift_ref, size_ref, acc, left, right, own, blocks, arrived)
    cut(dims, acc, send_ref, keep_ref)
    for e, copy in enumerate(rows):
        copy.wait()
        live = live_tile((span, size), first, size_ref[e])
        start[e] = jnp.where(live, start[e], 0.0)


def self_kernel(dims, shift_ref, left, right, mine, theirs, acc, own):
    acc[...] = jnp.zeros_like(acc)
    place_rows(dims, own, [mine, theirs])
    for t in range(dims[1]):

        @pl.when(shift_ref[t] == 0)
        def _():
            add_pair(acc, left.at[t], right.at[t], own)


def rest_kernel(dims, shift_ref, size_ref, acc_ref, first_block, left, right, *refs):
    sectors = dims[0]
    pieces, refs = refs[: 2 * sectors - 2], refs[2 * sectors - 2 :]
    halos, (send_ref, keep_ref, own, acc, wb) = refs[:-5], refs[-5:]
    acc[...] = acc_ref[...]
    own[sector_at(0, sectors)] = first_block[...]
    for turn in range(1, sectors):
        place_rows(dims, own.at[sector_at(turn, sectors)], pieces[2 * turn - 2 : 2 * turn])
    for n, halo in enumerate(halos):
        place_rows(dims, wb.at[n], [halo.at[0], halo.at[1]])
    blocks = [wb.at[n] for n in range(len(halos))]
    add_pairs(dims, 0, shift_ref, size_ref, acc, left, right, own, blocks, skip_own=True)
    cut(dims, acc, send_ref, keep_ref)


def full_kernel(dims, turn, shift_ref, size_ref, own, left, right, *refs):
    halos, (send_ref, keep_ref, acc, wb) = refs[:-4], refs[-4:]
    acc[...] = jnp.zeros_like(acc)
    for n, halo in enumerate(halos):
        place_rows(dims, wb.at[n], [halo.at[0], halo.at[1]])
    blocks = [wb.at[n] for n in range(len(halos))]
    add_pairs(dims, turn, shift_ref, size_ref, acc, left, right, own, blocks)
    cut(dims, acc, send_ref, keep_ref)


def sums_kernel(dims, turn, size_ref, vector_ref, block, sums):
    size = dims[2]
    s = sector_at(turn, dims[0])
    sums[...] = jnp.zeros_like(sums)
    tile = min(64, size)

    @pl.loop(0, size // tile)
    def _(n):
        first = pl.multiple_of(n * tile, tile)
        rows = pl.ds(first, tile)
        live = live_tile((tile, size), first, size_ref[s])
        start = jnp.where(live, vector_ref[s, rows, :], 0.0)
        shifted = (block[rows, :] if turn == 0 else block[s, rows, :]).astype(jnp.float32)
        for k, term in enumerate((shifted * shifted, shifted * start, start * start)):
            sums[k : k + 1, :] += jnp.sum(term, 0, keepdims=True)


def shift_kernel(dims, turn, scale, size_ref, start, left_row, right_row, *refs):
    sectors, terms, size, count, low, span = dims
    parts, (held_ref, shifted_ref, plus_ref, minus_ref) = refs[:-4], refs[-4:]
    s = sector_at(turn, sectors)
    first = row_finder(count, low, span)(0, 0)
    total = parts[0][...]
    for part in parts[1:]:
        total += part[...].astype(jnp.float32)
    mixed = jnp.where(live_tile((span, size), first, size_ref[s]), scale * total, 0.0)
    energy = energy_rows(left_row, right_row, s, first, span)
    begin = start[s]
    shifted = mixed + (energy - GUESS) * begin
    held_ref[...] = shifted.astype(jnp.bfloat16)
    shifted_ref[...] = shifted
    plus_ref[...] = energy * shifted
    minus_ref[...] = energy * begin + mixed


def finish_kernel(dims, cells, scale, size_ref, start, *refs):
    sectors, terms, size, count, low, span = dims
    shifted, plus, minus = [refs[k * sectors : (k + 1) * sectors] for k in range(3)]
    parts, refs = refs[3 * sectors : 3 * sectors + count * sectors], refs[3 * sectors + count * sectors :]
    tables, (next_ref, sigma_ref) = refs[:-2], refs[-2:]
    first = row_finder(count, low, span)(0, 0)
    sums = sum(table[...] for table in tables)
    shifted_sq, overlap, norm_sq = [
        jnp.sum(sums[k : k + 1, :], axis=1, keepdims=True) for k in range(3)
    ]
    correlation = overlap + GUESS * norm_sq
    ritz = (correlation / cells) / (norm_sq / cells + epsilon)
    delta = ritz - GUESS
    res_sq = shifted_sq - 2.0 * delta * overlap + delta * delta * norm_sq
    inverse = lax.rsqrt(res_sq / cells + epsilon)
    for turn in range(sectors):
        s = sector_at(turn, sectors)
        next_ref[s] = (shifted[turn][...] - delta * start[s]) * inverse
        total = parts[turn * count][...]
        for part in parts[turn * count + 1 : (turn + 1) * count]:
            total += part[...].astype(jnp.float32)
        mixed = jnp.where(live_tile((span, size), first, size_ref[s]), scale * total, 0.0)
        sigma_ref[s] = (plus[turn][...] - delta * minus[turn][...] + mixed) * inverse


SMEM = pl.BlockSpec(memory_space=pltpu.SMEM)
VMEM = pl.BlockSpec(memory_space=pltpu.VMEM)
HBM = pl.BlockSpec(memory_space=pltpu.HBM)
LIMIT = pltpu.CompilerParams(vmem_limit_bytes=24 * 2**20)


def call(kernel, out_shape, scalars, arrays, matrices=(), scratch=(), flops=2**20):
    matrices = [pltpu.with_memory_space_constraint(m, pltpu.HBM) for m in matrices]
    return pl.pallas_call(
        kernel,
        out_shape=out_shape,
        in_specs=[SMEM] * len(scalars) + [VMEM] * len(arrays) + [HBM] * len(matrices),
        out_specs=[VMEM] * len(out_shape),
        scratch_shapes=scratch,
        compiler_params=LIMIT,
        cost_estimate=pl.CostEstimate(flops=flops, bytes_accessed=flops // 256, transcendentals=0),
    )(*scalars, *arrays, *matrices)


def after_all(value, *others):
    return lax.optimization_barrier((value, *others))[0]


def on_device(
    lanczos_vector, left_block, right_block, left_energy, right_energy, sector_shifts, sector_sizes
):
    sectors, size = lanczos_vector.shape[:2]
    terms, ranks = left_block.shape[1], lax.axis_size("term")
    groups = lax.axis_size("sector")
    scale = float(terms * ranks) ** (-0.5)
    cells = float(sectors * groups * size * size)
    span = size // ranks
    low = 2 if ranks % 2 == 0 else 1
    count = ranks // low
    dims = (sectors, terms, size, count, low, span)
    turns = range(sectors)
    pair_flops = 4 * size**3
    rows = pltpu.VMEM((sectors, span, size), jnp.float32)
    square = pltpu.VMEM((size, size), jnp.float32)
    square_low = pltpu.VMEM((size, size), jnp.bfloat16)
    cut_shapes = [jax.ShapeDtypeStruct((count, span, size), d) for d in (jnp.bfloat16, jnp.float32)]
    pairs = [
        [p for i in range(start, groups - 1, 2) for p in ((i, i + 1), (i + 1, i))]
        for start in range(2)
    ]

    def halo(edge, which):
        return lax.ppermute(edge, "sector", pairs[which]) if pairs[which] else edge

    def low_sum(send, keep):
        if low == 1:
            return keep
        return keep + lax.ppermute(send, "term", pairs_low(ranks)).astype(jnp.float32)

    hops = range(count - 1, 0, -1)

    def high_parts(total):
        return [total[0]] + [
            lax.ppermute(total[k].astype(jnp.bfloat16), "term", pairs_high(ranks, low, k))
            for k in hops
        ]

    def gather_high(held):
        got = {k: lax.ppermute(held, "term", pairs_high(ranks, low, k)) for k in hops}
        return jnp.concatenate([held] + [got[k] for k in range(1, count)])

    with jax.named_scope("first"):
        parts = 2 if size % 256 == 0 else 1
        block = jax.ShapeDtypeStruct((size, size), jnp.bfloat16)
        rounded, *edges = call(
            round_kernel,
            [pltpu.VMEM(lanczos_vector.shape, jnp.bfloat16), block, block],
            (),
            (),
            (sector_sizes, lanczos_vector),
            [
                pltpu.VMEM(lanczos_vector.shape, jnp.float32),
                pltpu.SMEM((sectors,), jnp.int32),
                pltpu.SemaphoreType.DMA((sectors * parts + 1,)),
            ],
        )
        halos = [halo(edge, which) for which, edge in enumerate(edges)]
        matrices = pltpu.VMEM((terms, size, size), jnp.bfloat16)
        cuts, left, right = [], [None] * sectors, [None] * sectors
        for turn in turns:
            send, keep, left[turn], right[turn], *more = call(
                functools.partial(load_kernel, dims, turn),
                [*cut_shapes, matrices, matrices] + ([rows] if turn == 0 else []),
                (),
                (rounded, *[halos[h] for h in halos_at(turn, sectors)]),
                (sector_shifts, sector_sizes, left_block, right_block, lanczos_vector),
                [
                    square,
                    pltpu.SMEM((terms,), jnp.int32),
                    pltpu.SMEM((sectors,), jnp.int32),
                    pltpu.SemaphoreType.DMA((2, terms, 2)),
                    pltpu.SemaphoreType.DMA((sectors,)),
                    pltpu.SemaphoreType.DMA((2,)),
                ],
                terms * pair_flops,
            )
            cuts.append((send, keep))
            start = more[0] if turn == 0 else start
        totals = [low_sum(*c) for c in cuts]

    with jax.named_scope("gather"):
        shifted, plus, minus, pieces = [[None] * sectors for _ in range(4)]
        row = pltpu.VMEM((span, size), jnp.float32)
        parts = [high_parts(total) for total in totals]
        for turn in turns:
            held, shifted[turn], plus[turn], minus[turn] = call(
                functools.partial(shift_kernel, dims, turn, scale),
                [jax.ShapeDtypeStruct((span, size), jnp.bfloat16), row, row, row],
                (sector_sizes,),
                (start, left_energy, right_energy, *parts[turn]),
            )
            mine = gather_high(held[None])
            theirs = lax.ppermute(mine, "term", pairs_low(ranks)) if low > 1 else mine
            pieces[turn] = [mine, theirs]
    def sector_sums(turn, block):
        return call(
            functools.partial(sums_kernel, dims, turn),
            [jax.ShapeDtypeStruct((8, size), jnp.float32)],
            (sector_sizes,),
            (lanczos_vector, block),
            flops=1,
        )[0]

    with jax.named_scope("second"):
        acc, block = call(
            functools.partial(self_kernel, dims),
            [square, square_low],
            (sector_shifts,),
            (left[0], right[0], *pieces[0]),
            flops=1,
        )
        sums = [sector_sums(0, block)]
        whole = after_all(jnp.stack(pieces[0]), pieces[-1][1], acc, sums[0])
        halos = [halo(edge, n) for n, edge in enumerate((whole, jnp.stack(pieces[-1])))]
        *first_cut, own = call(
            functools.partial(rest_kernel, dims),
            [*cut_shapes, pltpu.VMEM((sectors, size, size), jnp.bfloat16)],
            (sector_shifts, sector_sizes),
            (
                acc,
                block,
                left[0],
                right[0],
                *[piece for both in pieces[1:] for piece in both],
                *[halos[h] for h in halos_at(0, sectors)],
            ),
            scratch=[square, pltpu.VMEM((2, size, size), jnp.bfloat16)],
            flops=terms * pair_flops // 2,
        )
        cuts = [first_cut]
        for turn in turns[1:]:
            sums.append(sector_sums(turn, after_all(own, *first_cut)))
        own = after_all(own, *sums)
        for turn in turns[1:]:
            cuts.append(
                call(
                    functools.partial(full_kernel, dims, turn),
                    cut_shapes,
                    (sector_shifts, sector_sizes),
                    (own, left[turn], right[turn], *[halos[h] for h in halos_at(turn, sectors)]),
                    scratch=[square, pltpu.VMEM((2, size, size), jnp.bfloat16)],
                    flops=terms * pair_flops,
                )
            )
        totals = [low_sum(*c) for c in cuts]

    with jax.named_scope("scalars"):
        parts = [high_parts(total) for total in totals]
        sums = after_all(sum(sums), totals[-1], parts[0][-1])
        tables, reach = [sums], 1
        while reach < groups:
            if groups & (groups - 1):
                tables, reach = [lax.psum(sums, "sector")], groups
            else:
                sums, width = sum(tables), min(4, groups // reach)
                tables = [sums] + [
                    lax.ppermute(sums, "sector", [(i, i ^ (reach * k)) for i in range(groups)])
                    for k in range(1, width)
                ]
                reach *= width
        out = jax.ShapeDtypeStruct((sectors, span, size), jnp.float32)
        flat = [part for each in parts for part in each]
        return call(
            functools.partial(finish_kernel, dims, cells, scale),
            [out, out],
            (sector_sizes,),
            (start, *shifted, *plus, *minus, *flat, *tables),
        )


def solution(mesh):
    return jax.shard_map(
        on_device,
        mesh=mesh,
        in_specs=(
            P("sector", None, None),
            P("sector", "term", None, None),
            P("sector", "term", None, None),
            P("sector", None),
            P("sector", None),
            P("term"),
            P("sector"),
        ),
        out_specs=(P("sector", "term", None), P("sector", "term", None)),
        check_vma=False,
    )
```

```python
import functools
import jax
import jax.numpy as jnp
from jax import lax
from jax.experimental import pallas as pl
from jax.experimental.pallas import tpu as pltpu
from jax.sharding import PartitionSpec as P

epsilon = 1e-06
NT = (((1,), (1,)), ((), ()))
GUESS = 4.5


def other(hi, step, count):
    return hi ^ step if count & (count - 1) == 0 else (step - hi) % count


def traced_other(hi, step, count):
    return hi ^ step if count & (count - 1) == 0 else lax.rem(step - hi + count, count)


def pairs_low(size):
    return [(i, i ^ 1) for i in range(size)]


def pairs_high(size, low, step):
    count = size // low
    return [(i, other(i // low, step, count) * low + i % low) for i in range(size)]


def row_finder(count, low, span):
    rank = lax.axis_index("term")
    hi, lo = rank // low, lax.rem(rank, low)

    def row_of(step, far):
        digit = 1 - lo if far else lo
        return pl.multiple_of((traced_other(hi, step, count) * low + digit) * span, span)

    return row_of


def add_pair(acc, left, right, block):
    mixed = jnp.dot(left[...], block[...], preferred_element_type=jnp.float32)
    acc[...] += lax.dot_general(
        mixed.astype(jnp.bfloat16), right[...], NT, preferred_element_type=jnp.float32
    )


def sector_at(turn, sectors):
    odd = lax.rem(lax.axis_index("sector"), 2)
    return odd * turn + (1 - odd) * (sectors - 1 - turn)


def halos_at(turn, sectors):
    return ([0] if turn == 0 else []) + ([1] if turn == sectors - 1 else [])


def halo_side(halo):
    here, groups = lax.axis_index("sector"), lax.axis_size("sector")
    side = (1 - 2 * lax.rem(here, 2)) * (1 - 2 * halo)
    return side, (here + side >= 0) & (here + side < groups)


def add_pairs(dims, turn, shift_ref, acc, left, right, own, halos, arrived=None, skip_own=False):
    sectors, terms = dims[:2]
    s = sector_at(turn, sectors)
    for t in range(terms):
        if arrived is not None:
            arrived(t)
        partner = s + shift_ref[t]
        inside = (partner >= 0) & (partner < sectors)
        if skip_own:
            inside &= shift_ref[t] != 0

        @pl.when(inside)
        def _():
            add_pair(acc, left.at[t], right.at[t], own.at[partner])

        for block, halo in zip(halos, halos_at(turn, sectors)):
            side, there = halo_side(halo)

            @pl.when((shift_ref[t] == side) & there)
            def _():
                add_pair(acc, left.at[t], right.at[t], block)


def place_rows(dims, wb, pieces):
    sectors, terms, size, count, low, span = dims
    row_of = row_finder(count, low, span)
    for far in range(low):
        for step in range(count):
            wb[pl.ds(row_of(step, far), span), :] = pieces[far][step]


def cut(dims, acc, send_ref, keep_ref):
    sectors, terms, size, count, low, span = dims
    row_of = row_finder(count, low, span)
    for step in range(count):
        if low > 1:
            send_ref[step] = acc[pl.ds(row_of(step, 1), span), :].astype(jnp.bfloat16)
        keep_ref[step] = acc[pl.ds(row_of(step, 0), span), :]


def live_tile(shape, first_row, limit):
    row = first_row + lax.broadcasted_iota(jnp.int32, shape, 0)
    return (row < limit) & (lax.broadcasted_iota(jnp.int32, shape, 1) < limit)


def energy_rows(left_row, right_row, s, first, span):
    shape = (span, left_row.shape[1])
    row = first + lax.broadcasted_iota(jnp.int32, shape, 0)
    here = row == lax.broadcasted_iota(jnp.int32, shape, 1)
    left = jnp.sum(jnp.where(here, left_row[pl.ds(s, 1), :], 0.0), axis=1, keepdims=True)
    return left + right_row[pl.ds(s, 1), :]


def round_kernel(size_hbm, vector_hbm, rounded, edge, other_edge, vector, sizes, sems):
    sectors, size = vector.shape[:2]
    parts = sems.shape[0] // sectors
    rows = size // parts
    tile = min(64, rows)
    limits = pltpu.make_async_copy(size_hbm, sizes, sems.at[sectors * parts])
    limits.start()
    copies = [
        pltpu.make_async_copy(
            vector_hbm.at[sector_at(turn, sectors), pl.ds(n * rows, rows), :],
            vector.at[turn, pl.ds(n * rows, rows), :],
            sems.at[turn * parts + n],
        )
        for turn in range(sectors)
        for n in range(parts)
    ]
    for copy in copies:
        copy.start()
    limits.wait()
    for turn in range(sectors):
        s = sector_at(turn, sectors)
        for n in range(parts):
            copies[turn * parts + n].wait()

            @pl.loop(0, rows // tile)
            def _(k):
                first = pl.multiple_of(n * rows + k * tile, tile)
                part = pl.ds(first, tile)
                live = live_tile((tile, size), first, sizes[s])
                value = jnp.where(live, vector[turn, part, :], 0.0).astype(jnp.bfloat16)
                rounded[s, part, :] = value
                if turn == 0:
                    edge[part, :] = value
                if turn == sectors - 1:
                    other_edge[part, :] = value


def load_kernel(dims, turn, own, *refs):
    sectors, terms, size, count, low, span = dims
    blocks, refs = refs[: len(halos_at(turn, sectors))], refs[len(halos_at(turn, sectors)) :]
    shift_hbm, size_hbm, left_hbm, right_hbm, vector_hbm, send_ref, keep_ref, left, right, *refs = refs
    start, refs = (refs[0], refs[1:]) if turn == 0 else (None, refs)
    acc, shift_ref, size_ref, sems, row_sems, scalar_sems = refs
    s = sector_at(turn, sectors)
    scalars = [
        pltpu.make_async_copy(shift_hbm, shift_ref, scalar_sems.at[0]),
        pltpu.make_async_copy(size_hbm, size_ref, scalar_sems.at[1]),
    ]
    copies = [
        [
            pltpu.make_async_copy(hbm.at[s, t, part, :], vmem.at[t, part, :], sems.at[k, t, n])
            for k, (hbm, vmem) in enumerate(((left_hbm, left), (right_hbm, right)))
            for n, part in enumerate((pl.ds(0, size // 2), pl.ds(size // 2, size // 2)))
        ]
        for t in range(terms)
    ]
    first = row_finder(count, low, span)(0, 0)
    rows = [
        pltpu.make_async_copy(vector_hbm.at[e, pl.ds(first, span), :], start.at[e], row_sems.at[e])
        for e in range(sectors if turn == 0 else 0)
    ]
    for copy in scalars:
        copy.start()
    for pair in copies:
        for copy in pair:
            copy.start()
    for copy in rows:
        copy.start()
    acc[...] = jnp.zeros_like(acc)
    for copy in scalars:
        copy.wait()

    def arrived(t):
        for copy in copies[t]:
            copy.wait()

    add_pairs(dims, turn, shift_ref, acc, left, right, own, blocks, arrived)
    cut(dims, acc, send_ref, keep_ref)
    for e, copy in enumerate(rows):
        copy.wait()
        live = live_tile((span, size), first, size_ref[e])
        start[e] = jnp.where(live, start[e], 0.0)


def self_kernel(dims, shift_ref, left, right, mine, theirs, acc, own):
    acc[...] = jnp.zeros_like(acc)
    place_rows(dims, own, [mine, theirs])
    for t in range(dims[1]):

        @pl.when(shift_ref[t] == 0)
        def _():
            add_pair(acc, left.at[t], right.at[t], own)


def rest_kernel(dims, shift_ref, acc_ref, first_block, left, right, *refs):
    sectors = dims[0]
    pieces, refs = refs[: 2 * sectors - 2], refs[2 * sectors - 2 :]
    halos, (send_ref, keep_ref, own, acc, wb) = refs[:-5], refs[-5:]
    acc[...] = acc_ref[...]
    own[sector_at(0, sectors)] = first_block[...]
    for turn in range(1, sectors):
        place_rows(dims, own.at[sector_at(turn, sectors)], pieces[2 * turn - 2 : 2 * turn])
    for n, halo in enumerate(halos):
        place_rows(dims, wb.at[n], [halo.at[0], halo.at[1]])
    blocks = [wb.at[n] for n in range(len(halos))]
    add_pairs(dims, 0, shift_ref, acc, left, right, own, blocks, skip_own=True)
    cut(dims, acc, send_ref, keep_ref)


def full_kernel(dims, turn, shift_ref, own, left, right, *refs):
    halos, (send_ref, keep_ref, acc, wb) = refs[:-4], refs[-4:]
    acc[...] = jnp.zeros_like(acc)
    for n, halo in enumerate(halos):
        place_rows(dims, wb.at[n], [halo.at[0], halo.at[1]])
    blocks = [wb.at[n] for n in range(len(halos))]
    add_pairs(dims, turn, shift_ref, acc, left, right, own, blocks)
    cut(dims, acc, send_ref, keep_ref)


def sums_kernel(dims, turn, size_ref, vector_ref, block, sums):
    size = dims[2]
    s = sector_at(turn, dims[0])
    sums[...] = jnp.zeros_like(sums)
    tile = min(64, size)

    @pl.loop(0, size // tile)
    def _(n):
        first = pl.multiple_of(n * tile, tile)
        rows = pl.ds(first, tile)
        live = live_tile((tile, size), first, size_ref[s])
        start = jnp.where(live, vector_ref[s, rows, :], 0.0)
        shifted = (block[rows, :] if turn == 0 else block[s, rows, :]).astype(jnp.float32)
        for k, term in enumerate((shifted * shifted, shifted * start, start * start)):
            sums[k : k + 1, :] += jnp.sum(term, 0, keepdims=True)


def shift_kernel(dims, turn, scale, size_ref, start, left_row, right_row, *refs):
    sectors, terms, size, count, low, span = dims
    parts, (held_ref, shifted_ref, plus_ref, minus_ref) = refs[:-4], refs[-4:]
    s = sector_at(turn, sectors)
    first = row_finder(count, low, span)(0, 0)
    total = parts[0][...]
    for part in parts[1:]:
        total += part[...].astype(jnp.float32)
    mixed = jnp.where(live_tile((span, size), first, size_ref[s]), scale * total, 0.0)
    energy = energy_rows(left_row, right_row, s, first, span)
    begin = start[s]
    shifted = mixed + (energy - GUESS) * begin
    held_ref[...] = shifted.astype(jnp.bfloat16)
    shifted_ref[...] = shifted
    plus_ref[...] = energy * shifted
    minus_ref[...] = energy * begin + mixed


def finish_kernel(dims, cells, scale, size_ref, start, *refs):
    sectors, terms, size, count, low, span = dims
    shifted, plus, minus = [refs[k * sectors : (k + 1) * sectors] for k in range(3)]
    parts, refs = refs[3 * sectors : 3 * sectors + count * sectors], refs[3 * sectors + count * sectors :]
    tables, (next_ref, sigma_ref) = refs[:-2], refs[-2:]
    first = row_finder(count, low, span)(0, 0)
    sums = sum(table[...] for table in tables)
    shifted_sq, overlap, norm_sq = [
        jnp.sum(sums[k : k + 1, :], axis=1, keepdims=True) for k in range(3)
    ]
    correlation = overlap + GUESS * norm_sq
    ritz = (correlation / cells) / (norm_sq / cells + epsilon)
    delta = ritz - GUESS
    res_sq = shifted_sq - 2.0 * delta * overlap + delta * delta * norm_sq
    inverse = lax.rsqrt(res_sq / cells + epsilon)
    for turn in range(sectors):
        s = sector_at(turn, sectors)
        next_ref[s] = (shifted[turn][...] - delta * start[s]) * inverse
        total = parts[turn * count][...]
        for part in parts[turn * count + 1 : (turn + 1) * count]:
            total += part[...].astype(jnp.float32)
        mixed = jnp.where(live_tile((span, size), first, size_ref[s]), scale * total, 0.0)
        sigma_ref[s] = (plus[turn][...] - delta * minus[turn][...] + mixed) * inverse


SMEM = pl.BlockSpec(memory_space=pltpu.SMEM)
VMEM = pl.BlockSpec(memory_space=pltpu.VMEM)
HBM = pl.BlockSpec(memory_space=pltpu.HBM)
LIMIT = pltpu.CompilerParams(vmem_limit_bytes=24 * 2**20)


def call(kernel, out_shape, scalars, arrays, matrices=(), scratch=(), flops=2**20):
    matrices = [pltpu.with_memory_space_constraint(m, pltpu.HBM) for m in matrices]
    return pl.pallas_call(
        kernel,
        out_shape=out_shape,
        in_specs=[SMEM] * len(scalars) + [VMEM] * len(arrays) + [HBM] * len(matrices),
        out_specs=[VMEM] * len(out_shape),
        scratch_shapes=scratch,
        compiler_params=LIMIT,
        cost_estimate=pl.CostEstimate(flops=flops, bytes_accessed=flops // 256, transcendentals=0),
    )(*scalars, *arrays, *matrices)


def after_all(value, *others):
    return lax.optimization_barrier((value, *others))[0]


def on_device(
    lanczos_vector, left_block, right_block, left_energy, right_energy, sector_shifts, sector_sizes
):
    sectors, size = lanczos_vector.shape[:2]
    terms, ranks = left_block.shape[1], lax.axis_size("term")
    groups = lax.axis_size("sector")
    scale = float(terms * ranks) ** (-0.5)
    cells = float(sectors * groups * size * size)
    span = size // ranks
    low = 2 if ranks % 2 == 0 else 1
    count = ranks // low
    dims = (sectors, terms, size, count, low, span)
    turns = range(sectors)
    pair_flops = 4 * size**3
    rows = pltpu.VMEM((sectors, span, size), jnp.float32)
    square = pltpu.VMEM((size, size), jnp.float32)
    square_low = pltpu.VMEM((size, size), jnp.bfloat16)
    cut_shapes = [jax.ShapeDtypeStruct((count, span, size), d) for d in (jnp.bfloat16, jnp.float32)]
    pairs = [
        [p for i in range(start, groups - 1, 2) for p in ((i, i + 1), (i + 1, i))]
        for start in range(2)
    ]

    def halo(edge, which):
        return lax.ppermute(edge, "sector", pairs[which]) if pairs[which] else edge

    def low_sum(send, keep):
        if low == 1:
            return keep
        return keep + lax.ppermute(send, "term", pairs_low(ranks)).astype(jnp.float32)

    hops = range(count - 1, 0, -1)

    def high_parts(total):
        return [total[0]] + [
            lax.ppermute(total[k].astype(jnp.bfloat16), "term", pairs_high(ranks, low, k))
            for k in hops
        ]

    def gather_high(held):
        got = {k: lax.ppermute(held, "term", pairs_high(ranks, low, k)) for k in hops}
        return jnp.concatenate([held] + [got[k] for k in range(1, count)])

    with jax.named_scope("first"):
        parts = 4 if size % 256 == 0 else 1
        block = jax.ShapeDtypeStruct((size, size), jnp.bfloat16)
        rounded, *edges = call(
            round_kernel,
            [pltpu.VMEM(lanczos_vector.shape, jnp.bfloat16), block, block],
            (),
            (),
            (sector_sizes, lanczos_vector),
            [
                pltpu.VMEM(lanczos_vector.shape, jnp.float32),
                pltpu.SMEM((sectors,), jnp.int32),
                pltpu.SemaphoreType.DMA((sectors * parts + 1,)),
            ],
        )
        halos = [halo(edge, which) for which, edge in enumerate(edges)]
        matrices = pltpu.VMEM((terms, size, size), jnp.bfloat16)
        cuts, left, right = [], [None] * sectors, [None] * sectors
        for turn in turns:
            send, keep, left[turn], right[turn], *more = call(
                functools.partial(load_kernel, dims, turn),
                [*cut_shapes, matrices, matrices] + ([rows] if turn == 0 else []),
                (),
                (rounded, *[halos[h] for h in halos_at(turn, sectors)]),
                (sector_shifts, sector_sizes, left_block, right_block, lanczos_vector),
                [
                    square,
                    pltpu.SMEM((terms,), jnp.int32),
                    pltpu.SMEM((sectors,), jnp.int32),
                    pltpu.SemaphoreType.DMA((2, terms, 2)),
                    pltpu.SemaphoreType.DMA((sectors,)),
                    pltpu.SemaphoreType.DMA((2,)),
                ],
                terms * pair_flops,
            )
            cuts.append((send, keep))
            start = more[0] if turn == 0 else start
        totals = [low_sum(*c) for c in cuts]

    with jax.named_scope("gather"):
        shifted, plus, minus, pieces = [[None] * sectors for _ in range(4)]
        row = pltpu.VMEM((span, size), jnp.float32)
        parts = [high_parts(total) for total in totals]
        for turn in turns:
            held, shifted[turn], plus[turn], minus[turn] = call(
                functools.partial(shift_kernel, dims, turn, scale),
                [jax.ShapeDtypeStruct((span, size), jnp.bfloat16), row, row, row],
                (sector_sizes,),
                (start, left_energy, right_energy, *parts[turn]),
            )
            mine = gather_high(held[None])
            theirs = lax.ppermute(mine, "term", pairs_low(ranks)) if low > 1 else mine
            pieces[turn] = [mine, theirs]
    def sector_sums(turn, block):
        return call(
            functools.partial(sums_kernel, dims, turn),
            [jax.ShapeDtypeStruct((8, size), jnp.float32)],
            (sector_sizes,),
            (lanczos_vector, block),
            flops=1,
        )[0]

    with jax.named_scope("second"):
        acc, block = call(
            functools.partial(self_kernel, dims),
            [square, square_low],
            (sector_shifts,),
            (left[0], right[0], *pieces[0]),
            flops=1,
        )
        sums = [sector_sums(0, block)]
        whole = after_all(jnp.stack(pieces[0]), pieces[-1][1], acc, sums[0])
        halos = [halo(edge, n) for n, edge in enumerate((whole, jnp.stack(pieces[-1])))]
        *first_cut, own = call(
            functools.partial(rest_kernel, dims),
            [*cut_shapes, pltpu.VMEM((sectors, size, size), jnp.bfloat16)],
            (sector_shifts,),
            (
                acc,
                block,
                left[0],
                right[0],
                *[piece for both in pieces[1:] for piece in both],
                *[halos[h] for h in halos_at(0, sectors)],
            ),
            scratch=[square, pltpu.VMEM((2, size, size), jnp.bfloat16)],
            flops=terms * pair_flops // 2,
        )
        cuts = [first_cut]
        for turn in turns[1:]:
            sums.append(sector_sums(turn, after_all(own, *first_cut)))
        own = after_all(own, *sums)
        for turn in turns[1:]:
            cuts.append(
                call(
                    functools.partial(full_kernel, dims, turn),
                    cut_shapes,
                    (sector_shifts,),
                    (own, left[turn], right[turn], *[halos[h] for h in halos_at(turn, sectors)]),
                    scratch=[square, pltpu.VMEM((2, size, size), jnp.bfloat16)],
                    flops=terms * pair_flops,
                )
            )
        totals = [low_sum(*c) for c in cuts]

    with jax.named_scope("scalars"):
        parts = [high_parts(total) for total in totals]
        sums = after_all(sum(sums), totals[-1], parts[0][-1])
        tables, reach = [sums], 1
        while reach < groups:
            if groups & (groups - 1):
                tables, reach = [lax.psum(sums, "sector")], groups
            else:
                sums, width = sum(tables), min(4, groups // reach)
                tables = [sums] + [
                    lax.ppermute(sums, "sector", [(i, i ^ (reach * k)) for i in range(groups)])
                    for k in range(1, width)
                ]
                reach *= width
        out = jax.ShapeDtypeStruct((sectors, span, size), jnp.float32)
        flat = [part for each in parts for part in each]
        return call(
            functools.partial(finish_kernel, dims, cells, scale),
            [out, out],
            (sector_sizes,),
            (start, *shifted, *plus, *minus, *flat, *tables),
        )


def solution(mesh):
    return jax.shard_map(
        on_device,
        mesh=mesh,
        in_specs=(
            P("sector", None, None),
            P("sector", "term", None, None),
            P("sector", "term", None, None),
            P("sector", None),
            P("sector", None),
            P("term"),
            P("sector"),
        ),
        out_specs=(P("sector", "term", None), P("sector", "term", None)),
        check_vma=False,
    )
```
